512 devices in a mesh: ev: 128 (over z, y, core), st: 4 (over x).
Axes of the slice: x: 4, y: 8, z: 8, core: 2. Of those that a mesh axis runs over, the one named last changes fastest.
Arguments:
- traces: float32 [12, 3, 1024, 1024], P('st', None, 'ev'), may hold values from -6 to 6
- ray_slowness: float32 [3, 12, 1024], P(None, 'st', 'ev'), may hold values from -5 to 5
- travel_time: float32 [12, 1024], P('st', 'ev'), may hold values from -6 to 6
- pair_first: int32 [16384], P('ev'), may hold values from 0 to 1023, as said below
- pair_second: int32 [16384], P('ev'), may hold values from 0 to 1023, as said below
- pair_lag: int32 [12, 16384], P('st', 'ev'), may hold values from -240 to 240
- pair_live: int32 [128], P('ev'), may hold values from 1 to 128, 8192 in all
Outputs:
- refined_shift: float32 [12, 16384], P('st', 'ev')
- location: float32 [4, 1024], P(None, 'ev')
The draws below stay inside these ranges and needn't reach their ends.
Inputs may be any that keep to these rules, and one draw needn't show every extreme that they name: pair_first[p] is an event held by the same index of ev as pair slot p. pair_second[p] is an event held by the index of ev of pair slot p or by one of the two indices beside it. `pair_live`: slots at or past an index's count hold padding; some index of ev is full.
All inputs are finite; a program needn't handle non-finite values. No bound on the sum of `pair_live` on one device may be relied on, other than what follows from the above.
Results may differ from the reference program's by a relative error of at most 0.0003.
Values sent between devices are 32-bit elements; how exact they have to be, the bound alone decides.
No kernel may reach another device: no remote copies, remote signals or barrier semaphores. Data moves between devices by JAX's collectives and lax.ppermute only.
A program may use at most 192 MiB of HBM per device.

```python
import math
import jax
import jax.numpy as jnp
import numpy as np
from jax import lax

S = 1024
STATIONS = 12
COMPONENTS = 3
LAGS = 32
PBLOCK = 128
ITERS = 2
EV_DEV = 8
PAIR_DEV = 128
EVENTS = 1024
PAIRS = 16384
N_EV = 128


def draw_pair_first(key, part):
    key = jax.random.fold_in(key, 11)
    slot_ids = jnp.arange(PAIRS, dtype=jnp.int32)
    owners = slot_ids // PAIR_DEV
    return owners * EV_DEV + jax.random.randint(key, slot_ids.shape, 0, EV_DEV, dtype=jnp.int32)


def draw_pair_second(key, part):
    key = jax.random.fold_in(key, 23)
    side_key, event_key = jax.random.split(key)
    slot_ids = jnp.arange(PAIRS, dtype=jnp.int32)
    owners = slot_ids // PAIR_DEV
    holders = EVENTS // EV_DEV
    sides = jax.random.randint(side_key, slot_ids.shape, -1, 2, dtype=jnp.int32)
    neighbour = jnp.clip(owners + sides, 0, holders - 1)
    return neighbour * EV_DEV + jax.random.randint(event_key, slot_ids.shape, 0, EV_DEV, dtype=jnp.int32)


def plant(result, key, least, largest):
    index_at = [jax.random.randint(jax.random.fold_in(key, axis), (), 0, length) for axis, length in enumerate(result.shape)]
    longest = result.shape.index(max(result.shape))
    beside = index_at[:longest] + [(index_at[longest] + 1) % result.shape[longest]] + index_at[longest + 1:]
    return result.at[tuple(index_at)].set(least).at[tuple(beside)].set(largest)


def level_of(rng, extent, shards, least, top_value):
    level = 1.0
    for position, parts in shards:
        steps = jax.random.uniform(jax.random.fold_in(jax.random.fold_in(rng, 6), position), (parts,), jnp.float32, least / len(shards), top_value / len(shards))
        level = level * jnp.repeat(jnp.exp(steps), extent[position] // parts).reshape((-1,) + (1,) * (len(extent) - 1 - position))
    return level


def split_up(amount, total, most, lean):
    loads = [(1 << 20) // math.isqrt(standing ** lean) + 1 for standing in range(2, amount + 1)]
    spare, given = total - most - (amount - 1), [1] * (amount - 1)
    while spare > 0:
        candidates = [i for i in range(amount - 1) if given[i] < most]
        mass, remaining = sum([loads[i] for i in candidates]), spare
        for i in candidates:
            more = min(most - given[i], max(1, remaining * loads[i] // mass), spare)
            given[i] = given[i] + more
            spare = spare - more
    return np.array([most] + given)


def uneven_parts(own_key, amount, total, most, slope):
    if amount == 2:
        one = jax.random.randint(own_key, (), max(1, total - most), min(most, total - 1) + 1)
        return jnp.stack([one, total - one])
    lengths = jnp.asarray(split_up(amount, total, most, slope), jnp.int32)
    couples = (amount - 1) // 2
    giver, receiver = lengths[1:1 + 2 * couples:2], lengths[2:2 + 2 * couples:2]
    margin = jnp.minimum(giver - 1, most - receiver)
    moved = jax.random.randint(jax.random.fold_in(own_key, 1), (couples,), 0, 1 << 20) % (margin + 1)
    lengths = lengths.at[1:1 + 2 * couples:2].set(giver - moved).at[2:2 + 2 * couples:2].set(receiver + moved)
    return lengths[jax.random.permutation(jax.random.fold_in(own_key, 2), amount)]


def normal_values(own_key, shape, spread, bound, cuts=(), kind=jnp.bfloat16):
    result = spread * jax.random.normal(own_key, shape, jnp.float32)
    if cuts:
        result = result * level_of(own_key, shape, cuts, -0.22, 0.18)
    return jnp.clip(result, -bound, bound).astype(kind)


def setup_inputs(seed: int = 0) -> dict:
    splits = jax.random.split(jax.random.key(seed), 8)
    traces = normal_values(splits[0], (STATIONS, COMPONENTS, EVENTS, S), 1.0, 6.0, ((0, 4), (2, 128)), jnp.float32)
    ray_slowness = normal_values(splits[1], (3, STATIONS, EVENTS), 1.0, 5.0, ((1, 4), (2, 128)), jnp.float32)
    travel_time = normal_values(splits[2], (STATIONS, EVENTS), 1.0, 6.0, ((0, 4), (1, 128)), jnp.float32)
    pair_first = draw_pair_first(jax.random.fold_in(splits[7], 71), 0)
    pair_second = draw_pair_second(jax.random.fold_in(splits[7], 71), 0)
    pair_lag = plant(jax.random.randint(splits[5], (STATIONS, PAIRS), -(S // 4 - LAGS // 2), S // 4 - LAGS // 2 + 1), jax.random.fold_in(splits[5], 1), -(S // 4 - LAGS // 2), (S // 4 - LAGS // 2 + 1) - 1).astype(jnp.int32)
    pair_live = uneven_parts(splits[6], N_EV, PAIRS // 2, PAIR_DEV, 2).astype(jnp.int32)
    return {"traces": traces, "ray_slowness": ray_slowness, "travel_time": travel_time, "pair_first": pair_first, "pair_second": pair_second, "pair_lag": pair_lag, "pair_live": pair_live}


eps_small = 1e-06
sample_step = 0.01

def norm_of(values):
    return jnp.sqrt(jnp.sum(values * values) + eps_small)

def reference(traces, ray_slowness, travel_time, pair_first, pair_second, pair_lag, pair_live):
    length = S
    quarter = length // 4
    positions = jnp.arange(length, dtype=jnp.int32)
    window_mask = ((positions >= quarter) & (positions < 3 * quarter)).astype(traces.dtype)
    windowed = traces * window_mask
    first_energy = lax.optimization_barrier(jnp.sum(windowed * windowed, axis=-1))
    second_energy = lax.optimization_barrier(jnp.sum(traces * traces, axis=-1))
    first_spec = jnp.fft.rfft(windowed, axis=-1)
    second_spec = jnp.fft.rfft(traces, axis=-1)
    slot_ids = jnp.arange(PAIRS, dtype=jnp.int32)
    live_rows = (slot_ids % PAIR_DEV < pair_live[slot_ids // PAIR_DEV]).astype(traces.dtype)
    lag_offsets = jnp.arange(LAGS, dtype=jnp.int32) - LAGS // 2
    centred = lag_offsets.astype(traces.dtype)

    def one_block(block_index):
        row_start = block_index * PBLOCK
        first_ids = lax.dynamic_slice_in_dim(pair_first, row_start, PBLOCK)
        second_ids = lax.dynamic_slice_in_dim(pair_second, row_start, PBLOCK)
        lag_block = lax.dynamic_slice_in_dim(pair_lag, row_start, PBLOCK, 1)
        cross = jnp.conj(first_spec[:, :, first_ids]) * second_spec[:, :, second_ids]
        circular = jnp.fft.irfft(cross, n=length, axis=-1)
        lag_index = (lag_block[:, None, :, None] + lag_offsets) % length
        lag_index = jnp.broadcast_to(lag_index, circular.shape[:3] + (LAGS,)).astype(jnp.int32)
        xcorr = jnp.take_along_axis(circular, lag_index, axis=-1)
        energy_scale = (first_energy[:, :, first_ids] + eps_small) * (second_energy[:, :, second_ids] + eps_small)
        energy = lax.optimization_barrier(jnp.sum(xcorr * xcorr / energy_scale[..., None], axis=1))
        return lax.optimization_barrier(jnp.sum(energy * centred, axis=-1)) / (lax.optimization_barrier(jnp.sum(energy, axis=-1)) + eps_small)
    blocks = lax.map(one_block, jnp.arange(PAIRS // PBLOCK, dtype=jnp.int32))
    refined_shift = jnp.transpose(blocks, (1, 0, 2)).reshape(STATIONS, PAIRS) * live_rows
    deriv = jnp.concatenate([ray_slowness, jnp.ones((1, STATIONS, EVENTS), ray_slowness.dtype)], axis=0)
    deriv_first = deriv[:, :, pair_first]
    deriv_second = deriv[:, :, pair_second]

    def forward(model_vec):
        terms = deriv_first * model_vec[:, None, pair_first] - deriv_second * model_vec[:, None, pair_second]
        return live_rows * lax.optimization_barrier(jnp.sum(terms, axis=0))

    def adjoint(data_vec):
        first_terms = lax.optimization_barrier(jnp.sum(deriv_first * data_vec[None], axis=1))
        second_terms = lax.optimization_barrier(jnp.sum(deriv_second * data_vec[None], axis=1))
        total_sum = jnp.zeros((4, EVENTS), first_terms.dtype)
        total_sum = total_sum.at[:, pair_first].add(first_terms)
        return total_sum.at[:, pair_second].add(-second_terms)
    rhs = live_rows * (sample_step * (pair_lag.astype(traces.dtype) + refined_shift) - travel_time[:, pair_first] + travel_time[:, pair_second])
    beta_norm = norm_of(rhs)
    unit_data = rhs / beta_norm
    back_vec = adjoint(unit_data)
    alpha_norm = norm_of(back_vec)
    model_dir = back_vec / alpha_norm
    search_dir = model_dir
    location = jnp.zeros((4, EVENTS), traces.dtype)
    phi_bar = beta_norm
    rho_bar = alpha_norm
    for turn in range(ITERS):
        resid_data = forward(model_dir) - alpha_norm * unit_data
        beta_norm = norm_of(resid_data)
        unit_data = resid_data / beta_norm
        rho_value = jnp.sqrt(rho_bar * rho_bar + beta_norm * beta_norm)
        cosine = rho_bar / rho_value
        sine_term = beta_norm / rho_value
        phi_value = cosine * phi_bar
        phi_bar = sine_term * phi_bar
        location = location + phi_value / rho_value * search_dir
        if turn < ITERS - 1:
            back_vec = adjoint(unit_data) - beta_norm * model_dir
            alpha_norm = norm_of(back_vec)
            model_dir = back_vec / alpha_norm
            theta_value = sine_term * alpha_norm
            rho_bar = -cosine * alpha_norm
            search_dir = model_dir - theta_value / rho_value * search_dir
    return (refined_shift, location)
```

```python
import jax
import jax.numpy as jnp
from jax import lax
from jax.experimental import pallas as pl
from jax.experimental.pallas import tpu as pltpu
from jax.sharding import Mesh
from jax.sharding import PartitionSpec as P

LAGS = 32
LANES = 128
ROWS = 8
EV_DEV = 8
NEAR = 3 * EV_DEV
STATIONS_DEV = 3
TRACES_DEV = 9
LENGTH = 1024
CHUNKS = LENGTH // LANES
QUARTER = LENGTH // 4
WINDOW = LENGTH // 2
SPAN = WINDOW + LANES
SPAN_CHUNKS = SPAN // LANES
PAIR_DEV = 128
TRACE_ROWS = NEAR * CHUNKS
VMEM_BYTES = 48 * 1024 * 1024
DEAD = -1000.0

eps_small = 1e-06
sample_step = 0.01
exact_mode = lax.Precision.HIGHEST
NT = (((1,), (1,)), ((), ()))
NN = (((1,), (0,)), ((), ()))


def device_index():
    return lax.axis_index("g") * 2 + lax.axis_index("c")


def dot_exact(left, right, dims):
    return lax.dot_general(
        left, right, dims, precision=exact_mode, preferred_element_type=jnp.float32
    )


def dot_bf16(left, right, dims):
    return lax.dot_general(left, right, dims, preferred_element_type=jnp.float32)


def split_bf16(values):
    high = values.astype(jnp.bfloat16)
    low = (values - high.astype(jnp.float32)).astype(jnp.bfloat16)
    return high, low


def pack_kernel(live_ref, traces_ref, slowness_ref, time_ref, first_ref, second_ref, out_ref):
    base = device_index() * EV_DEV - EV_DEV
    out_ref[0:TRACES_DEV] = traces_ref[...]
    out_ref[TRACES_DEV] = jnp.zeros((ROWS, LENGTH), jnp.float32)
    slots = lax.broadcasted_iota(jnp.int32, (1, PAIR_DEV), 1)
    alive = slots < live_ref[0]
    for row, ids_ref in enumerate((first_ref, second_ref)):
        ids = (ids_ref[...] - base).astype(jnp.float32)
        out_ref[TRACES_DEV, row : row + 1, 0:LANES] = jnp.where(alive, ids, DEAD)
    out_ref[TRACES_DEV, 0:STATIONS_DEV, LANES : LANES + EV_DEV] = time_ref[...]
    for q in range(3):
        lane = (2 + q) * LANES
        out_ref[TRACES_DEV, 0:STATIONS_DEV, lane : lane + EV_DEV] = slowness_ref[q]


def incidence(aux, offset):
    events = lax.broadcasted_iota(jnp.int32, (NEAR, PAIR_DEV), 0).astype(jnp.float32)
    starts = aux[0:1, 0:LANES] + offset
    ends = aux[1:2, 0:LANES] + offset
    return (events == starts).astype(jnp.float32) - (events == ends).astype(jnp.float32)


def near_block(left, own, right, part):
    lane = part * LANES
    return jnp.concatenate(
        [aux[0:STATIONS_DEV, lane : lane + EV_DEV] for aux in (left, own, right)], axis=1
    )


def shift_kernel(
    second_ref,
    lag_ref,
    own_ref,
    left_ref,
    right_ref,
    lag_rows_ref,
    shift_ref,
    block_ref,
    near_ref,
    moved_ref,
    high_ref,
    low_ref,
):
    base = device_index() * EV_DEV - EV_DEV
    for part, ref in enumerate((left_ref, own_ref, right_ref)):
        for item in range(TRACES_DEV):
            values = ref[item]
            power = jnp.sum(values * values, axis=1, keepdims=True)
            values = values * lax.rsqrt(power + eps_small)
            for chunk in range(CHUNKS):
                start = item * TRACE_ROWS + part * EV_DEV * CHUNKS + chunk
                near_ref[pl.ds(start, EV_DEV, stride=CHUNKS), :] = values[
                    :, chunk * LANES : (chunk + 1) * LANES
                ]
    near_ref[pl.ds(TRACES_DEV * TRACE_ROWS, 2 * ROWS), :] = jnp.zeros((2 * ROWS, LANES), jnp.float32)

    lane_ids = lax.broadcasted_iota(jnp.int32, (ROWS, LANES), 1)

    def align(slot, carry):
        event = jnp.clip(second_ref[slot] - base, 0, NEAR - 1)
        for station in range(STATIONS_DEV):
            begin = lag_ref[station, slot] + (QUARTER - LAGS // 2)
            chunk = begin // LANES
            lane = begin % LANES
            keep = lane_ids >= lane
            for component in range(3):
                item = station * 3 + component
                row = item * TRACE_ROWS + event * CHUNKS + chunk
                here = near_ref[pl.ds(row, ROWS), :]
                after = near_ref[pl.ds(row + 1, ROWS), :]
                moved = pltpu.roll(jnp.where(keep, here, after), (LANES - lane) % LANES, 1)
                to = pl.multiple_of((item * PAIR_DEV + slot) * ROWS, ROWS)
                moved_ref[pl.ds(to, ROWS), :] = moved
        return carry

    lax.fori_loop(0, PAIR_DEV, align, 0, unroll=4)

    lag_in_row = lax.broadcasted_iota(jnp.int32, (16, EV_DEV * LAGS), 1)
    row_ids = lax.broadcasted_iota(jnp.int32, (16, EV_DEV * LAGS), 0)
    centred = (lag_in_row % LAGS - LAGS // 2).astype(jnp.float32)
    weights = jnp.where(row_ids < EV_DEV, centred, 1.0)
    pick = jnp.where(lag_in_row // LAGS == row_ids % EV_DEV, weights, 0.0)

    aux_left, aux_own, aux_right = left_ref[TRACES_DEV], own_ref[TRACES_DEV], right_ref[TRACES_DEV]
    signs = incidence(aux_own, 0.0)
    events = lax.broadcasted_iota(jnp.int32, (EV_DEV, PAIR_DEV), 0).astype(jnp.float32)
    first_hot = (events == aux_own[0:1, 0:LANES] - EV_DEV).astype(jnp.float32)
    station_shift = []
    for station in range(STATIONS_DEV):
        energy = jnp.zeros((PAIR_DEV, EV_DEV * LAGS), jnp.float32)
        for component in range(3):
            item = station * 3 + component
            window = own_ref[item, :, QUARTER : QUARTER + WINDOW]
            power = jnp.sum(window * window, axis=1, keepdims=True)
            window = window * lax.rsqrt(power + eps_small)
            padded = jnp.concatenate([window, jnp.zeros((EV_DEV, LANES), jnp.float32)], axis=1)
            for event in range(EV_DEV):
                wide = jnp.broadcast_to(padded[event : event + 1], (LAGS, SPAN))
                wide = pltpu.roll(wide, 0, 1, stride=1, stride_axis=0)
                high, low = split_bf16(wide)
                high_ref[pl.ds(event * LAGS, LAGS), :] = high
                low_ref[pl.ds(event * LAGS, LAGS), :] = low
            pieces = [
                moved_ref[pl.ds(item * PAIR_DEV * ROWS + chunk, PAIR_DEV, stride=ROWS), :]
                for chunk in range(SPAN_CHUNKS)
            ]
            high, low = split_bf16(jnp.concatenate(pieces, axis=1))
            xcorr = dot_bf16(high, high_ref[...], NT)
            xcorr = xcorr + dot_bf16(low, high_ref[...], NT)
            xcorr = xcorr + dot_bf16(high, low_ref[...], NT)
            energy = energy + xcorr * xcorr
        sums = dot_exact(pick, energy, NT)
        above = jnp.sum(sums[0:EV_DEV] * first_hot, axis=0, keepdims=True)
        below = jnp.sum(sums[EV_DEV:] * first_hot, axis=0, keepdims=True)
        station_shift.append(above / (below + eps_small))
    slots_alive = (aux_own[0:1, 0:LANES] >= 0.0).astype(jnp.float32)
    shift = jnp.concatenate(station_shift, axis=0) * slots_alive
    shift_ref[...] = shift

    times = near_block(aux_left, aux_own, aux_right, 1)
    rhs = slots_alive * (
        sample_step * (lag_rows_ref[...].astype(jnp.float32) + shift)
    ) - dot_exact(times, signs, NN)
    per_event = dot_exact(rhs, signs, NT)
    station_group = lax.axis_index("x")
    own_signs = signs[EV_DEV : 2 * EV_DEV]
    counts = dot_exact(own_signs, signs, NT)
    for aux, offset in ((aux_left, -float(EV_DEV)), (aux_right, float(EV_DEV))):
        other = incidence(aux, offset)
        counts = counts + dot_exact(other[EV_DEV : 2 * EV_DEV], other, NT)
    block_ref[...] = jnp.zeros((ROWS, LANES), jnp.float32)
    for q in range(3):
        slowness = near_block(aux_left, aux_own, aux_right, 2 + q)
        block_ref[q : q + 1, 0:NEAR] = jnp.sum(slowness * per_event, axis=0, keepdims=True)
    block_ref[3:4, 0:NEAR] = jnp.sum(per_event, axis=0, keepdims=True)
    total = jnp.sum(jnp.sum(rhs * rhs, axis=1, keepdims=True), axis=0, keepdims=True)
    block_ref[0:1, NEAR : NEAR + 1] = total
    block_ref[:, 32 : 32 + NEAR] = jnp.where(station_group == 0, counts, 0.0)
    for group in range(4):
        row = 4 * (group // 2)
        lane = 64 + 32 * (group % 2)
        for q in range(3):
            own = aux_own[0:STATIONS_DEV, (2 + q) * LANES : (2 + q) * LANES + EV_DEV]
            at = lane + q * EV_DEV
            block_ref[row : row + STATIONS_DEV, at : at + EV_DEV] = jnp.where(
                station_group == group, own, 0.0
            )


def solve_kernel(gathered_ref, out_ref, rows_ref):
    half = LANES // 2
    tables = []
    for row in range(ROWS):
        for core in range(2):
            values = gathered_ref[pl.ds(core * half * ROWS + row, half, stride=ROWS), :]
            rows_ref[pl.ds(row * LANES + core, half, stride=2), :] = values
        tables.append(jnp.transpose(rows_ref[pl.ds(row * LANES, LANES), :]))

    def along(lower, own, upper):
        return own + pltpu.roll(upper, 1, 1) + pltpu.roll(lower, LANES - 1, 1)

    back = [along(tables[q][0:8], tables[q][8:16], tables[q][16:24]) for q in range(4)]
    counts = [
        [tables[a][32 + 8 * side : 40 + 8 * side] for side in range(3)] for a in range(EV_DEV)
    ]
    deriv = []
    for group in range(4):
        for station in range(STATIONS_DEV):
            table = tables[4 * (group // 2) + station]
            lane = 64 + 32 * (group % 2)
            deriv.append([table[lane + 8 * q : lane + 8 * q + 8] for q in range(3)])

    def total(values):
        return jnp.sum(jnp.sum(values, axis=1, keepdims=True), axis=0, keepdims=True)

    def inner(left, right):
        terms = left[0] * right[0]
        for q in range(1, 4):
            terms = terms + left[q] * right[q]
        return total(terms)

    def normal(model):
        result = [jnp.zeros((EV_DEV, LANES), jnp.float32) for _ in range(4)]
        for rates in deriv:
            data = model[3]
            for q in range(3):
                data = data + rates[q] * model[q]
            sides = [None, None, None]
            for a in range(EV_DEV):
                row = jnp.broadcast_to(data[a : a + 1], (EV_DEV, LANES))
                for side in range(3):
                    term = counts[a][side] * row
                    sides[side] = term if a == 0 else sides[side] + term
            mixed = along(*sides)
            for q in range(3):
                result[q] = result[q] + rates[q] * mixed
            result[3] = result[3] + mixed
        return result

    rhs_square = total(tables[0][NEAR : NEAR + 1])
    beta = jnp.sqrt(rhs_square + eps_small)
    unit_square = rhs_square / (beta * beta)
    adjoint = [value / beta for value in back]
    alpha = jnp.sqrt(inner(adjoint, adjoint) + eps_small)
    model = [value / alpha for value in adjoint]
    search = model
    location = [jnp.zeros((EV_DEV, LANES), jnp.float32) for _ in range(4)]
    phi_bar = beta
    rho_bar = alpha
    for turn in range(2):
        normal_model = normal(model)
        square = inner(model, normal_model) - 2.0 * alpha * inner(model, adjoint)
        square = jnp.maximum(square + alpha * alpha * unit_square, 0.0)
        beta = jnp.sqrt(square + eps_small)
        rho = jnp.sqrt(rho_bar * rho_bar + beta * beta)
        cosine = rho_bar / rho
        sine = beta / rho
        phi = cosine * phi_bar
        phi_bar = sine * phi_bar
        step = phi / rho
        location = [location[q] + step * search[q] for q in range(4)]
        if turn == 0:
            unit_square = square / (beta * beta)
            adjoint = [(normal_model[q] - alpha * adjoint[q]) / beta for q in range(4)]
            vector = [adjoint[q] - beta * model[q] for q in range(4)]
            alpha = jnp.sqrt(inner(vector, vector) + eps_small)
            model = [value / alpha for value in vector]
            theta = sine * alpha
            rho_bar = -cosine * alpha
            search = [model[q] - theta / rho * search[q] for q in range(4)]

    lanes = lax.broadcasted_iota(jnp.int32, (ROWS, LANES), 1)
    mine = (lanes == device_index()).astype(jnp.float32)
    own = dot_exact(mine, jnp.concatenate(location, axis=0), NT)
    for q in range(4):
        out_ref[q : q + 1, :] = own[0:1, q * EV_DEV : (q + 1) * EV_DEV]


def passed_along(block, distance):
    count = lax.axis_size("g") * lax.axis_size("c")
    route = [(i - distance, i) for i in range(count) if 0 <= i - distance < count]
    return lax.ppermute(block, ("g", "c"), route)


def body(traces, ray_slowness, travel_time, pair_first, pair_second, pair_lag, pair_live):
    vmem = pl.BlockSpec(memory_space=pltpu.VMEM)
    smem = pl.BlockSpec(memory_space=pltpu.SMEM)
    params = pltpu.CompilerParams(vmem_limit_bytes=VMEM_BYTES)
    message = pl.pallas_call(
        pack_kernel,
        out_shape=jax.ShapeDtypeStruct((TRACES_DEV + 1, ROWS, LENGTH), jnp.float32),
        in_specs=[smem] + [vmem] * 5,
        out_specs=vmem,
        compiler_params=params,
        name="pack",
    )(
        pair_live,
        traces.reshape(TRACES_DEV, EV_DEV, LENGTH),
        ray_slowness,
        travel_time,
        pair_first.reshape(1, PAIR_DEV),
        pair_second.reshape(1, PAIR_DEV),
    )
    from_left = passed_along(message, 1)
    from_right = passed_along(message, -1)
    refined_shift, block = pl.pallas_call(
        shift_kernel,
        out_shape=(
            jax.ShapeDtypeStruct((STATIONS_DEV, PAIR_DEV), jnp.float32),
            jax.ShapeDtypeStruct((ROWS, LANES), jnp.float32),
        ),
        in_specs=[smem, smem] + [vmem] * 4,
        out_specs=(vmem, vmem),
        scratch_shapes=[
            pltpu.VMEM((TRACES_DEV * TRACE_ROWS + 2 * ROWS, LANES), jnp.float32),
            pltpu.VMEM((TRACES_DEV * PAIR_DEV * ROWS, LANES), jnp.float32),
            pltpu.VMEM((EV_DEV * LAGS, SPAN), jnp.bfloat16),
            pltpu.VMEM((EV_DEV * LAGS, SPAN), jnp.bfloat16),
        ],
        compiler_params=params,
        name="shifts",
    )(pair_second, pair_lag, message, from_left, from_right, pair_lag)
    block = lax.psum(block, "x")
    chips = lax.axis_size("g")
    copies = jnp.broadcast_to(block[None], (chips, ROWS, LANES))
    gathered = lax.all_to_all(copies, "g", 0, 0, tiled=True)
    gathered = lax.all_gather(gathered, "c", axis=0)
    location = pl.pallas_call(
        solve_kernel,
        out_shape=jax.ShapeDtypeStruct((4, EV_DEV), jnp.float32),
        in_specs=[vmem],
        out_specs=vmem,
        scratch_shapes=[pltpu.VMEM((ROWS * LANES, LANES), jnp.float32)],
        compiler_params=params,
        name="solve",
    )(gathered.reshape(2 * chips * ROWS, LANES))
    return refined_shift, location


def solution(mesh):
    ev, st = mesh.devices.shape
    fine = Mesh(mesh.devices.reshape(ev // 2, 2, st), ("g", "c", "x"))
    event_axes = ("g", "c")
    in_specs = (
        P("x", None, event_axes, None),
        P(None, "x", event_axes),
        P("x", event_axes),
        P(event_axes),
        P(event_axes),
        P("x", event_axes),
        P(event_axes),
    )
    out_specs = (P("x", event_axes), P(None, event_axes))
    return jax.shard_map(body, mesh=fine, in_specs=in_specs, out_specs=out_specs, check_vma=False)
```

```python
import jax
import jax.numpy as jnp
from jax import lax
from jax.experimental import pallas as pl
from jax.experimental.pallas import tpu as pltpu
from jax.sharding import Mesh
from jax.sharding import PartitionSpec as P

LAGS = 32
LANES = 128
ROWS = 8
EV_DEV = 8
NEAR = 3 * EV_DEV
STATIONS_DEV = 3
TRACES_DEV = 9
LENGTH = 1024
CHUNKS = LENGTH // LANES
QUARTER = LENGTH // 4
WINDOW = LENGTH // 2
SPAN = WINDOW + LANES
SPAN_CHUNKS = SPAN // LANES
PAIR_DEV = 128
TRACE_ROWS = NEAR * CHUNKS
VMEM_BYTES = 48 * 1024 * 1024
DEAD = -1000.0

eps_small = 1e-06
sample_step = 0.01
exact_mode = lax.Precision.HIGHEST
NT = (((1,), (1,)), ((), ()))
NN = (((1,), (0,)), ((), ()))


def device_index():
    return lax.axis_index("g") * 2 + lax.axis_index("c")


def dot_exact(left, right, dims):
    return lax.dot_general(
        left, right, dims, precision=exact_mode, preferred_element_type=jnp.float32
    )


def dot_bf16(left, right, dims):
    return lax.dot_general(left, right, dims, preferred_element_type=jnp.float32)


def split_bf16(values):
    high = values.astype(jnp.bfloat16)
    low = (values - high.astype(jnp.float32)).astype(jnp.bfloat16)
    return high, low


def pack_kernel(
    live_ref,
    traces_ref,
    slowness_ref,
    time_ref,
    first_ref,
    second_ref,
    lag_ref,
    out_ref,
    rows_ref,
    lanes_ref,
    live,
    slowness,
    time,
    first,
    second,
    lag,
    sems,
):
    copies = [
        pltpu.make_async_copy(source, target, sems.at[at])
        for at, (source, target) in enumerate(
            (
                (traces_ref, out_ref.at[pl.ds(0, TRACES_DEV)]),
                (live_ref, live),
                (slowness_ref, slowness),
                (time_ref, time),
                (first_ref, first),
                (second_ref, second),
                (lag_ref, lag),
            )
        )
    ]
    for copy in copies:
        copy.start()
    out_ref[TRACES_DEV] = jnp.zeros((ROWS, LENGTH), jnp.float32)
    for copy in copies[1:]:
        copy.wait()
    me = device_index()
    base = me * EV_DEV - EV_DEV
    slots = lax.broadcasted_iota(jnp.int32, (1, PAIR_DEV), 1)
    alive = slots < live[0]
    for row, ids in enumerate((first, second)):
        near = (ids[...] - base).astype(jnp.float32)
        out_ref[TRACES_DEV, row : row + 1, 0:LANES] = jnp.where(alive, near, DEAD)
    out_ref[TRACES_DEV, 0:STATIONS_DEV, LANES : LANES + EV_DEV] = time[...]
    for q in range(3):
        lane = (2 + q) * LANES
        out_ref[TRACES_DEV, 0:STATIONS_DEV, lane : lane + EV_DEV] = slowness[q]
    begin = lag[...] + (QUARTER - LAGS // 2)
    holder = lax.shift_right_arithmetic(second[...], 3)
    part = jnp.where(holder == me, 0, jnp.where(holder == jnp.bitwise_xor(me, 1), 1, 2))
    event = part * EV_DEV + jnp.bitwise_and(second[...], EV_DEV - 1)
    rows_ref[...] = event * CHUNKS + lax.shift_right_arithmetic(begin, 7)
    lanes_ref[...] = jnp.bitwise_and(begin, LANES - 1)
    copies[0].wait()


def fill_table(ref, table_ref, part):
    for item in range(TRACES_DEV):
        values = ref[item]
        power = jnp.sum(values * values, axis=1, keepdims=True)
        values = values * lax.rsqrt(power + eps_small)
        for chunk in range(CHUNKS):
            start = item * TRACE_ROWS + part * EV_DEV * CHUNKS + chunk
            table_ref[pl.ds(start, EV_DEV, stride=CHUNKS), :] = values[
                :, chunk * LANES : (chunk + 1) * LANES
            ]


def first_kernel(own_ref, high_ref, low_ref):
    for item in range(TRACES_DEV):
        window = own_ref[item, :, QUARTER : QUARTER + WINDOW]
        power = jnp.sum(window * window, axis=1, keepdims=True)
        window = window * lax.rsqrt(power + eps_small)
        padded = jnp.concatenate([window, jnp.zeros((EV_DEV, LANES), jnp.float32)], axis=1)
        for event in range(EV_DEV):
            wide = jnp.broadcast_to(padded[event : event + 1], (LAGS, SPAN))
            wide = pltpu.roll(wide, 0, 1, stride=1, stride_axis=0)
            high, low = split_bf16(wide)
            high_ref[item, pl.ds(event * LAGS, LAGS), :] = high
            low_ref[item, pl.ds(event * LAGS, LAGS), :] = low


def incidence(aux, offset):
    events = lax.broadcasted_iota(jnp.int32, (NEAR, PAIR_DEV), 0).astype(jnp.float32)
    starts = aux[0:1, 0:LANES] + offset
    ends = aux[1:2, 0:LANES] + offset
    return (events == starts).astype(jnp.float32) - (events == ends).astype(jnp.float32)


def near_block(left, own, right, part):
    lane = part * LANES
    return jnp.concatenate(
        [aux[0:STATIONS_DEV, lane : lane + EV_DEV] for aux in (left, own, right)], axis=1
    )


def shift_kernel(
    rows_ref,
    lanes_ref,
    own_ref,
    mate_ref,
    cross_ref,
    lag_ref,
    high_ref,
    low_ref,
    shift_ref,
    block_ref,
    table_ref,
    moved_ref,
):
    for part, ref in enumerate((own_ref, mate_ref, cross_ref)):
        fill_table(ref, table_ref, part)
    table_ref[pl.ds(TRACES_DEV * TRACE_ROWS, 2 * ROWS), :] = jnp.zeros(
        (2 * ROWS, LANES), jnp.float32
    )

    lane_ids = lax.broadcasted_iota(jnp.int32, (ROWS, LANES), 1)

    def align(slot, carry):
        for station in range(STATIONS_DEV):
            row = rows_ref[station, slot]
            lane = lanes_ref[station, slot]
            turn = jnp.bitwise_and(-lane, LANES - 1)
            keep = lane_ids >= lane
            for component in range(3):
                item = station * 3 + component
                here = table_ref[pl.ds(row + item * TRACE_ROWS, ROWS), :]
                after = table_ref[pl.ds(row + (item * TRACE_ROWS + 1), ROWS), :]
                moved = pltpu.roll(jnp.where(keep, here, after), turn, 1)
                to = pl.multiple_of((item * PAIR_DEV + slot) * ROWS, ROWS)
                moved_ref[pl.ds(to, ROWS), :] = moved
        return carry

    lax.fori_loop(0, PAIR_DEV, align, 0, unroll=8)

    aux_own = own_ref[TRACES_DEV]
    even = lax.axis_index("c") == 0
    aux_left = jnp.where(even, cross_ref[TRACES_DEV], mate_ref[TRACES_DEV])
    aux_right = jnp.where(even, mate_ref[TRACES_DEV], cross_ref[TRACES_DEV])

    energies = []
    for station in range(STATIONS_DEV):
        energy = jnp.zeros((PAIR_DEV, EV_DEV * LAGS), jnp.float32)
        for component in range(3):
            item = station * 3 + component
            pieces = [
                moved_ref[pl.ds(item * PAIR_DEV * ROWS + chunk, PAIR_DEV, stride=ROWS), :]
                for chunk in range(SPAN_CHUNKS)
            ]
            high, low = split_bf16(jnp.concatenate(pieces, axis=1))
            both = dot_bf16(jnp.concatenate([high, low], axis=0), high_ref[item], NT)
            xcorr = both[0:PAIR_DEV] + both[PAIR_DEV:] + dot_bf16(high, low_ref[item], NT)
            energy = energy + xcorr * xcorr
        energies.append(energy)
    lag_in_row = lax.broadcasted_iota(jnp.int32, (16, EV_DEV * LAGS), 1)
    row_ids = lax.broadcasted_iota(jnp.int32, (16, EV_DEV * LAGS), 0)
    centred = (lag_in_row % LAGS - LAGS // 2).astype(jnp.float32)
    weights = jnp.where(row_ids < EV_DEV, centred, 1.0)
    pick = jnp.where(lag_in_row // LAGS == row_ids % EV_DEV, weights, 0.0).astype(jnp.bfloat16)
    high, low = split_bf16(jnp.concatenate(energies, axis=0))
    sums = dot_bf16(pick, high, NT) + dot_bf16(pick, low, NT)
    events = lax.broadcasted_iota(jnp.int32, (EV_DEV, PAIR_DEV), 0).astype(jnp.float32)
    first_hot = (events == aux_own[0:1, 0:LANES] - EV_DEV).astype(jnp.float32)
    station_shift = []
    for station in range(STATIONS_DEV):
        lane = station * PAIR_DEV
        above = jnp.sum(sums[0:EV_DEV, lane : lane + PAIR_DEV] * first_hot, axis=0, keepdims=True)
        below = jnp.sum(sums[EV_DEV:, lane : lane + PAIR_DEV] * first_hot, axis=0, keepdims=True)
        station_shift.append(above / (below + eps_small))
    slots_alive = (aux_own[0:1, 0:LANES] >= 0.0).astype(jnp.float32)
    shift = jnp.concatenate(station_shift, axis=0) * slots_alive
    shift_ref[...] = shift

    signs = incidence(aux_own, 0.0)
    times = near_block(aux_left, aux_own, aux_right, 1)
    rhs = slots_alive * (
        sample_step * (lag_ref[...].astype(jnp.float32) + shift)
    ) - dot_exact(times, signs, NN)
    per_event = dot_exact(rhs, signs, NT)
    station_group = lax.axis_index("x")
    own_signs = signs[EV_DEV : 2 * EV_DEV].astype(jnp.bfloat16)
    counts = dot_bf16(own_signs, signs.astype(jnp.bfloat16), NT)
    for aux, offset in ((aux_left, -float(EV_DEV)), (aux_right, float(EV_DEV))):
        other = incidence(aux, offset).astype(jnp.bfloat16)
        counts = counts + dot_bf16(other[EV_DEV : 2 * EV_DEV], other, NT)
    block_ref[...] = jnp.zeros((ROWS, LANES), jnp.float32)
    for q in range(3):
        slowness = near_block(aux_left, aux_own, aux_right, 2 + q)
        block_ref[q : q + 1, 0:NEAR] = jnp.sum(slowness * per_event, axis=0, keepdims=True)
    block_ref[3:4, 0:NEAR] = jnp.sum(per_event, axis=0, keepdims=True)
    total = jnp.sum(jnp.sum(rhs * rhs, axis=1, keepdims=True), axis=0, keepdims=True)
    block_ref[0:1, NEAR : NEAR + 1] = total
    block_ref[:, 32 : 32 + NEAR] = jnp.where(station_group == 0, counts, 0.0)
    for group in range(4):
        row = 4 * (group // 2)
        lane = 64 + 32 * (group % 2)
        for q in range(3):
            own = aux_own[0:STATIONS_DEV, (2 + q) * LANES : (2 + q) * LANES + EV_DEV]
            at = lane + q * EV_DEV
            block_ref[row : row + STATIONS_DEV, at : at + EV_DEV] = jnp.where(
                station_group == group, own, 0.0
            )


def solve_kernel(gathered_ref, out_ref, rows_ref):
    half = LANES // 2
    tables = []
    for row in range(ROWS):
        for core in range(2):
            values = gathered_ref[pl.ds(core * half * ROWS + row, half, stride=ROWS), :]
            rows_ref[pl.ds(row * LANES + core, half, stride=2), :] = values
        tables.append(jnp.transpose(rows_ref[pl.ds(row * LANES, LANES), :]))

    def along(lower, own, upper):
        return own + pltpu.roll(upper, 1, 1) + pltpu.roll(lower, LANES - 1, 1)

    back = [along(tables[q][0:8], tables[q][8:16], tables[q][16:24]) for q in range(4)]
    counts = [
        [tables[a][32 + 8 * side : 40 + 8 * side] for side in range(3)] for a in range(EV_DEV)
    ]
    deriv = []
    for group in range(4):
        for station in range(STATIONS_DEV):
            table = tables[4 * (group // 2) + station]
            lane = 64 + 32 * (group % 2)
            deriv.append([table[lane + 8 * q : lane + 8 * q + 8] for q in range(3)])

    def total(values):
        return jnp.sum(jnp.sum(values, axis=1, keepdims=True), axis=0, keepdims=True)

    def inner(left, right):
        terms = left[0] * right[0]
        for q in range(1, 4):
            terms = terms + left[q] * right[q]
        return total(terms)

    def normal(model):
        result = [jnp.zeros((EV_DEV, LANES), jnp.float32) for _ in range(4)]
        for rates in deriv:
            data = model[3]
            for q in range(3):
                data = data + rates[q] * model[q]
            sides = [None, None, None]
            for a in range(EV_DEV):
                row = jnp.broadcast_to(data[a : a + 1], (EV_DEV, LANES))
                for side in range(3):
                    term = counts[a][side] * row
                    sides[side] = term if a == 0 else sides[side] + term
            mixed = along(*sides)
            for q in range(3):
                result[q] = result[q] + rates[q] * mixed
            result[3] = result[3] + mixed
        return result

    rhs_square = total(tables[0][NEAR : NEAR + 1])
    beta = jnp.sqrt(rhs_square + eps_small)
    unit_square = rhs_square / (beta * beta)
    adjoint = [value / beta for value in back]
    alpha = jnp.sqrt(inner(adjoint, adjoint) + eps_small)
    model = [value / alpha for value in adjoint]
    search = model
    location = [jnp.zeros((EV_DEV, LANES), jnp.float32) for _ in range(4)]
    phi_bar = beta
    rho_bar = alpha
    for turn in range(2):
        normal_model = normal(model)
        square = inner(model, normal_model) - 2.0 * alpha * inner(model, adjoint)
        square = jnp.maximum(square + alpha * alpha * unit_square, 0.0)
        beta = jnp.sqrt(square + eps_small)
        rho = jnp.sqrt(rho_bar * rho_bar + beta * beta)
        cosine = rho_bar / rho
        sine = beta / rho
        phi = cosine * phi_bar
        phi_bar = sine * phi_bar
        step = phi / rho
        location = [location[q] + step * search[q] for q in range(4)]
        if turn == 0:
            unit_square = square / (beta * beta)
            adjoint = [(normal_model[q] - alpha * adjoint[q]) / beta for q in range(4)]
            vector = [adjoint[q] - beta * model[q] for q in range(4)]
            alpha = jnp.sqrt(inner(vector, vector) + eps_small)
            model = [value / alpha for value in vector]
            theta = sine * alpha
            rho_bar = -cosine * alpha
            search = [model[q] - theta / rho * search[q] for q in range(4)]

    lanes = lax.broadcasted_iota(jnp.int32, (ROWS, LANES), 1)
    mine = (lanes == device_index()).astype(jnp.float32)
    own = dot_exact(mine, jnp.concatenate(location, axis=0), NT)
    for q in range(4):
        out_ref[q : q + 1, :] = own[0:1, q * EV_DEV : (q + 1) * EV_DEV]


def swapped(block, partner):
    count = lax.axis_size("g") * lax.axis_size("c")
    route = [(i, partner(i)) for i in range(count) if 0 <= partner(i) < count]
    return lax.ppermute(block, ("g", "c"), route)


def in_other_core(index):
    return index + 1 - 2 * (index % 2)


def in_other_chip(index):
    return index - 1 + 2 * (index % 2)


VMEM = pl.BlockSpec(memory_space=pltpu.VMEM)
SMEM = pl.BlockSpec(memory_space=pltpu.SMEM)
HBM = pl.BlockSpec(memory_space=pltpu.HBM)
PARAMS = pltpu.CompilerParams(vmem_limit_bytes=VMEM_BYTES)


def pack(traces, ray_slowness, travel_time, pair_first, pair_second, pair_lag, pair_live):
    return pl.pallas_call(
        pack_kernel,
        out_shape=(
            jax.ShapeDtypeStruct((TRACES_DEV + 1, ROWS, LENGTH), jnp.float32),
            jax.ShapeDtypeStruct((STATIONS_DEV, PAIR_DEV), jnp.int32),
            jax.ShapeDtypeStruct((STATIONS_DEV, PAIR_DEV), jnp.int32),
        ),
        in_specs=[HBM] * 7,
        out_specs=(VMEM, VMEM, VMEM),
        scratch_shapes=[
            pltpu.SMEM((1,), jnp.int32),
            pltpu.VMEM((3, STATIONS_DEV, EV_DEV), jnp.float32),
            pltpu.VMEM((STATIONS_DEV, EV_DEV), jnp.float32),
            pltpu.VMEM((1, PAIR_DEV), jnp.int32),
            pltpu.VMEM((1, PAIR_DEV), jnp.int32),
            pltpu.VMEM((STATIONS_DEV, PAIR_DEV), jnp.int32),
            pltpu.SemaphoreType.DMA((7,)),
        ],
        compiler_params=PARAMS,
        name="pack",
    )(
        pair_live,
        traces.reshape(TRACES_DEV, EV_DEV, LENGTH),
        ray_slowness,
        travel_time,
        pair_first.reshape(1, PAIR_DEV),
        pair_second.reshape(1, PAIR_DEV),
        pair_lag,
    )


def firsts(message):
    toeplitz = jax.ShapeDtypeStruct((TRACES_DEV, EV_DEV * LAGS, SPAN), jnp.bfloat16)
    return pl.pallas_call(
        first_kernel,
        out_shape=(toeplitz, toeplitz),
        in_specs=[VMEM],
        out_specs=(VMEM, VMEM),
        compiler_params=PARAMS,
        name="firsts",
    )(message)


def shifts(rows, lanes, message, from_mate, from_cross, pair_lag, high, low):
    return pl.pallas_call(
        shift_kernel,
        out_shape=(
            jax.ShapeDtypeStruct((STATIONS_DEV, PAIR_DEV), jnp.float32),
            jax.ShapeDtypeStruct((ROWS, LANES), jnp.float32),
        ),
        in_specs=[SMEM, SMEM] + [VMEM] * 6,
        out_specs=(VMEM, VMEM),
        scratch_shapes=[
            pltpu.VMEM((TRACES_DEV * TRACE_ROWS + 2 * ROWS, LANES), jnp.float32),
            pltpu.VMEM((TRACES_DEV * PAIR_DEV * ROWS, LANES), jnp.float32),
        ],
        compiler_params=PARAMS,
        name="shifts",
    )(rows, lanes, message, from_mate, from_cross, pair_lag, high, low)


def solve(gathered):
    return pl.pallas_call(
        solve_kernel,
        out_shape=jax.ShapeDtypeStruct((4, EV_DEV), jnp.float32),
        in_specs=[VMEM],
        out_specs=VMEM,
        scratch_shapes=[pltpu.VMEM((ROWS * LANES, LANES), jnp.float32)],
        compiler_params=PARAMS,
        name="solve",
    )(gathered)


def body(traces, ray_slowness, travel_time, pair_first, pair_second, pair_lag, pair_live):
    message, rows, lanes = pack(
        traces, ray_slowness, travel_time, pair_first, pair_second, pair_lag, pair_live
    )
    from_cross = swapped(message, in_other_chip)
    from_mate = swapped(message, in_other_core)
    high, low = firsts(message)
    refined_shift, block = shifts(
        rows, lanes, message, from_mate, from_cross, pair_lag, high, low
    )
    block = lax.psum(block, "x")
    chips = lax.axis_size("g")
    copies = jnp.broadcast_to(block[None], (chips, ROWS, LANES))
    gathered = lax.all_to_all(copies, "g", 0, 0, tiled=True)
    gathered = lax.all_gather(gathered, "c", axis=0)
    location = solve(gathered.reshape(2 * chips * ROWS, LANES))
    return refined_shift, location


def solution(mesh):
    ev, st = mesh.devices.shape
    fine = Mesh(mesh.devices.reshape(ev // 2, 2, st), ("g", "c", "x"))
    event_axes = ("g", "c")
    in_specs = (
        P("x", None, event_axes, None),
        P(None, "x", event_axes),
        P("x", event_axes),
        P(event_axes),
        P(event_axes),
        P("x", event_axes),
        P(event_axes),
    )
    out_specs = (P("x", event_axes), P(None, event_axes))
    return jax.shard_map(body, mesh=fine, in_specs=in_specs, out_specs=out_specs, check_vma=False)
```

```python
import jax
import jax.numpy as jnp
from jax import lax
from jax.experimental import pallas as pl
from jax.experimental.pallas import tpu as pltpu
from jax.sharding import Mesh
from jax.sharding import PartitionSpec as P

LAGS = 32
LANES = 128
ROWS = 8
EV_DEV = 8
NEAR = 3 * EV_DEV
STATIONS_DEV = 3
TRACES_DEV = 9
LENGTH = 1024
CHUNKS = LENGTH // LANES
QUARTER = LENGTH // 4
WINDOW = LENGTH // 2
SPAN = WINDOW + LANES
SPAN_CHUNKS = SPAN // LANES
PAIR_DEV = 128
PART_ROWS = TRACES_DEV * EV_DEV * CHUNKS
VMEM_BYTES = 24 * 1024 * 1024
WHOLE_BYTES = 60 * 1024 * 1024
DEAD = -1000.0
PAYLOAD = 5 * LANES
SQUARE_AT = 4 * NEAR

eps_small = 1e-06
sample_step = 0.01
exact_mode = lax.Precision.HIGHEST
NT = (((1,), (1,)), ((), ()))
NN = (((1,), (0,)), ((), ()))


def device_index():
    return lax.axis_index("g") * 2 + lax.axis_index("c")


def dot_exact(left, right, dims):
    return lax.dot_general(
        left, right, dims, precision=exact_mode, preferred_element_type=jnp.float32
    )


def dot_bf16(left, right, dims):
    return lax.dot_general(left, right, dims, preferred_element_type=jnp.float32)


def count_place(event):
    return LANES + NEAR * event if event < 5 else 2 * LANES + NEAR * (event - 5)


def rate_place(group, station, q):
    index = (group * STATIONS_DEV + station) * 3 + q
    return 3 * LANES + 8 * index if index < 32 else 2 * LANES + 96 + 8 * (index - 32)


def dot_signs(left, signs, dims):
    high = left.astype(jnp.bfloat16)
    rest = left - high.astype(jnp.float32)
    middle = rest.astype(jnp.bfloat16)
    low = (rest - middle.astype(jnp.float32)).astype(jnp.bfloat16)
    rows = left.shape[0]
    parts = dot_bf16(jnp.concatenate([high, middle, low], axis=0), signs, dims)
    return parts[0:rows] + parts[rows : 2 * rows] + parts[2 * rows :]


def split_bf16(values):
    high = values.astype(jnp.bfloat16)
    low = (values - high.astype(jnp.float32)).astype(jnp.bfloat16)
    return high, low


def pack_kernel(
    live_ref,
    traces_ref,
    slowness_ref,
    time_ref,
    first_ref,
    second_ref,
    lag_ref,
    out_ref,
    traces,
    live,
    slowness,
    time,
    first,
    second,
    lag,
    aux,
    sems,
):
    pairs = [(traces_ref.at[pl.ds(3 * part, 3)], traces.at[pl.ds(3 * part, 3)]) for part in range(3)]
    pairs += [
        (live_ref, live),
        (slowness_ref, slowness),
        (time_ref, time),
        (first_ref, first),
        (second_ref, second),
        (lag_ref, lag),
    ]
    copies = [
        pltpu.make_async_copy(source, target, sems.at[at])
        for at, (source, target) in enumerate(pairs)
    ]
    moves = [
        pltpu.make_async_copy(traces.at[part], out_ref.at[part], sems.at[len(copies) + at])
        for at, part in enumerate([pl.ds(3 * third, 3) for third in range(3)])
    ]
    for copy in copies:
        copy.start()
    aux[...] = jnp.zeros((ROWS, LENGTH), jnp.float32)
    for copy in copies[3:]:
        copy.wait()
    base = device_index() * EV_DEV - EV_DEV
    slots = lax.broadcasted_iota(jnp.int32, (1, PAIR_DEV), 1)
    alive = slots < live[0]
    for row, ids in enumerate((first, second)):
        near = (ids[...] - base).astype(jnp.float32)
        aux[row : row + 1, 0:LANES] = jnp.where(alive, near, DEAD)
        aux[row : row + 1, 6 * LANES : 7 * LANES] = near
    aux[0:STATIONS_DEV, LANES : LANES + EV_DEV] = time[...]
    for q in range(3):
        lane = (2 + q) * LANES
        aux[0:STATIONS_DEV, lane : lane + EV_DEV] = slowness[q]
    aux[0:STATIONS_DEV, 5 * LANES : 6 * LANES] = lag[...].astype(jnp.float32)
    moves.append(pltpu.make_async_copy(aux, out_ref.at[TRACES_DEV], sems.at[len(copies) + 3]))
    moves[3].start()
    for third in range(3):
        copies[third].wait()
        moves[third].start()
    for move in moves:
        move.wait()


def first_kernel(own_ref, high_ref, low_ref, places_ref, pick_ref, rates_ref):
    for item in range(TRACES_DEV):
        window = own_ref[item, :, QUARTER : QUARTER + WINDOW]
        power = jnp.sum(window * window, axis=1, keepdims=True)
        window = window * lax.rsqrt(power + eps_small)
        padded = jnp.concatenate([window, jnp.zeros((EV_DEV, LANES), jnp.float32)], axis=1)
        for event in range(EV_DEV):
            wide = jnp.broadcast_to(padded[event : event + 1], (LAGS, SPAN))
            wide = pltpu.roll(wide, 0, 1, stride=1, stride_axis=0)
            high, low = split_bf16(wide)
            high_ref[item, pl.ds(event * LAGS, LAGS), :] = high
            low_ref[item, pl.ds(event * LAGS, LAGS), :] = low
    aux = own_ref[TRACES_DEV]
    first = aux[0:1, 6 * LANES : 7 * LANES].astype(jnp.int32)
    second = aux[1:2, 6 * LANES : 7 * LANES].astype(jnp.int32)
    begin = aux[0:STATIONS_DEV, 5 * LANES : 6 * LANES].astype(jnp.int32) + (QUARTER - LAGS // 2)
    side = lax.shift_right_arithmetic(second, 3)
    mate_side = 2 - 2 * lax.axis_index("c")
    far = jnp.logical_and(side != 1, side != mate_side)
    part = jnp.where(side == 1, 0, jnp.where(far, 2, 1))
    event = jnp.bitwise_and(second, EV_DEV - 1)
    rows = part * PART_ROWS + event * CHUNKS + lax.shift_right_arithmetic(begin, 7)
    upper = lax.broadcasted_iota(jnp.int32, (PAIR_DEV, PAIR_DEV), 0)
    lower = lax.broadcasted_iota(jnp.int32, (PAIR_DEV, PAIR_DEV), 1)
    ahead = (upper <= lower).astype(jnp.bfloat16)
    marked = jnp.broadcast_to(far.astype(jnp.float32), (ROWS, PAIR_DEV)).astype(jnp.bfloat16)
    place = dot_bf16(marked, ahead, NN)[0:1]
    place = jnp.where(far, place - 1.0, -1.0)
    hot = (upper.astype(jnp.float32) == place).astype(jnp.bfloat16)
    slots = lax.broadcasted_iota(jnp.int32, (ROWS, PAIR_DEV), 1).astype(jnp.bfloat16)
    listed = dot_bf16(slots, hot, NT)[0:1].astype(jnp.int32)
    count = jnp.sum(far.astype(jnp.float32), axis=1, keepdims=True).astype(jnp.int32)
    spare = lax.broadcasted_iota(jnp.int32, (1, PAIR_DEV), 1) >= count
    listed = jnp.where(spare, listed[:, 0:1], listed)
    places_ref[0:3, :] = rows
    places_ref[3:6, :] = jnp.bitwise_and(begin, LANES - 1)
    places_ref[6:7, :] = listed
    places_ref[7:8, :] = jnp.broadcast_to(count, (1, PAIR_DEV))
    ends = jnp.bitwise_and(first, EV_DEV - 1).astype(jnp.float32)
    column = jnp.transpose(jnp.broadcast_to(ends, (LANES, PAIR_DEV)))
    groups = lax.broadcasted_iota(jnp.int32, (PAIR_DEV, LANES), 1) // LAGS
    for half in range(2):
        mine = column == (groups + half * (LANES // LAGS)).astype(jnp.float32)
        pick_ref[:, half * LANES : (half + 1) * LANES] = mine.astype(jnp.float32)
    rates_ref[...] = jnp.zeros((1, PAYLOAD), jnp.float32)
    for station in range(STATIONS_DEV):
        for q in range(3):
            lane = (2 + q) * LANES
            own = aux[station : station + 1, lane : lane + EV_DEV]
            for group in range(4):
                at = rate_place(group, station, q)
                rates_ref[:, at : at + EV_DEV] = jnp.where(
                    lax.axis_index("x") == group, own, 0.0
                )


def fill_table(ref, table_ref, part):
    for item in range(TRACES_DEV):
        values = ref[item]
        power = jnp.sum(values * values, axis=1, keepdims=True)
        values = values * lax.rsqrt(power + eps_small)
        for chunk in range(CHUNKS):
            start = part * PART_ROWS + item * EV_DEV * CHUNKS + chunk
            table_ref[pl.ds(start, EV_DEV, stride=CHUNKS), :] = values[
                :, chunk * LANES : (chunk + 1) * LANES
            ]


def align(places_ref, table_ref, moved_ref, slot, offset):
    lane_ids = lax.broadcasted_iota(jnp.int32, (ROWS, LANES), 1)
    for station in range(STATIONS_DEV):
        row = places_ref[station, slot] - offset
        lane = places_ref[3 + station, slot]
        turn = jnp.bitwise_and(-lane, LANES - 1)
        keep = lane_ids >= lane
        for component in range(3):
            item = station * 3 + component
            at = item * EV_DEV * CHUNKS
            here = table_ref[pl.ds(row + at, ROWS), :]
            after = table_ref[pl.ds(row + (at + 1), ROWS), :]
            moved = pltpu.roll(jnp.where(keep, here, after), turn, 1)
            to = pl.multiple_of((item * PAIR_DEV + slot) * ROWS, ROWS)
            moved_ref[pl.ds(to, ROWS), :] = moved


def early_kernel(places_ref, own_ref, mate_ref, moved_ref, table_ref):
    table_ref[pl.ds(2 * PART_ROWS, PART_ROWS + 2 * ROWS), :] = jnp.zeros(
        (PART_ROWS + 2 * ROWS, LANES), jnp.float32
    )
    fill_table(own_ref, table_ref, 0)
    fill_table(mate_ref, table_ref, 1)

    def step(slot, carry):
        align(places_ref, table_ref, moved_ref, slot, 0)
        return carry

    lax.fori_loop(0, PAIR_DEV, step, 0, unroll=32)


def incidence(aux, offset):
    events = lax.broadcasted_iota(jnp.int32, (NEAR, PAIR_DEV), 0).astype(jnp.float32)
    starts = aux[0:1, 0:LANES] + offset
    ends = aux[1:2, 0:LANES] + offset
    return (events == starts).astype(jnp.float32) - (events == ends).astype(jnp.float32)


def near_block(left, own, right, part):
    lane = part * LANES
    return jnp.concatenate(
        [aux[0:STATIONS_DEV, lane : lane + EV_DEV] for aux in (left, own, right)], axis=1
    )


def late_kernel(
    places_in_ref,
    moved_in_ref,
    own_ref,
    mate_ref,
    cross_ref,
    high_ref,
    low_ref,
    pick_ref,
    rates_ref,
    shift_ref,
    block_ref,
    moved_ref,
    table_ref,
    places_ref,
    sem,
):
    del moved_in_ref
    fetch = pltpu.make_async_copy(places_in_ref, places_ref, sem)
    fetch.start()
    table_ref[pl.ds(PART_ROWS, 2 * ROWS), :] = jnp.zeros((2 * ROWS, LANES), jnp.float32)
    fill_table(cross_ref, table_ref, 0)
    fetch.wait()

    def step(index, carry):
        for turn in range(8):
            slot = places_ref[6, index * 8 + turn]
            align(places_ref, table_ref, moved_ref, slot, 2 * PART_ROWS)
        return carry

    lax.fori_loop(0, lax.shift_right_arithmetic(places_ref[7, 0] + 7, 3), step, 0)

    aux_own = own_ref[TRACES_DEV]
    even = lax.axis_index("c") == 0
    aux_left = jnp.where(even, cross_ref[TRACES_DEV], mate_ref[TRACES_DEV])
    aux_right = jnp.where(even, mate_ref[TRACES_DEV], cross_ref[TRACES_DEV])

    lane_ids = lax.broadcasted_iota(jnp.int32, (1, LANES), 1)
    centred = (lane_ids - LAGS // 2).astype(jnp.float32)
    weights = jnp.where(lane_ids < LAGS, centred, jnp.where(lane_ids < 2 * LAGS, 1.0, 0.0))
    folded = []
    for station in range(STATIONS_DEV):
        energy = jnp.zeros((PAIR_DEV, EV_DEV * LAGS), jnp.float32)
        for component in range(3):
            item = station * 3 + component
            pieces = [
                moved_ref[pl.ds(item * PAIR_DEV * ROWS + chunk, PAIR_DEV, stride=ROWS), :]
                for chunk in range(SPAN_CHUNKS)
            ]
            high, low = split_bf16(jnp.concatenate(pieces, axis=1))
            both = dot_bf16(jnp.concatenate([high, low], axis=0), high_ref[item], NT)
            xcorr = both[0:PAIR_DEV] + both[PAIR_DEV:] + dot_bf16(high, low_ref[item], NT)
            energy = energy + xcorr * xcorr
        energy = energy * pick_ref[...]
        energy = energy[:, 0:LANES] + energy[:, LANES:]
        energy = energy + pltpu.roll(energy, LANES // 2, 1)
        energy = energy + pltpu.roll(energy, LANES // 4, 1)
        folded.append(energy)
    pair = folded[0] * weights + folded[1] * pltpu.roll(weights, LANES // 2, 1)
    tables = [jnp.transpose(pair), jnp.transpose(folded[2] * weights)]
    station_shift = []
    for station in range(STATIONS_DEV):
        rows = tables[station // 2][(station % 2) * 2 * LAGS : (station % 2 + 1) * 2 * LAGS]
        above = jnp.sum(rows[0:LAGS], axis=0, keepdims=True)
        below = jnp.sum(rows[LAGS:], axis=0, keepdims=True)
        station_shift.append(above / (below + eps_small))
    slots_alive = (aux_own[0:1, 0:LANES] >= 0.0).astype(jnp.float32)
    shift = jnp.concatenate(station_shift, axis=0) * slots_alive
    shift_ref[...] = shift

    signs = incidence(aux_own, 0.0).astype(jnp.bfloat16)
    times = dot_signs(near_block(aux_left, aux_own, aux_right, 1), signs, NN)
    lags = aux_own[0:STATIONS_DEV, 5 * LANES : 6 * LANES]
    rhs = slots_alive * (sample_step * (lags + shift)) - times
    per_event = dot_signs(rhs, signs, NT)
    counts = dot_bf16(signs[EV_DEV : 2 * EV_DEV], signs, NT)
    for aux, offset in ((aux_left, -float(EV_DEV)), (aux_right, float(EV_DEV))):
        other = incidence(aux, offset).astype(jnp.bfloat16)
        counts = counts + dot_bf16(other[EV_DEV : 2 * EV_DEV], other, NT)
    counts = jnp.where(lax.axis_index("x") == 0, counts, 0.0)
    block_ref[...] = rates_ref[...]
    for event in range(EV_DEV):
        at = count_place(event)
        block_ref[:, at : at + NEAR] = counts[event : event + 1]
    for q in range(4):
        terms = per_event
        if q < 3:
            terms = terms * near_block(aux_left, aux_own, aux_right, 2 + q)
        block_ref[:, q * NEAR : (q + 1) * NEAR] = jnp.sum(terms, axis=0, keepdims=True)
    total = jnp.sum(jnp.sum(rhs * rhs, axis=1, keepdims=True), axis=0, keepdims=True)
    block_ref[:, SQUARE_AT : SQUARE_AT + 1] = total


def solve_kernel(gathered_ref, shift_ref, out_ref, shift_out_ref, rows_ref):
    shift_out_ref[...] = shift_ref[...]
    half = LANES // 2
    tables = []
    for row in range(PAYLOAD // LANES):
        for core in range(2):
            values = gathered_ref[pl.ds(core * half, half), row * LANES : (row + 1) * LANES]
            rows_ref[pl.ds(row * LANES + core, half, stride=2), :] = values
        tables.append(jnp.transpose(rows_ref[pl.ds(row * LANES, LANES), :]))

    def read(at):
        return tables[at // LANES][at % LANES : at % LANES + 8]

    def along(lower, own, upper):
        return own + pltpu.roll(upper, 1, 1) + pltpu.roll(lower, LANES - 1, 1)

    back = [along(*[read(q * NEAR + 8 * side) for side in range(3)]) for q in range(4)]
    counts = [[read(count_place(a) + 8 * side) for side in range(3)] for a in range(EV_DEV)]
    deriv = [
        [read(rate_place(group, station, q)) for q in range(3)]
        for group in range(4)
        for station in range(STATIONS_DEV)
    ]

    def total(values):
        return jnp.sum(jnp.sum(values, axis=1, keepdims=True), axis=0, keepdims=True)

    def inner(left, right):
        terms = left[0] * right[0]
        for q in range(1, 4):
            terms = terms + left[q] * right[q]
        return total(terms)

    def normal(model):
        result = [jnp.zeros((EV_DEV, LANES), jnp.float32) for _ in range(4)]
        for rates in deriv:
            data = model[3]
            for q in range(3):
                data = data + rates[q] * model[q]
            sides = [None, None, None]
            for a in range(EV_DEV):
                row = jnp.broadcast_to(data[a : a + 1], (EV_DEV, LANES))
                for side in range(3):
                    term = counts[a][side] * row
                    sides[side] = term if a == 0 else sides[side] + term
            mixed = along(*sides)
            for q in range(3):
                result[q] = result[q] + rates[q] * mixed
            result[3] = result[3] + mixed
        return result

    rhs_square = total(tables[0][SQUARE_AT : SQUARE_AT + 1])
    beta = jnp.sqrt(rhs_square + eps_small)
    unit_square = rhs_square / (beta * beta)
    adjoint = [value / beta for value in back]
    alpha = jnp.sqrt(inner(adjoint, adjoint) + eps_small)
    model = [value / alpha for value in adjoint]
    search = model
    location = [jnp.zeros((EV_DEV, LANES), jnp.float32) for _ in range(4)]
    phi_bar = beta
    rho_bar = alpha
    for turn in range(2):
        normal_model = normal(model)
        square = inner(model, normal_model) - 2.0 * alpha * inner(model, adjoint)
        square = jnp.maximum(square + alpha * alpha * unit_square, 0.0)
        beta = jnp.sqrt(square + eps_small)
        rho = jnp.sqrt(rho_bar * rho_bar + beta * beta)
        cosine = rho_bar / rho
        sine = beta / rho
        phi = cosine * phi_bar
        phi_bar = sine * phi_bar
        step = phi / rho
        location = [location[q] + step * search[q] for q in range(4)]
        if turn == 0:
            unit_square = square / (beta * beta)
            adjoint = [(normal_model[q] - alpha * adjoint[q]) / beta for q in range(4)]
            vector = [adjoint[q] - beta * model[q] for q in range(4)]
            alpha = jnp.sqrt(inner(vector, vector) + eps_small)
            model = [value / alpha for value in vector]
            theta = sine * alpha
            rho_bar = -cosine * alpha
            search = [model[q] - theta / rho * search[q] for q in range(4)]

    lanes = lax.broadcasted_iota(jnp.int32, (ROWS, LANES), 1)
    mine = (lanes == device_index()).astype(jnp.float32)
    own = dot_exact(mine, jnp.concatenate(location, axis=0), NT)
    for q in range(4):
        out_ref[q : q + 1, :] = own[0:1, q * EV_DEV : (q + 1) * EV_DEV]


def swapped(block, partner):
    count = lax.axis_size("g") * lax.axis_size("c")
    route = [(i, partner(i)) for i in range(count) if 0 <= partner(i) < count]
    return lax.ppermute(block, ("g", "c"), route)


def in_other_core(index):
    return index + 1 - 2 * (index % 2)


def in_other_chip(index):
    return index - 1 + 2 * (index % 2)


VMEM = pl.BlockSpec(memory_space=pltpu.VMEM)
SMEM = pl.BlockSpec(memory_space=pltpu.SMEM)
HBM = pl.BlockSpec(memory_space=pltpu.HBM)
PARAMS = pltpu.CompilerParams(vmem_limit_bytes=VMEM_BYTES)
WHOLE_VMEM = pltpu.CompilerParams(vmem_limit_bytes=WHOLE_BYTES)


def pack(traces, ray_slowness, travel_time, pair_first, pair_second, pair_lag, pair_live):
    return pl.pallas_call(
        pack_kernel,
        out_shape=jax.ShapeDtypeStruct((TRACES_DEV + 1, ROWS, LENGTH), jnp.float32),
        in_specs=[HBM] * 7,
        out_specs=HBM,
        scratch_shapes=[
            pltpu.VMEM((TRACES_DEV, EV_DEV, LENGTH), jnp.float32),
            pltpu.SMEM((1,), jnp.int32),
            pltpu.VMEM((3, STATIONS_DEV, EV_DEV), jnp.float32),
            pltpu.VMEM((STATIONS_DEV, EV_DEV), jnp.float32),
            pltpu.VMEM((1, PAIR_DEV), jnp.int32),
            pltpu.VMEM((1, PAIR_DEV), jnp.int32),
            pltpu.VMEM((STATIONS_DEV, PAIR_DEV), jnp.int32),
            pltpu.VMEM((ROWS, LENGTH), jnp.float32),
            pltpu.SemaphoreType.DMA((13,)),
        ],
        compiler_params=WHOLE_VMEM,
        name="pack",
    )(
        pair_live,
        traces.reshape(TRACES_DEV, EV_DEV, LENGTH),
        ray_slowness,
        travel_time,
        pair_first.reshape(1, PAIR_DEV),
        pair_second.reshape(1, PAIR_DEV),
        pair_lag,
    )


def firsts(message):
    toeplitz = jax.ShapeDtypeStruct((TRACES_DEV, EV_DEV * LAGS, SPAN), jnp.bfloat16)
    return pl.pallas_call(
        first_kernel,
        out_shape=(
            toeplitz,
            toeplitz,
            jax.ShapeDtypeStruct((ROWS, PAIR_DEV), jnp.int32),
            jax.ShapeDtypeStruct((PAIR_DEV, EV_DEV * LAGS), jnp.float32),
            jax.ShapeDtypeStruct((1, PAYLOAD), jnp.float32),
        ),
        in_specs=[VMEM],
        out_specs=(VMEM,) * 5,
        compiler_params=PARAMS,
        name="firsts",
    )(message)


MOVED = jax.ShapeDtypeStruct((TRACES_DEV * PAIR_DEV * ROWS, LANES), jnp.float32)


def early(places, message, from_mate):
    return pl.pallas_call(
        early_kernel,
        out_shape=MOVED,
        in_specs=[SMEM, VMEM, VMEM],
        out_specs=VMEM,
        scratch_shapes=[pltpu.VMEM((3 * PART_ROWS + 2 * ROWS, LANES), jnp.float32)],
        compiler_params=PARAMS,
        name="early",
    )(places, message, from_mate)


def late(places, moved, message, from_mate, from_cross, high, low, pick, rates):
    refined_shift, block, _ = pl.pallas_call(
        late_kernel,
        out_shape=(
            jax.ShapeDtypeStruct((STATIONS_DEV, PAIR_DEV), jnp.float32),
            jax.ShapeDtypeStruct((1, PAYLOAD), jnp.float32),
            MOVED,
        ),
        in_specs=[VMEM] * 9,
        out_specs=(VMEM, VMEM, VMEM),
        scratch_shapes=[
            pltpu.VMEM((PART_ROWS + 2 * ROWS, LANES), jnp.float32),
            pltpu.SMEM((ROWS, PAIR_DEV), jnp.int32),
            pltpu.SemaphoreType.DMA,
        ],
        input_output_aliases={1: 2},
        compiler_params=PARAMS,
        name="late",
    )(places, moved, message, from_mate, from_cross, high, low, pick, rates)
    return refined_shift, block


def solve(gathered, shift):
    return pl.pallas_call(
        solve_kernel,
        out_shape=(
            jax.ShapeDtypeStruct((4, EV_DEV), jnp.float32),
            jax.ShapeDtypeStruct((STATIONS_DEV, PAIR_DEV), jnp.float32),
        ),
        in_specs=[VMEM, VMEM],
        out_specs=(VMEM, VMEM),
        scratch_shapes=[pltpu.VMEM((PAYLOAD, LANES), jnp.float32)],
        compiler_params=PARAMS,
        name="solve",
    )(gathered, shift)


def body(traces, ray_slowness, travel_time, pair_first, pair_second, pair_lag, pair_live):
    message = pack(
        traces, ray_slowness, travel_time, pair_first, pair_second, pair_lag, pair_live
    )
    from_cross = swapped(message, in_other_chip)
    from_mate = swapped(message, in_other_core)
    high, low, places, pick, rates = firsts(message)
    moved = early(places, message, from_mate)
    shift, block = late(
        places, moved, message, from_mate, from_cross, high, low, pick, rates
    )
    block = lax.psum(block, "x")
    chips = lax.axis_size("g")
    copies = jnp.broadcast_to(block, (chips, PAYLOAD))
    gathered = lax.all_to_all(copies, "g", 0, 0, tiled=True)
    gathered = lax.all_gather(gathered, "c", axis=0)
    location, refined_shift = solve(gathered.reshape(2 * chips, PAYLOAD), shift)
    return refined_shift, location


def solution(mesh):
    ev, st = mesh.devices.shape
    fine = Mesh(mesh.devices.reshape(ev // 2, 2, st), ("g", "c", "x"))
    event_axes = ("g", "c")
    in_specs = (
        P("x", None, event_axes, None),
        P(None, "x", event_axes),
        P("x", event_axes),
        P(event_axes),
        P(event_axes),
        P("x", event_axes),
        P(event_axes),
    )
    out_specs = (P("x", event_axes), P(None, event_axes))
    return jax.shard_map(body, mesh=fine, in_specs=in_specs, out_specs=out_specs, check_vma=False)
```

```python
import jax
import jax.numpy as jnp
from jax import lax
from jax.experimental import pallas as pl
from jax.experimental.pallas import tpu as pltpu
from jax.sharding import Mesh
from jax.sharding import PartitionSpec as P

LAGS = 32
LANES = 128
ROWS = 8
EV_DEV = 8
NEAR = 3 * EV_DEV
STATIONS_DEV = 3
TRACES_DEV = 9
LENGTH = 1024
CHUNKS = LENGTH // LANES
QUARTER = LENGTH // 4
WINDOW = LENGTH // 2
SPAN = WINDOW + LANES
SPAN_CHUNKS = SPAN // LANES
PAIR_DEV = 128
PART_ROWS = TRACES_DEV * EV_DEV * CHUNKS
VMEM_BYTES = 24 * 1024 * 1024
DEAD = -1000.0
PAYLOAD = 5 * LANES
SQUARE_AT = 4 * NEAR

eps_small = 1e-06
sample_step = 0.01
exact_mode = lax.Precision.HIGHEST
NT = (((1,), (1,)), ((), ()))
NN = (((1,), (0,)), ((), ()))


def device_index():
    return lax.axis_index("g") * 2 + lax.axis_index("c")


def dot_exact(left, right, dims):
    return lax.dot_general(
        left, right, dims, precision=exact_mode, preferred_element_type=jnp.float32
    )


def dot_bf16(left, right, dims):
    return lax.dot_general(left, right, dims, preferred_element_type=jnp.float32)


def count_place(event):
    return LANES + NEAR * event if event < 5 else 2 * LANES + NEAR * (event - 5)


def rate_place(group, station, q):
    index = (group * STATIONS_DEV + station) * 3 + q
    return 3 * LANES + 8 * index if index < 32 else 2 * LANES + 96 + 8 * (index - 32)


def dot_signs(left, signs, dims):
    high = left.astype(jnp.bfloat16)
    rest = left - high.astype(jnp.float32)
    middle = rest.astype(jnp.bfloat16)
    low = (rest - middle.astype(jnp.float32)).astype(jnp.bfloat16)
    rows = left.shape[0]
    parts = dot_bf16(jnp.concatenate([high, middle, low], axis=0), signs, dims)
    return parts[0:rows] + parts[rows : 2 * rows] + parts[2 * rows :]


def split_bf16(values):
    high = values.astype(jnp.bfloat16)
    low = (values - high.astype(jnp.float32)).astype(jnp.bfloat16)
    return high, low


def pack_kernel(
    live_ref,
    traces_ref,
    slowness_ref,
    time_ref,
    first_ref,
    second_ref,
    lag_ref,
    out_ref,
    slowness,
    time,
    first,
    second,
    lag,
    sems,
):
    pairs = [
        (traces_ref, out_ref.at[pl.ds(0, TRACES_DEV)]),
        (slowness_ref, slowness),
        (time_ref, time),
        (first_ref, first),
        (second_ref, second),
        (lag_ref, lag),
    ]
    copies = [
        pltpu.make_async_copy(source, target, sems.at[at])
        for at, (source, target) in enumerate(pairs)
    ]
    for copy in copies:
        copy.start()
    aux = out_ref.at[TRACES_DEV]
    aux[...] = jnp.zeros((ROWS, LENGTH), jnp.float32)
    for copy in copies[1:]:
        copy.wait()
    base = device_index() * EV_DEV - EV_DEV
    slots = lax.broadcasted_iota(jnp.int32, (1, PAIR_DEV), 1)
    alive = slots < live_ref[0]
    for row, ids in enumerate((first, second)):
        near = (ids[...] - base).astype(jnp.float32)
        aux[row : row + 1, 0:LANES] = jnp.where(alive, near, DEAD)
        aux[row : row + 1, 6 * LANES : 7 * LANES] = near
    aux[0:STATIONS_DEV, LANES : LANES + EV_DEV] = time[...]
    for q in range(3):
        lane = (2 + q) * LANES
        aux[0:STATIONS_DEV, lane : lane + EV_DEV] = slowness[q]
    aux[0:STATIONS_DEV, 5 * LANES : 6 * LANES] = lag[...].astype(jnp.float32)
    copies[0].wait()


def first_kernel(own_ref, high_ref, low_ref, places_ref, pick_ref, rates_ref):
    for item in range(TRACES_DEV):
        window = own_ref[item, :, QUARTER : QUARTER + WINDOW]
        power = jnp.sum(window * window, axis=1, keepdims=True)
        window = window * lax.rsqrt(power + eps_small)
        padded = jnp.concatenate([window, jnp.zeros((EV_DEV, LANES), jnp.float32)], axis=1)
        for event in range(EV_DEV):
            wide = jnp.broadcast_to(padded[event : event + 1], (LAGS, SPAN))
            wide = pltpu.roll(wide, 0, 1, stride=1, stride_axis=0)
            high, low = split_bf16(wide)
            high_ref[item, pl.ds(event * LAGS, LAGS), :] = high
            low_ref[item, pl.ds(event * LAGS, LAGS), :] = low
    aux = own_ref[TRACES_DEV]
    first = aux[0:1, 6 * LANES : 7 * LANES].astype(jnp.int32)
    second = aux[1:2, 6 * LANES : 7 * LANES].astype(jnp.int32)
    begin = aux[0:STATIONS_DEV, 5 * LANES : 6 * LANES].astype(jnp.int32) + (QUARTER - LAGS // 2)
    side = lax.shift_right_arithmetic(second, 3)
    mate_side = 2 - 2 * lax.axis_index("c")
    away = jnp.logical_and(side != 1, side != mate_side)
    part = jnp.where(side == 1, 0, jnp.where(away, 2, 1))
    alive = aux[0:1, 0:LANES] >= 0.0
    far = jnp.logical_and(away, alive)
    event = jnp.bitwise_and(second, EV_DEV - 1)
    rows = part * PART_ROWS + event * CHUNKS + lax.shift_right_arithmetic(begin, 7)
    upper = lax.broadcasted_iota(jnp.int32, (PAIR_DEV, PAIR_DEV), 0)
    lower = lax.broadcasted_iota(jnp.int32, (PAIR_DEV, PAIR_DEV), 1)
    ahead = (upper <= lower).astype(jnp.bfloat16)
    marked = jnp.broadcast_to(far.astype(jnp.float32), (ROWS, PAIR_DEV)).astype(jnp.bfloat16)
    place = dot_bf16(marked, ahead, NN)[0:1]
    place = jnp.where(far, place - 1.0, -1.0)
    hot = (upper.astype(jnp.float32) == place).astype(jnp.bfloat16)
    slots = lax.broadcasted_iota(jnp.int32, (ROWS, PAIR_DEV), 1).astype(jnp.bfloat16)
    listed = dot_bf16(slots, hot, NT)[0:1].astype(jnp.int32)
    count = jnp.sum(far.astype(jnp.float32), axis=1, keepdims=True).astype(jnp.int32)
    spare = lax.broadcasted_iota(jnp.int32, (1, PAIR_DEV), 1) >= count
    listed = jnp.where(spare, listed[:, 0:1], listed)
    places_ref[0:3, :] = rows
    places_ref[3:6, :] = jnp.bitwise_and(begin, LANES - 1)
    places_ref[6:7, :] = listed
    live_count = jnp.sum(alive.astype(jnp.float32), axis=1, keepdims=True).astype(jnp.int32)
    places_ref[7:8, :] = jnp.where(
        lax.broadcasted_iota(jnp.int32, (1, PAIR_DEV), 1) == 0, count, live_count
    )
    ends = jnp.bitwise_and(first, EV_DEV - 1).astype(jnp.float32)
    column = jnp.transpose(jnp.broadcast_to(ends, (LANES, PAIR_DEV)))
    groups = lax.broadcasted_iota(jnp.int32, (PAIR_DEV, LANES), 1) // LAGS
    for half in range(2):
        mine = column == (groups + half * (LANES // LAGS)).astype(jnp.float32)
        pick_ref[:, half * LANES : (half + 1) * LANES] = mine.astype(jnp.float32)
    rates_ref[...] = jnp.zeros((1, PAYLOAD), jnp.float32)
    for station in range(STATIONS_DEV):
        for q in range(3):
            lane = (2 + q) * LANES
            own = aux[station : station + 1, lane : lane + EV_DEV]
            for group in range(4):
                at = rate_place(group, station, q)
                rates_ref[:, at : at + EV_DEV] = jnp.where(
                    lax.axis_index("x") == group, own, 0.0
                )


def fill_table(ref, table_ref, part):
    for item in range(TRACES_DEV):
        values = ref[item]
        power = jnp.sum(values * values, axis=1, keepdims=True)
        values = values * lax.rsqrt(power + eps_small)
        for chunk in range(CHUNKS):
            start = part * PART_ROWS + item * EV_DEV * CHUNKS + chunk
            table_ref[pl.ds(start, EV_DEV, stride=CHUNKS), :] = values[
                :, chunk * LANES : (chunk + 1) * LANES
            ]


def align(places_ref, table_ref, moved_ref, slot, offset):
    lane_ids = lax.broadcasted_iota(jnp.int32, (ROWS, LANES), 1)
    for station in range(STATIONS_DEV):
        row = places_ref[station, slot] - offset
        lane = places_ref[3 + station, slot]
        turn = jnp.bitwise_and(-lane, LANES - 1)
        keep = lane_ids >= lane
        for component in range(3):
            item = station * 3 + component
            at = item * EV_DEV * CHUNKS
            here = table_ref[pl.ds(row + at, ROWS), :]
            after = table_ref[pl.ds(row + (at + 1), ROWS), :]
            moved = pltpu.roll(jnp.where(keep, here, after), turn, 1)
            to = pl.multiple_of((item * PAIR_DEV + slot) * ROWS, ROWS)
            moved_ref[pl.ds(to, ROWS), :] = moved


def early_kernel(places_ref, chip_ref, moved_ref, table_ref):
    table_ref[pl.ds(2 * PART_ROWS, PART_ROWS + 2 * ROWS), :] = jnp.zeros(
        (PART_ROWS + 2 * ROWS, LANES), jnp.float32
    )
    core = lax.axis_index("c")
    fill_table(chip_ref.at[core], table_ref, 0)
    fill_table(chip_ref.at[1 - core], table_ref, 1)

    def step(index, carry):
        for turn in range(16):
            align(places_ref, table_ref, moved_ref, index * 16 + turn, 0)
        return carry

    lax.fori_loop(0, lax.shift_right_arithmetic(places_ref[7, 1] + 15, 4), step, 0)


def incidence(aux, offset):
    events = lax.broadcasted_iota(jnp.int32, (NEAR, PAIR_DEV), 0).astype(jnp.float32)
    starts = aux[0:1, 0:LANES] + offset
    ends = aux[1:2, 0:LANES] + offset
    return (events == starts).astype(jnp.float32) - (events == ends).astype(jnp.float32)


def near_block(left, own, right, part):
    lane = part * LANES
    return jnp.concatenate(
        [aux[0:STATIONS_DEV, lane : lane + EV_DEV] for aux in (left, own, right)], axis=1
    )


def late_kernel(
    places_in_ref,
    moved_in_ref,
    chip_ref,
    cross_ref,
    high_ref,
    low_ref,
    pick_ref,
    rates_ref,
    shift_ref,
    block_ref,
    moved_ref,
    table_ref,
    places_ref,
    sem,
):
    del moved_in_ref
    fetch = pltpu.make_async_copy(places_in_ref, places_ref, sem)
    fetch.start()
    table_ref[pl.ds(PART_ROWS, 2 * ROWS), :] = jnp.zeros((2 * ROWS, LANES), jnp.float32)
    fill_table(cross_ref, table_ref, 0)
    fetch.wait()

    def step(index, carry):
        for turn in range(8):
            slot = places_ref[6, index * 8 + turn]
            align(places_ref, table_ref, moved_ref, slot, 2 * PART_ROWS)
        return carry

    lax.fori_loop(0, lax.shift_right_arithmetic(places_ref[7, 0] + 7, 3), step, 0)

    core = lax.axis_index("c")
    aux_own = chip_ref[core, TRACES_DEV]
    aux_left = jnp.where(core == 0, cross_ref[TRACES_DEV], chip_ref[0, TRACES_DEV])
    aux_right = jnp.where(core == 0, chip_ref[1, TRACES_DEV], cross_ref[TRACES_DEV])

    lane_ids = lax.broadcasted_iota(jnp.int32, (1, LANES), 1)
    centred = (lane_ids - LAGS // 2).astype(jnp.float32)
    weights = jnp.where(lane_ids < LAGS, centred, jnp.where(lane_ids < 2 * LAGS, 1.0, 0.0))
    folded = []
    for station in range(STATIONS_DEV):
        energy = jnp.zeros((PAIR_DEV, EV_DEV * LAGS), jnp.float32)
        for component in range(3):
            item = station * 3 + component
            pieces = [
                moved_ref[pl.ds(item * PAIR_DEV * ROWS + chunk, PAIR_DEV, stride=ROWS), :]
                for chunk in range(SPAN_CHUNKS)
            ]
            high, low = split_bf16(jnp.concatenate(pieces, axis=1))
            both = dot_bf16(jnp.concatenate([high, low], axis=0), high_ref[item], NT)
            xcorr = both[0:PAIR_DEV] + both[PAIR_DEV:] + dot_bf16(high, low_ref[item], NT)
            energy = energy + xcorr * xcorr
        energy = energy * pick_ref[...]
        energy = energy[:, 0:LANES] + energy[:, LANES:]
        energy = energy + pltpu.roll(energy, LANES // 2, 1)
        energy = energy + pltpu.roll(energy, LANES // 4, 1)
        folded.append(energy)
    pair = folded[0] * weights + folded[1] * pltpu.roll(weights, LANES // 2, 1)
    tables = [jnp.transpose(pair), jnp.transpose(folded[2] * weights)]
    station_shift = []
    for station in range(STATIONS_DEV):
        rows = tables[station // 2][(station % 2) * 2 * LAGS : (station % 2 + 1) * 2 * LAGS]
        above = jnp.sum(rows[0:LAGS], axis=0, keepdims=True)
        below = jnp.sum(rows[LAGS:], axis=0, keepdims=True)
        station_shift.append(above / (below + eps_small))
    alive = aux_own[0:1, 0:LANES] >= 0.0
    shift = jnp.where(alive, jnp.concatenate(station_shift, axis=0), 0.0)
    shift_ref[...] = shift

    signs = incidence(aux_own, 0.0).astype(jnp.bfloat16)
    times = dot_signs(near_block(aux_left, aux_own, aux_right, 1), signs, NN)
    lags = aux_own[0:STATIONS_DEV, 5 * LANES : 6 * LANES]
    rhs = jnp.where(alive, sample_step * (lags + shift), 0.0) - times
    per_event = dot_signs(rhs, signs, NT)
    counts = dot_bf16(signs[EV_DEV : 2 * EV_DEV], signs, NT)
    for aux, offset in ((aux_left, -float(EV_DEV)), (aux_right, float(EV_DEV))):
        other = incidence(aux, offset).astype(jnp.bfloat16)
        counts = counts + dot_bf16(other[EV_DEV : 2 * EV_DEV], other, NT)
    counts = jnp.where(lax.axis_index("x") == 0, counts, 0.0)
    block_ref[...] = rates_ref[...]
    for event in range(EV_DEV):
        at = count_place(event)
        block_ref[:, at : at + NEAR] = counts[event : event + 1]
    for q in range(4):
        terms = per_event
        if q < 3:
            terms = terms * near_block(aux_left, aux_own, aux_right, 2 + q)
        block_ref[:, q * NEAR : (q + 1) * NEAR] = jnp.sum(terms, axis=0, keepdims=True)
    total = jnp.sum(jnp.sum(rhs * rhs, axis=1, keepdims=True), axis=0, keepdims=True)
    block_ref[:, SQUARE_AT : SQUARE_AT + 1] = total


def solve_kernel(gathered_ref, shift_ref, out_ref, shift_out_ref, rows_ref):
    shift_out_ref[...] = shift_ref[...]
    half = LANES // 2
    tables = []
    for row in range(PAYLOAD // LANES):
        for core in range(2):
            values = gathered_ref[pl.ds(core * half, half), row * LANES : (row + 1) * LANES]
            rows_ref[pl.ds(row * LANES + core, half, stride=2), :] = values
        tables.append(jnp.transpose(rows_ref[pl.ds(row * LANES, LANES), :]))

    def read(at):
        return tables[at // LANES][at % LANES : at % LANES + 8]

    def along(lower, own, upper):
        return own + pltpu.roll(upper, 1, 1) + pltpu.roll(lower, LANES - 1, 1)

    back = [along(*[read(q * NEAR + 8 * side) for side in range(3)]) for q in range(4)]
    counts = [[read(count_place(a) + 8 * side) for side in range(3)] for a in range(EV_DEV)]
    deriv = [
        [read(rate_place(group, station, q)) for q in range(3)]
        for group in range(4)
        for station in range(STATIONS_DEV)
    ]

    def total(values):
        return jnp.sum(jnp.sum(values, axis=1, keepdims=True), axis=0, keepdims=True)

    def inner(left, right):
        terms = left[0] * right[0]
        for q in range(1, 4):
            terms = terms + left[q] * right[q]
        return total(terms)

    def normal(model):
        result = [jnp.zeros((EV_DEV, LANES), jnp.float32) for _ in range(4)]
        for rates in deriv:
            data = model[3]
            for q in range(3):
                data = data + rates[q] * model[q]
            sides = [None, None, None]
            for a in range(EV_DEV):
                row = jnp.broadcast_to(data[a : a + 1], (EV_DEV, LANES))
                for side in range(3):
                    term = counts[a][side] * row
                    sides[side] = term if a == 0 else sides[side] + term
            mixed = along(*sides)
            for q in range(3):
                result[q] = result[q] + rates[q] * mixed
            result[3] = result[3] + mixed
        return result

    rhs_square = total(tables[0][SQUARE_AT : SQUARE_AT + 1])
    beta = jnp.sqrt(rhs_square + eps_small)
    unit_square = rhs_square / (beta * beta)
    adjoint = [value / beta for value in back]
    alpha = jnp.sqrt(inner(adjoint, adjoint) + eps_small)
    model = [value / alpha for value in adjoint]
    search = model
    location = [jnp.zeros((EV_DEV, LANES), jnp.float32) for _ in range(4)]
    phi_bar = beta
    rho_bar = alpha
    for turn in range(2):
        normal_model = normal(model)
        square = inner(model, normal_model) - 2.0 * alpha * inner(model, adjoint)
        square = jnp.maximum(square + alpha * alpha * unit_square, 0.0)
        beta = jnp.sqrt(square + eps_small)
        rho = jnp.sqrt(rho_bar * rho_bar + beta * beta)
        cosine = rho_bar / rho
        sine = beta / rho
        phi = cosine * phi_bar
        phi_bar = sine * phi_bar
        step = phi / rho
        location = [location[q] + step * search[q] for q in range(4)]
        if turn == 0:
            unit_square = square / (beta * beta)
            adjoint = [(normal_model[q] - alpha * adjoint[q]) / beta for q in range(4)]
            vector = [adjoint[q] - beta * model[q] for q in range(4)]
            alpha = jnp.sqrt(inner(vector, vector) + eps_small)
            model = [value / alpha for value in vector]
            theta = sine * alpha
            rho_bar = -cosine * alpha
            search = [model[q] - theta / rho * search[q] for q in range(4)]

    lanes = lax.broadcasted_iota(jnp.int32, (ROWS, LANES), 1)
    mine = (lanes == device_index()).astype(jnp.float32)
    own = dot_exact(mine, jnp.concatenate(location, axis=0), NT)
    for q in range(4):
        out_ref[q : q + 1, :] = own[0:1, q * EV_DEV : (q + 1) * EV_DEV]


def from_other_chip(block):
    count = lax.axis_size("g") * lax.axis_size("c")
    partners = [(i, i - 1 + 2 * (i % 2)) for i in range(count)]
    route = [(i, other) for i, other in partners if 0 <= other < count]
    return lax.ppermute(block, ("g", "c"), route)


VMEM = pl.BlockSpec(memory_space=pltpu.VMEM)
SMEM = pl.BlockSpec(memory_space=pltpu.SMEM)
HBM = pl.BlockSpec(memory_space=pltpu.HBM)
PARAMS = pltpu.CompilerParams(vmem_limit_bytes=VMEM_BYTES)


def pack(traces, ray_slowness, travel_time, pair_first, pair_second, pair_lag, pair_live):
    arguments = (
        traces.reshape(TRACES_DEV, EV_DEV, LENGTH),
        ray_slowness,
        travel_time,
        pair_first.reshape(1, PAIR_DEV),
        pair_second.reshape(1, PAIR_DEV),
        pair_lag,
    )
    return pl.pallas_call(
        pack_kernel,
        out_shape=pltpu.VMEM((TRACES_DEV + 1, ROWS, LENGTH), jnp.float32),
        in_specs=[SMEM] + [HBM] * 6,
        out_specs=VMEM,
        scratch_shapes=[
            pltpu.VMEM((3, STATIONS_DEV, EV_DEV), jnp.float32),
            pltpu.VMEM((STATIONS_DEV, EV_DEV), jnp.float32),
            pltpu.VMEM((1, PAIR_DEV), jnp.int32),
            pltpu.VMEM((1, PAIR_DEV), jnp.int32),
            pltpu.VMEM((STATIONS_DEV, PAIR_DEV), jnp.int32),
            pltpu.SemaphoreType.DMA((6,)),
        ],
        compiler_params=PARAMS,
        name="pack",
    )(pair_live, *[pltpu.with_memory_space_constraint(value, pltpu.HBM) for value in arguments])


def firsts(message):
    toeplitz = jax.ShapeDtypeStruct((TRACES_DEV, EV_DEV * LAGS, SPAN), jnp.bfloat16)
    return pl.pallas_call(
        first_kernel,
        out_shape=(
            toeplitz,
            toeplitz,
            jax.ShapeDtypeStruct((ROWS, PAIR_DEV), jnp.int32),
            jax.ShapeDtypeStruct((PAIR_DEV, EV_DEV * LAGS), jnp.float32),
            jax.ShapeDtypeStruct((1, PAYLOAD), jnp.float32),
        ),
        in_specs=[VMEM],
        out_specs=(VMEM,) * 5,
        compiler_params=PARAMS,
        name="firsts",
    )(message)


MOVED = jax.ShapeDtypeStruct((TRACES_DEV * PAIR_DEV * ROWS, LANES), jnp.float32)


def early(places, chip):
    return pl.pallas_call(
        early_kernel,
        out_shape=MOVED,
        in_specs=[SMEM, VMEM],
        out_specs=VMEM,
        scratch_shapes=[pltpu.VMEM((3 * PART_ROWS + 2 * ROWS, LANES), jnp.float32)],
        compiler_params=PARAMS,
        name="early",
    )(places, chip)


def late(places, moved, chip, from_cross, high, low, pick, rates):
    refined_shift, block, _ = pl.pallas_call(
        late_kernel,
        out_shape=(
            jax.ShapeDtypeStruct((STATIONS_DEV, PAIR_DEV), jnp.float32),
            jax.ShapeDtypeStruct((1, PAYLOAD), jnp.float32),
            MOVED,
        ),
        in_specs=[VMEM] * 8,
        out_specs=(VMEM, VMEM, VMEM),
        scratch_shapes=[
            pltpu.VMEM((PART_ROWS + 2 * ROWS, LANES), jnp.float32),
            pltpu.SMEM((ROWS, PAIR_DEV), jnp.int32),
            pltpu.SemaphoreType.DMA,
        ],
        input_output_aliases={1: 2},
        compiler_params=PARAMS,
        name="late",
    )(places, moved, chip, from_cross, high, low, pick, rates)
    return refined_shift, block


def solve(gathered, shift):
    return pl.pallas_call(
        solve_kernel,
        out_shape=(
            jax.ShapeDtypeStruct((4, EV_DEV), jnp.float32),
            jax.ShapeDtypeStruct((STATIONS_DEV, PAIR_DEV), jnp.float32),
        ),
        in_specs=[VMEM, VMEM],
        out_specs=(VMEM, VMEM),
        scratch_shapes=[pltpu.VMEM((PAYLOAD, LANES), jnp.float32)],
        compiler_params=PARAMS,
        name="solve",
    )(gathered, shift)


def body(traces, ray_slowness, travel_time, pair_first, pair_second, pair_lag, pair_live):
    message = pack(
        traces, ray_slowness, travel_time, pair_first, pair_second, pair_lag, pair_live
    )
    from_cross = from_other_chip(message)
    high, low, places, pick, rates = firsts(message)
    chip = lax.all_gather(message, "c", axis=0)
    moved = early(places, chip)
    shift, block = late(places, moved, chip, from_cross, high, low, pick, rates)
    block = lax.psum(block, "x")
    chips = lax.axis_size("g")
    copies = jnp.broadcast_to(block, (chips, PAYLOAD))
    gathered = lax.all_to_all(copies, "g", 0, 0, tiled=True)
    gathered = lax.all_gather(gathered, "c", axis=0)
    location, refined_shift = solve(gathered.reshape(2 * chips, PAYLOAD), shift)
    return refined_shift, location


def solution(mesh):
    ev, st = mesh.devices.shape
    fine = Mesh(mesh.devices.reshape(ev // 2, 2, st), ("g", "c", "x"))
    event_axes = ("g", "c")
    in_specs = (
        P("x", None, event_axes, None),
        P(None, "x", event_axes),
        P("x", event_axes),
        P(event_axes),
        P(event_axes),
        P("x", event_axes),
        P(event_axes),
    )
    out_specs = (P("x", event_axes), P(None, event_axes))
    return jax.shard_map(body, mesh=fine, in_specs=in_specs, out_specs=out_specs, check_vma=False)
```

```python
import jax
import jax.numpy as jnp
from jax import lax
from jax.experimental import pallas as pl
from jax.experimental.pallas import tpu as pltpu
from jax.sharding import Mesh
from jax.sharding import PartitionSpec as P

LAGS = 32
LANES = 128
ROWS = 8
EV_DEV = 8
NEAR = 3 * EV_DEV
STATIONS_DEV = 3
TRACES_DEV = 9
LENGTH = 1024
CHUNKS = LENGTH // LANES
QUARTER = LENGTH // 4
WINDOW = LENGTH // 2
SPAN = WINDOW + LANES
SPAN_CHUNKS = SPAN // LANES
PAIR_DEV = 128
PART_ROWS = TRACES_DEV * EV_DEV * CHUNKS
VMEM_BYTES = 24 * 1024 * 1024
DEAD = -1000.0
PAYLOAD = 5 * LANES
SQUARE_AT = 4 * NEAR

eps_small = 1e-06
sample_step = 0.01
exact_mode = lax.Precision.HIGHEST
NT = (((1,), (1,)), ((), ()))
NN = (((1,), (0,)), ((), ()))


def device_index():
    return lax.axis_index("g") * 2 + lax.axis_index("c")


def dot_exact(left, right, dims):
    return lax.dot_general(
        left, right, dims, precision=exact_mode, preferred_element_type=jnp.float32
    )


def dot_bf16(left, right, dims):
    return lax.dot_general(left, right, dims, preferred_element_type=jnp.float32)


def count_place(event):
    return LANES + NEAR * event if event < 5 else 2 * LANES + NEAR * (event - 5)


def rate_place(group, station, q):
    index = (group * STATIONS_DEV + station) * 3 + q
    return 3 * LANES + 8 * index if index < 32 else 2 * LANES + 96 + 8 * (index - 32)


def dot_signs(left, signs, dims):
    high = left.astype(jnp.bfloat16)
    rest = left - high.astype(jnp.float32)
    middle = rest.astype(jnp.bfloat16)
    low = (rest - middle.astype(jnp.float32)).astype(jnp.bfloat16)
    rows = left.shape[0]
    parts = dot_bf16(jnp.concatenate([high, middle, low], axis=0), signs, dims)
    return parts[0:rows] + parts[rows : 2 * rows] + parts[2 * rows :]


def split_bf16(values):
    high = values.astype(jnp.bfloat16)
    low = (values - high.astype(jnp.float32)).astype(jnp.bfloat16)
    return high, low


def pack_kernel(
    live_ref,
    traces_ref,
    slowness_ref,
    time_ref,
    first_ref,
    second_ref,
    lag_ref,
    out_ref,
    slowness,
    time,
    first,
    second,
    lag,
    sems,
):
    pairs = [
        (traces_ref, out_ref.at[pl.ds(0, TRACES_DEV)]),
        (slowness_ref, slowness),
        (time_ref, time),
        (first_ref, first),
        (second_ref, second),
        (lag_ref, lag),
    ]
    copies = [
        pltpu.make_async_copy(source, target, sems.at[at])
        for at, (source, target) in enumerate(pairs)
    ]
    for copy in copies:
        copy.start()
    aux = out_ref.at[TRACES_DEV]
    aux[...] = jnp.zeros((ROWS, LENGTH), jnp.float32)
    for copy in copies[1:]:
        copy.wait()
    base = device_index() * EV_DEV - EV_DEV
    slots = lax.broadcasted_iota(jnp.int32, (1, PAIR_DEV), 1)
    alive = slots < live_ref[0]
    for row, ids in enumerate((first, second)):
        near = (ids[...] - base).astype(jnp.float32)
        aux[row : row + 1, 0:LANES] = jnp.where(alive, near, DEAD)
        aux[row : row + 1, 6 * LANES : 7 * LANES] = near
    aux[0:STATIONS_DEV, LANES : LANES + EV_DEV] = time[...]
    for q in range(3):
        lane = (2 + q) * LANES
        aux[0:STATIONS_DEV, lane : lane + EV_DEV] = slowness[q]
    aux[0:STATIONS_DEV, 5 * LANES : 6 * LANES] = lag[...].astype(jnp.float32)
    copies[0].wait()


def first_kernel(own_ref, high_ref, low_ref, places_ref, pick_ref, rates_ref):
    for item in range(TRACES_DEV):
        window = own_ref[item, :, QUARTER : QUARTER + WINDOW]
        power = jnp.sum(window * window, axis=1, keepdims=True)
        window = window * lax.rsqrt(power + eps_small)
        padded = jnp.concatenate([window, jnp.zeros((EV_DEV, LANES), jnp.float32)], axis=1)
        for event in range(EV_DEV):
            wide = jnp.broadcast_to(padded[event : event + 1], (LAGS, SPAN))
            wide = pltpu.roll(wide, 0, 1, stride=1, stride_axis=0)
            high, low = split_bf16(wide)
            high_ref[item, pl.ds(event * LAGS, LAGS), :] = high
            low_ref[item, pl.ds(event * LAGS, LAGS), :] = low
    aux = own_ref[TRACES_DEV]
    first = aux[0:1, 6 * LANES : 7 * LANES].astype(jnp.int32)
    second = aux[1:2, 6 * LANES : 7 * LANES].astype(jnp.int32)
    begin = aux[0:STATIONS_DEV, 5 * LANES : 6 * LANES].astype(jnp.int32) + (QUARTER - LAGS // 2)
    side = lax.shift_right_arithmetic(second, 3)
    mate_side = 2 - 2 * lax.axis_index("c")
    away = jnp.logical_and(side != 1, side != mate_side)
    part = jnp.where(side == 1, 0, jnp.where(away, 2, 1))
    alive = aux[0:1, 0:LANES] >= 0.0
    far = jnp.logical_and(away, alive)
    event = jnp.bitwise_and(second, EV_DEV - 1)
    rows = part * PART_ROWS + event * CHUNKS + lax.shift_right_arithmetic(begin, 7)
    upper = lax.broadcasted_iota(jnp.int32, (PAIR_DEV, PAIR_DEV), 0)
    lower = lax.broadcasted_iota(jnp.int32, (PAIR_DEV, PAIR_DEV), 1)
    ahead = (upper <= lower).astype(jnp.bfloat16)
    marked = jnp.broadcast_to(far.astype(jnp.float32), (ROWS, PAIR_DEV)).astype(jnp.bfloat16)
    place = dot_bf16(marked, ahead, NN)[0:1]
    place = jnp.where(far, place - 1.0, -1.0)
    hot = (upper.astype(jnp.float32) == place).astype(jnp.bfloat16)
    slots = lax.broadcasted_iota(jnp.int32, (ROWS, PAIR_DEV), 1).astype(jnp.bfloat16)
    listed = dot_bf16(slots, hot, NT)[0:1].astype(jnp.int32)
    count = jnp.sum(far.astype(jnp.float32), axis=1, keepdims=True).astype(jnp.int32)
    spare = lax.broadcasted_iota(jnp.int32, (1, PAIR_DEV), 1) >= count
    listed = jnp.where(spare, listed[:, 0:1], listed)
    places_ref[0:3, :] = rows
    places_ref[3:6, :] = jnp.bitwise_and(begin, LANES - 1)
    places_ref[6:7, :] = listed
    live_count = jnp.sum(alive.astype(jnp.float32), axis=1, keepdims=True).astype(jnp.int32)
    places_ref[7:8, :] = jnp.where(
        lax.broadcasted_iota(jnp.int32, (1, PAIR_DEV), 1) == 0, count, live_count
    )
    ends = jnp.bitwise_and(first, EV_DEV - 1).astype(jnp.float32)
    column = jnp.transpose(jnp.broadcast_to(ends, (LANES, PAIR_DEV)))
    groups = lax.broadcasted_iota(jnp.int32, (PAIR_DEV, LANES), 1) // LAGS
    for half in range(2):
        mine = column == (groups + half * (LANES // LAGS)).astype(jnp.float32)
        pick_ref[:, half * LANES : (half + 1) * LANES] = mine.astype(jnp.float32)
    rates_ref[...] = jnp.zeros((1, PAYLOAD), jnp.float32)
    for station in range(STATIONS_DEV):
        for q in range(3):
            lane = (2 + q) * LANES
            own = aux[station : station + 1, lane : lane + EV_DEV]
            for group in range(4):
                at = rate_place(group, station, q)
                rates_ref[:, at : at + EV_DEV] = jnp.where(
                    lax.axis_index("x") == group, own, 0.0
                )


def fill_table(ref, table_ref, part):
    for item in range(TRACES_DEV):
        values = ref[item]
        power = jnp.sum(values * values, axis=1, keepdims=True)
        values = values * lax.rsqrt(power + eps_small)
        for chunk in range(CHUNKS):
            start = part * PART_ROWS + item * EV_DEV * CHUNKS + chunk
            table_ref[pl.ds(start, EV_DEV, stride=CHUNKS), :] = values[
                :, chunk * LANES : (chunk + 1) * LANES
            ]


def align(places_ref, table_ref, moved_ref, slot, offset):
    lane_ids = lax.broadcasted_iota(jnp.int32, (ROWS, LANES), 1)
    for station in range(STATIONS_DEV):
        row = places_ref[station, slot] - offset
        lane = places_ref[3 + station, slot]
        turn = jnp.bitwise_and(-lane, LANES - 1)
        keep = lane_ids >= lane
        for component in range(3):
            item = station * 3 + component
            at = item * EV_DEV * CHUNKS
            here = table_ref[pl.ds(row + at, ROWS), :]
            after = table_ref[pl.ds(row + (at + 1), ROWS), :]
            moved = pltpu.roll(jnp.where(keep, here, after), turn, 1)
            to = pl.multiple_of((item * PAIR_DEV + slot) * ROWS, ROWS)
            moved_ref[pl.ds(to, ROWS), :] = moved


def early_kernel(places_ref, chip_ref, moved_ref, table_ref):
    table_ref[pl.ds(2 * PART_ROWS, PART_ROWS + 2 * ROWS), :] = jnp.zeros(
        (PART_ROWS + 2 * ROWS, LANES), jnp.float32
    )
    core = lax.axis_index("c")
    fill_table(chip_ref.at[core], table_ref, 0)
    fill_table(chip_ref.at[1 - core], table_ref, 1)

    def step(index, carry):
        for turn in range(16):
            align(places_ref, table_ref, moved_ref, index * 16 + turn, 0)
        return carry

    lax.fori_loop(0, lax.shift_right_arithmetic(places_ref[7, 1] + 15, 4), step, 0)


def incidence(aux, offset):
    events = lax.broadcasted_iota(jnp.int32, (NEAR, PAIR_DEV), 0).astype(jnp.float32)
    starts = aux[0:1, 0:LANES] + offset
    ends = aux[1:2, 0:LANES] + offset
    return (events == starts).astype(jnp.float32) - (events == ends).astype(jnp.float32)


def near_block(left, own, right, part):
    lane = part * LANES
    return jnp.concatenate(
        [aux[0:STATIONS_DEV, lane : lane + EV_DEV] for aux in (left, own, right)], axis=1
    )


def late_kernel(
    places_in_ref,
    moved_in_ref,
    chip_ref,
    cross_ref,
    high_ref,
    low_ref,
    pick_ref,
    rates_ref,
    shift_ref,
    block_ref,
    moved_ref,
    table_ref,
    places_ref,
    sem,
):
    del moved_in_ref
    fetch = pltpu.make_async_copy(places_in_ref, places_ref, sem)
    fetch.start()
    table_ref[pl.ds(PART_ROWS, 2 * ROWS), :] = jnp.zeros((2 * ROWS, LANES), jnp.float32)
    fill_table(cross_ref, table_ref, 0)
    fetch.wait()

    def step(index, carry):
        for turn in range(8):
            slot = places_ref[6, index * 8 + turn]
            align(places_ref, table_ref, moved_ref, slot, 2 * PART_ROWS)
        return carry

    lax.fori_loop(0, lax.shift_right_arithmetic(places_ref[7, 0] + 7, 3), step, 0)

    core = lax.axis_index("c")
    aux_own = chip_ref[core, TRACES_DEV]
    aux_left = jnp.where(core == 0, cross_ref[TRACES_DEV], chip_ref[0, TRACES_DEV])
    aux_right = jnp.where(core == 0, chip_ref[1, TRACES_DEV], cross_ref[TRACES_DEV])

    lane_ids = lax.broadcasted_iota(jnp.int32, (1, LANES), 1)
    centred = (lane_ids - LAGS // 2).astype(jnp.float32)
    weights = jnp.where(lane_ids < LAGS, centred, jnp.where(lane_ids < 2 * LAGS, 1.0, 0.0))
    folded = []
    for station in range(STATIONS_DEV):
        energy = jnp.zeros((PAIR_DEV, EV_DEV * LAGS), jnp.float32)
        for component in range(3):
            item = station * 3 + component
            pieces = [
                moved_ref[pl.ds(item * PAIR_DEV * ROWS + chunk, PAIR_DEV, stride=ROWS), :]
                for chunk in range(SPAN_CHUNKS)
            ]
            high, low = split_bf16(jnp.concatenate(pieces, axis=1))
            both = dot_bf16(jnp.concatenate([high, low], axis=0), high_ref[item], NT)
            xcorr = both[0:PAIR_DEV] + both[PAIR_DEV:] + dot_bf16(high, low_ref[item], NT)
            energy = energy + xcorr * xcorr
        energy = energy * pick_ref[...]
        energy = energy[:, 0:LANES] + energy[:, LANES:]
        energy = energy + pltpu.roll(energy, LANES // 2, 1)
        energy = energy + pltpu.roll(energy, LANES // 4, 1)
        folded.append(energy)
    pair = folded[0] * weights + folded[1] * pltpu.roll(weights, LANES // 2, 1)
    tables = [jnp.transpose(pair), jnp.transpose(folded[2] * weights)]
    station_shift = []
    for station in range(STATIONS_DEV):
        rows = tables[station // 2][(station % 2) * 2 * LAGS : (station % 2 + 1) * 2 * LAGS]
        above = jnp.sum(rows[0:LAGS], axis=0, keepdims=True)
        below = jnp.sum(rows[LAGS:], axis=0, keepdims=True)
        station_shift.append(above / (below + eps_small))
    alive = aux_own[0:1, 0:LANES] >= 0.0
    shift = jnp.where(alive, jnp.concatenate(station_shift, axis=0), 0.0)
    shift_ref[...] = shift

    signs = incidence(aux_own, 0.0).astype(jnp.bfloat16)
    times = dot_signs(near_block(aux_left, aux_own, aux_right, 1), signs, NN)
    lags = aux_own[0:STATIONS_DEV, 5 * LANES : 6 * LANES]
    rhs = jnp.where(alive, sample_step * (lags + shift), 0.0) - times
    per_event = dot_signs(rhs, signs, NT)
    counts = dot_bf16(signs[EV_DEV : 2 * EV_DEV], signs, NT)
    for aux, offset in ((aux_left, -float(EV_DEV)), (aux_right, float(EV_DEV))):
        other = incidence(aux, offset).astype(jnp.bfloat16)
        counts = counts + dot_bf16(other[EV_DEV : 2 * EV_DEV], other, NT)
    counts = jnp.where(lax.axis_index("x") == 0, counts, 0.0)
    block_ref[...] = rates_ref[...]
    for event in range(EV_DEV):
        at = count_place(event)
        block_ref[:, at : at + NEAR] = counts[event : event + 1]
    for q in range(4):
        terms = per_event
        if q < 3:
            terms = terms * near_block(aux_left, aux_own, aux_right, 2 + q)
        block_ref[:, q * NEAR : (q + 1) * NEAR] = jnp.sum(terms, axis=0, keepdims=True)
    total = jnp.sum(jnp.sum(rhs * rhs, axis=1, keepdims=True), axis=0, keepdims=True)
    block_ref[:, SQUARE_AT : SQUARE_AT + 1] = total


def solve_kernel(gathered_ref, shift_ref, out_ref, shift_out_ref, rows_ref):
    shift_out_ref[...] = shift_ref[...]
    half = LANES // 2
    tables = []
    for row in range(PAYLOAD // LANES):
        for core in range(2):
            values = gathered_ref[pl.ds(core * half, half), row * LANES : (row + 1) * LANES]
            rows_ref[pl.ds(row * LANES + core, half, stride=2), :] = values
        tables.append(jnp.transpose(rows_ref[pl.ds(row * LANES, LANES), :]))

    def read(at):
        return tables[at // LANES][at % LANES : at % LANES + 8]

    def along(lower, own, upper):
        return own + pltpu.roll(upper, 1, 1) + pltpu.roll(lower, LANES - 1, 1)

    back = [along(*[read(q * NEAR + 8 * side) for side in range(3)]) for q in range(4)]
    counts = [[read(count_place(a) + 8 * side) for side in range(3)] for a in range(EV_DEV)]
    deriv = [
        [read(rate_place(group, station, q)) for q in range(3)]
        for group in range(4)
        for station in range(STATIONS_DEV)
    ]

    def total(values):
        return jnp.sum(jnp.sum(values, axis=1, keepdims=True), axis=0, keepdims=True)

    def inner(left, right):
        terms = left[0] * right[0]
        for q in range(1, 4):
            terms = terms + left[q] * right[q]
        return total(terms)

    def normal(model):
        result = [jnp.zeros((EV_DEV, LANES), jnp.float32) for _ in range(4)]
        for rates in deriv:
            data = model[3]
            for q in range(3):
                data = data + rates[q] * model[q]
            sides = [None, None, None]
            for a in range(EV_DEV):
                row = jnp.broadcast_to(data[a : a + 1], (EV_DEV, LANES))
                for side in range(3):
                    term = counts[a][side] * row
                    sides[side] = term if a == 0 else sides[side] + term
            mixed = along(*sides)
            for q in range(3):
                result[q] = result[q] + rates[q] * mixed
            result[3] = result[3] + mixed
        return result

    rhs_square = total(tables[0][SQUARE_AT : SQUARE_AT + 1])
    beta = jnp.sqrt(rhs_square + eps_small)
    unit_square = rhs_square / (beta * beta)
    adjoint = [value / beta for value in back]
    alpha = jnp.sqrt(inner(adjoint, adjoint) + eps_small)
    model = [value / alpha for value in adjoint]
    search = model
    location = [jnp.zeros((EV_DEV, LANES), jnp.float32) for _ in range(4)]
    phi_bar = beta
    rho_bar = alpha
    for turn in range(2):
        normal_model = normal(model)
        square = inner(model, normal_model) - 2.0 * alpha * inner(model, adjoint)
        square = jnp.maximum(square + alpha * alpha * unit_square, 0.0)
        beta = jnp.sqrt(square + eps_small)
        rho = jnp.sqrt(rho_bar * rho_bar + beta * beta)
        cosine = rho_bar / rho
        sine = beta / rho
        phi = cosine * phi_bar
        phi_bar = sine * phi_bar
        step = phi / rho
        location = [location[q] + step * search[q] for q in range(4)]
        if turn == 0:
            unit_square = square / (beta * beta)
            adjoint = [(normal_model[q] - alpha * adjoint[q]) / beta for q in range(4)]
            vector = [adjoint[q] - beta * model[q] for q in range(4)]
            alpha = jnp.sqrt(inner(vector, vector) + eps_small)
            model = [value / alpha for value in vector]
            theta = sine * alpha
            rho_bar = -cosine * alpha
            search = [model[q] - theta / rho * search[q] for q in range(4)]

    lanes = lax.broadcasted_iota(jnp.int32, (ROWS, LANES), 1)
    mine = (lanes == device_index()).astype(jnp.float32)
    own = dot_exact(mine, jnp.concatenate(location, axis=0), NT)
    for q in range(4):
        out_ref[q : q + 1, :] = own[0:1, q * EV_DEV : (q + 1) * EV_DEV]


def from_other_chip(block):
    count = lax.axis_size("g") * lax.axis_size("c")
    partners = [(i, i - 1 + 2 * (i % 2)) for i in range(count)]
    route = [(i, other) for i, other in partners if 0 <= other < count]
    return lax.ppermute(block, ("g", "c"), route)


def spread(row, axis):
    copies = jnp.broadcast_to(row, (lax.axis_size(axis), row.shape[1]))
    return lax.all_to_all(copies, axis, 0, 0, tiled=True)


VMEM = pl.BlockSpec(memory_space=pltpu.VMEM)
SMEM = pl.BlockSpec(memory_space=pltpu.SMEM)
HBM = pl.BlockSpec(memory_space=pltpu.HBM)
PARAMS = pltpu.CompilerParams(vmem_limit_bytes=VMEM_BYTES)


def pack(traces, ray_slowness, travel_time, pair_first, pair_second, pair_lag, pair_live):
    arguments = (
        traces.reshape(TRACES_DEV, EV_DEV, LENGTH),
        ray_slowness,
        travel_time,
        pair_first.reshape(1, PAIR_DEV),
        pair_second.reshape(1, PAIR_DEV),
        pair_lag,
    )
    return pl.pallas_call(
        pack_kernel,
        out_shape=pltpu.VMEM((TRACES_DEV + 1, ROWS, LENGTH), jnp.float32),
        in_specs=[SMEM] + [HBM] * 6,
        out_specs=VMEM,
        scratch_shapes=[
            pltpu.VMEM((3, STATIONS_DEV, EV_DEV), jnp.float32),
            pltpu.VMEM((STATIONS_DEV, EV_DEV), jnp.float32),
            pltpu.VMEM((1, PAIR_DEV), jnp.int32),
            pltpu.VMEM((1, PAIR_DEV), jnp.int32),
            pltpu.VMEM((STATIONS_DEV, PAIR_DEV), jnp.int32),
            pltpu.SemaphoreType.DMA((6,)),
        ],
        compiler_params=PARAMS,
        name="pack",
    )(pair_live, *[pltpu.with_memory_space_constraint(value, pltpu.HBM) for value in arguments])


def firsts(message):
    toeplitz = jax.ShapeDtypeStruct((TRACES_DEV, EV_DEV * LAGS, SPAN), jnp.bfloat16)
    return pl.pallas_call(
        first_kernel,
        out_shape=(
            toeplitz,
            toeplitz,
            jax.ShapeDtypeStruct((ROWS, PAIR_DEV), jnp.int32),
            jax.ShapeDtypeStruct((PAIR_DEV, EV_DEV * LAGS), jnp.float32),
            jax.ShapeDtypeStruct((1, PAYLOAD), jnp.float32),
        ),
        in_specs=[VMEM],
        out_specs=(VMEM,) * 5,
        compiler_params=PARAMS,
        name="firsts",
    )(message)


MOVED = jax.ShapeDtypeStruct((TRACES_DEV * PAIR_DEV * ROWS, LANES), jnp.float32)


def early(places, chip):
    return pl.pallas_call(
        early_kernel,
        out_shape=MOVED,
        in_specs=[SMEM, VMEM],
        out_specs=VMEM,
        scratch_shapes=[pltpu.VMEM((3 * PART_ROWS + 2 * ROWS, LANES), jnp.float32)],
        compiler_params=PARAMS,
        name="early",
    )(places, chip)


def late(places, moved, chip, from_cross, high, low, pick, rates):
    refined_shift, block, _ = pl.pallas_call(
        late_kernel,
        out_shape=(
            jax.ShapeDtypeStruct((STATIONS_DEV, PAIR_DEV), jnp.float32),
            jax.ShapeDtypeStruct((1, PAYLOAD), jnp.float32),
            MOVED,
        ),
        in_specs=[VMEM] * 8,
        out_specs=(VMEM, VMEM, VMEM),
        scratch_shapes=[
            pltpu.VMEM((PART_ROWS + 2 * ROWS, LANES), jnp.float32),
            pltpu.SMEM((ROWS, PAIR_DEV), jnp.int32),
            pltpu.SemaphoreType.DMA,
        ],
        input_output_aliases={1: 2},
        compiler_params=PARAMS,
        name="late",
    )(places, moved, chip, from_cross, high, low, pick, rates)
    return refined_shift, block


def solve(gathered, shift):
    return pl.pallas_call(
        solve_kernel,
        out_shape=(
            jax.ShapeDtypeStruct((4, EV_DEV), jnp.float32),
            jax.ShapeDtypeStruct((STATIONS_DEV, PAIR_DEV), jnp.float32),
        ),
        in_specs=[VMEM, VMEM],
        out_specs=(VMEM, VMEM),
        scratch_shapes=[pltpu.VMEM((PAYLOAD, LANES), jnp.float32)],
        compiler_params=PARAMS,
        name="solve",
    )(gathered, shift)


def body(traces, ray_slowness, travel_time, pair_first, pair_second, pair_lag, pair_live):
    message = pack(
        traces, ray_slowness, travel_time, pair_first, pair_second, pair_lag, pair_live
    )
    from_cross = from_other_chip(message)
    high, low, places, pick, rates = firsts(message)
    chip = lax.all_gather(message, "c", axis=0)
    moved = early(places, chip)
    shift, block = late(places, moved, chip, from_cross, high, low, pick, rates)
    block = jnp.sum(spread(block, "x"), axis=0, keepdims=True)
    chips = lax.axis_size("g")
    gathered = lax.all_gather(spread(block, "g"), "c", axis=0)
    location, refined_shift = solve(gathered.reshape(2 * chips, PAYLOAD), shift)
    return refined_shift, location


def solution(mesh):
    ev, st = mesh.devices.shape
    fine = Mesh(mesh.devices.reshape(ev // 2, 2, st), ("g", "c", "x"))
    event_axes = ("g", "c")
    in_specs = (
        P("x", None, event_axes, None),
        P(None, "x", event_axes),
        P("x", event_axes),
        P(event_axes),
        P(event_axes),
        P("x", event_axes),
        P(event_axes),
    )
    out_specs = (P("x", event_axes), P(None, event_axes))
    return jax.shard_map(body, mesh=fine, in_specs=in_specs, out_specs=out_specs, check_vma=False)
```

```python
import jax
import jax.numpy as jnp
from jax import lax
from jax.experimental import pallas as pl
from jax.experimental.pallas import tpu as pltpu
from jax.sharding import Mesh
from jax.sharding import PartitionSpec as P

LAGS = 32
LANES = 128
ROWS = 8
EV_DEV = 8
NEAR = 3 * EV_DEV
STATIONS_DEV = 3
TRACES_DEV = 9
LENGTH = 1024
CHUNKS = LENGTH // LANES
QUARTER = LENGTH // 4
WINDOW = LENGTH // 2
SPAN = WINDOW + LANES
SPAN_CHUNKS = SPAN // LANES
PAIR_DEV = 128
PART_ROWS = TRACES_DEV * EV_DEV * CHUNKS
VMEM_BYTES = 24 * 1024 * 1024
DEAD = -1000.0
PLACE_ROWS = 16
GROUP = 16
PAYLOAD = 5 * LANES
SQUARE_AT = 4 * NEAR

eps_small = 1e-06
sample_step = 0.01
exact_mode = lax.Precision.HIGHEST
NT = (((1,), (1,)), ((), ()))
NN = (((1,), (0,)), ((), ()))


def device_index():
    return lax.axis_index("g") * 2 + lax.axis_index("c")


def dot_exact(left, right, dims):
    return lax.dot_general(
        left, right, dims, precision=exact_mode, preferred_element_type=jnp.float32
    )


def dot_bf16(left, right, dims):
    return lax.dot_general(left, right, dims, preferred_element_type=jnp.float32)


def count_place(event):
    return LANES + NEAR * event if event < 5 else 2 * LANES + NEAR * (event - 5)


def rate_place(group, station, q):
    index = (group * STATIONS_DEV + station) * 3 + q
    return 3 * LANES + 8 * index if index < 32 else 2 * LANES + 96 + 8 * (index - 32)


def dot_signs(left, signs, dims):
    high = left.astype(jnp.bfloat16)
    rest = left - high.astype(jnp.float32)
    middle = rest.astype(jnp.bfloat16)
    low = (rest - middle.astype(jnp.float32)).astype(jnp.bfloat16)
    rows = left.shape[0]
    parts = dot_bf16(jnp.concatenate([high, middle, low], axis=0), signs, dims)
    return parts[0:rows] + parts[rows : 2 * rows] + parts[2 * rows :]


def split_bf16(values):
    high = values.astype(jnp.bfloat16)
    low = (values - high.astype(jnp.float32)).astype(jnp.bfloat16)
    return high, low


def pack_kernel(
    live_ref,
    traces_ref,
    slowness_ref,
    time_ref,
    first_ref,
    second_ref,
    lag_ref,
    out_ref,
    slowness,
    time,
    first,
    second,
    lag,
    sems,
):
    pairs = [
        (traces_ref, out_ref.at[pl.ds(0, TRACES_DEV)]),
        (slowness_ref, slowness),
        (time_ref, time),
        (first_ref, first),
        (second_ref, second),
        (lag_ref, lag),
    ]
    copies = [
        pltpu.make_async_copy(source, target, sems.at[at])
        for at, (source, target) in enumerate(pairs)
    ]
    for copy in copies:
        copy.start()
    aux = out_ref.at[TRACES_DEV]
    aux[...] = jnp.zeros((ROWS, LENGTH), jnp.float32)
    for copy in copies[1:]:
        copy.wait()
    base = device_index() * EV_DEV - EV_DEV
    slots = lax.broadcasted_iota(jnp.int32, (1, PAIR_DEV), 1)
    alive = slots < live_ref[0]
    for row, ids in enumerate((first, second)):
        near = (ids[...] - base).astype(jnp.float32)
        aux[row : row + 1, 0:LANES] = jnp.where(alive, near, DEAD)
        aux[row : row + 1, 6 * LANES : 7 * LANES] = near
    aux[0:STATIONS_DEV, LANES : LANES + EV_DEV] = time[...]
    for q in range(3):
        lane = (2 + q) * LANES
        aux[0:STATIONS_DEV, lane : lane + EV_DEV] = slowness[q]
    aux[0:STATIONS_DEV, 5 * LANES : 6 * LANES] = lag[...].astype(jnp.float32)
    copies[0].wait()


def first_windows(own_ref, high_ref, low_ref, items):
    for item in items:
        window = own_ref[item, :, QUARTER : QUARTER + WINDOW]
        power = jnp.sum(window * window, axis=1, keepdims=True)
        window = window * lax.rsqrt(power + eps_small)
        padded = jnp.concatenate([window, jnp.zeros((EV_DEV, LANES), jnp.float32)], axis=1)
        for event in range(EV_DEV):
            wide = jnp.broadcast_to(padded[event : event + 1], (LAGS, SPAN))
            wide = pltpu.roll(wide, 0, 1, stride=1, stride_axis=0)
            high, low = split_bf16(wide)
            high_ref[item, pl.ds(event * LAGS, LAGS), :] = high
            low_ref[item, pl.ds(event * LAGS, LAGS), :] = low


def first_kernel(
    own_ref, high_ref, low_ref, places_ref, pick_ref, rates_ref, places, sem
):
    aux = own_ref[TRACES_DEV]
    first = aux[0:1, 6 * LANES : 7 * LANES].astype(jnp.int32)
    second = aux[1:2, 6 * LANES : 7 * LANES].astype(jnp.int32)
    begin = aux[0:STATIONS_DEV, 5 * LANES : 6 * LANES].astype(jnp.int32) + (QUARTER - LAGS // 2)
    side = lax.shift_right_arithmetic(second, 3)
    mate_side = 2 - 2 * lax.axis_index("c")
    away = jnp.logical_and(side != 1, side != mate_side)
    part = jnp.where(side == 1, 0, jnp.where(away, 2, 1))
    alive = aux[0:1, 0:LANES] >= 0.0
    far = jnp.logical_and(away, alive)
    event = jnp.bitwise_and(second, EV_DEV - 1)
    rows = part * PART_ROWS + event * CHUNKS + lax.shift_right_arithmetic(begin, 7)
    near = jnp.logical_and(jnp.logical_not(away), alive)
    upper = lax.broadcasted_iota(jnp.int32, (PAIR_DEV, PAIR_DEV), 0)
    lower = lax.broadcasted_iota(jnp.int32, (PAIR_DEV, PAIR_DEV), 1)
    lane_ids = lower[0:1]
    ahead = (upper <= lower).astype(jnp.bfloat16)
    slots = lax.broadcasted_iota(jnp.int32, (ROWS, PAIR_DEV), 1).astype(jnp.bfloat16)
    hots, counts, listed = [], [], []
    for marked in (far, near):
        ones = marked.astype(jnp.float32)
        wide = jnp.broadcast_to(ones, (ROWS, PAIR_DEV)).astype(jnp.bfloat16)
        place = jnp.where(marked, dot_bf16(wide, ahead, NN)[0:1] - 1.0, -1.0)
        hots.append((upper.astype(jnp.float32) == place).astype(jnp.bfloat16))
        counts.append(jnp.sum(ones, axis=1, keepdims=True).astype(jnp.int32))
    first_windows(own_ref, high_ref, low_ref, range(2))
    for hot in hots:
        listed.append(dot_bf16(slots, hot, NT)[0:1])
    first_windows(own_ref, high_ref, low_ref, range(2, 4))
    places[...] = jnp.zeros((PLACE_ROWS, PAIR_DEV), jnp.int32)
    places[0:3, :] = rows
    places[3:6, :] = jnp.bitwise_and(begin, LANES - 1)
    for at in range(2):
        filled = jnp.where(lane_ids < counts[at], listed[at], listed[at][:, 0:1])
        places[6 + at : 7 + at, :] = filled.astype(jnp.int32)
        places[8 + at : 9 + at, :] = jnp.broadcast_to(counts[at], (1, PAIR_DEV))
    move = pltpu.make_async_copy(places, places_ref, sem)
    move.start()
    first_windows(own_ref, high_ref, low_ref, range(4, TRACES_DEV))
    ends = jnp.bitwise_and(first, EV_DEV - 1).astype(jnp.float32)
    column = jnp.transpose(jnp.broadcast_to(ends, (LANES, PAIR_DEV)))
    groups = lax.broadcasted_iota(jnp.int32, (PAIR_DEV, LANES), 1) // LAGS
    for half in range(2):
        mine = column == (groups + half * (LANES // LAGS)).astype(jnp.float32)
        pick_ref[:, half * LANES : (half + 1) * LANES] = mine.astype(jnp.float32)
    rates_ref[...] = jnp.zeros((1, PAYLOAD), jnp.float32)
    for station in range(STATIONS_DEV):
        for q in range(3):
            lane = (2 + q) * LANES
            own = aux[station : station + 1, lane : lane + EV_DEV]
            for group in range(4):
                at = rate_place(group, station, q)
                rates_ref[:, at : at + EV_DEV] = jnp.where(
                    lax.axis_index("x") == group, own, 0.0
                )
    move.wait()


def fill_table(ref, table_ref, part):
    for item in range(TRACES_DEV):
        values = ref[item]
        power = jnp.sum(values * values, axis=1, keepdims=True)
        values = values * lax.rsqrt(power + eps_small)
        for chunk in range(CHUNKS):
            start = part * PART_ROWS + item * EV_DEV * CHUNKS + chunk
            table_ref[pl.ds(start, EV_DEV, stride=CHUNKS), :] = values[
                :, chunk * LANES : (chunk + 1) * LANES
            ]


def align(places_ref, table_ref, moved_ref, slot, offset):
    lane_ids = lax.broadcasted_iota(jnp.int32, (ROWS, LANES), 1)
    for station in range(STATIONS_DEV):
        row = places_ref[station, slot] - offset
        lane = places_ref[3 + station, slot]
        turn = jnp.bitwise_and(-lane, LANES - 1)
        keep = lane_ids >= lane
        for component in range(3):
            item = station * 3 + component
            at = item * EV_DEV * CHUNKS
            here = table_ref[pl.ds(row + at, ROWS), :]
            after = table_ref[pl.ds(row + (at + 1), ROWS), :]
            moved = pltpu.roll(jnp.where(keep, here, after), turn, 1)
            to = pl.multiple_of((item * PAIR_DEV + slot) * ROWS, ROWS)
            moved_ref[pl.ds(to, ROWS), :] = moved


def groups_of(count):
    return lax.div(count + (GROUP - 1), GROUP)


def early_kernel(places_ref, chip_ref, moved_ref, table_ref):
    table_ref[pl.ds(2 * PART_ROWS, 2 * ROWS), :] = jnp.zeros((2 * ROWS, LANES), jnp.float32)
    core = lax.axis_index("c")
    fill_table(chip_ref.at[core], table_ref, 0)
    fill_table(chip_ref.at[1 - core], table_ref, 1)

    def step(index, carry):
        for turn in range(GROUP):
            align(places_ref, table_ref, moved_ref, places_ref[7, index * GROUP + turn], 0)
        return carry

    lax.fori_loop(0, groups_of(places_ref[9, 0]), step, 0)


def incidence(aux, offset):
    events = lax.broadcasted_iota(jnp.int32, (NEAR, PAIR_DEV), 0).astype(jnp.float32)
    starts = aux[0:1, 0:LANES] + offset
    ends = aux[1:2, 0:LANES] + offset
    return (events == starts).astype(jnp.float32) - (events == ends).astype(jnp.float32)


def near_block(left, own, right, part):
    lane = part * LANES
    return jnp.concatenate(
        [aux[0:STATIONS_DEV, lane : lane + EV_DEV] for aux in (left, own, right)], axis=1
    )


def late_kernel(
    places_ref,
    moved_in_ref,
    chip_ref,
    cross_ref,
    high_ref,
    low_ref,
    pick_ref,
    rates_ref,
    shift_ref,
    block_ref,
    moved_ref,
    table_ref,
):
    del moved_in_ref
    table_ref[pl.ds(PART_ROWS, 2 * ROWS), :] = jnp.zeros((2 * ROWS, LANES), jnp.float32)
    fill_table(cross_ref, table_ref, 0)

    def step(index, carry):
        for turn in range(GROUP):
            slot = places_ref[6, index * GROUP + turn]
            align(places_ref, table_ref, moved_ref, slot, 2 * PART_ROWS)
        return carry

    lax.fori_loop(0, groups_of(places_ref[8, 0]), step, 0)

    core = lax.axis_index("c")
    aux_own = chip_ref[core, TRACES_DEV]
    aux_left = jnp.where(core == 0, cross_ref[TRACES_DEV], chip_ref[0, TRACES_DEV])
    aux_right = jnp.where(core == 0, chip_ref[1, TRACES_DEV], cross_ref[TRACES_DEV])

    lane_ids = lax.broadcasted_iota(jnp.int32, (1, LANES), 1)
    centred = (lane_ids - LAGS // 2).astype(jnp.float32)
    weights = jnp.where(lane_ids < LAGS, centred, jnp.where(lane_ids < 2 * LAGS, 1.0, 0.0))
    folded = []
    for station in range(STATIONS_DEV):
        energy = jnp.zeros((PAIR_DEV, EV_DEV * LAGS), jnp.float32)
        for component in range(3):
            item = station * 3 + component
            pieces = [
                moved_ref[pl.ds(item * PAIR_DEV * ROWS + chunk, PAIR_DEV, stride=ROWS), :]
                for chunk in range(SPAN_CHUNKS)
            ]
            high, low = split_bf16(jnp.concatenate(pieces, axis=1))
            both = dot_bf16(jnp.concatenate([high, low], axis=0), high_ref[item], NT)
            xcorr = both[0:PAIR_DEV] + both[PAIR_DEV:] + dot_bf16(high, low_ref[item], NT)
            energy = energy + xcorr * xcorr
        energy = energy * pick_ref[...]
        energy = energy[:, 0:LANES] + energy[:, LANES:]
        energy = energy + pltpu.roll(energy, LANES // 2, 1)
        energy = energy + pltpu.roll(energy, LANES // 4, 1)
        folded.append(energy)
    pair = folded[0] * weights + folded[1] * pltpu.roll(weights, LANES // 2, 1)
    tables = [jnp.transpose(pair), jnp.transpose(folded[2] * weights)]
    station_shift = []
    for station in range(STATIONS_DEV):
        rows = tables[station // 2][(station % 2) * 2 * LAGS : (station % 2 + 1) * 2 * LAGS]
        above = jnp.sum(rows[0:LAGS], axis=0, keepdims=True)
        below = jnp.sum(rows[LAGS:], axis=0, keepdims=True)
        station_shift.append(above / (below + eps_small))
    alive = aux_own[0:1, 0:LANES] >= 0.0
    shift = jnp.where(alive, jnp.concatenate(station_shift, axis=0), 0.0)
    shift_ref[...] = shift

    signs = incidence(aux_own, 0.0).astype(jnp.bfloat16)
    times = dot_signs(near_block(aux_left, aux_own, aux_right, 1), signs, NN)
    lags = aux_own[0:STATIONS_DEV, 5 * LANES : 6 * LANES]
    rhs = jnp.where(alive, sample_step * (lags + shift), 0.0) - times
    per_event = dot_signs(rhs, signs, NT)
    counts = dot_bf16(signs[EV_DEV : 2 * EV_DEV], signs, NT)
    for aux, offset in ((aux_left, -float(EV_DEV)), (aux_right, float(EV_DEV))):
        other = incidence(aux, offset).astype(jnp.bfloat16)
        counts = counts + dot_bf16(other[EV_DEV : 2 * EV_DEV], other, NT)
    counts = jnp.where(lax.axis_index("x") == 0, counts, 0.0)
    block_ref[...] = rates_ref[...]
    for event in range(EV_DEV):
        at = count_place(event)
        block_ref[:, at : at + NEAR] = counts[event : event + 1]
    for q in range(4):
        terms = per_event
        if q < 3:
            terms = terms * near_block(aux_left, aux_own, aux_right, 2 + q)
        block_ref[:, q * NEAR : (q + 1) * NEAR] = jnp.sum(terms, axis=0, keepdims=True)
    total = jnp.sum(jnp.sum(rhs * rhs, axis=1, keepdims=True), axis=0, keepdims=True)
    block_ref[:, SQUARE_AT : SQUARE_AT + 1] = total


def solve_kernel(gathered_ref, shift_ref, out_ref, shift_out_ref, rows_ref):
    shift_out_ref[...] = shift_ref[...]
    half = LANES // 2
    tables = []
    for row in range(PAYLOAD // LANES):
        for core in range(2):
            values = gathered_ref[pl.ds(core * half, half), row * LANES : (row + 1) * LANES]
            rows_ref[pl.ds(row * LANES + core, half, stride=2), :] = values
        tables.append(jnp.transpose(rows_ref[pl.ds(row * LANES, LANES), :]))

    def read(at):
        return tables[at // LANES][at % LANES : at % LANES + 8]

    def along(lower, own, upper):
        return own + pltpu.roll(upper, 1, 1) + pltpu.roll(lower, LANES - 1, 1)

    back = [along(*[read(q * NEAR + 8 * side) for side in range(3)]) for q in range(4)]
    counts = [[read(count_place(a) + 8 * side) for side in range(3)] for a in range(EV_DEV)]
    deriv = [
        [read(rate_place(group, station, q)) for q in range(3)]
        for group in range(4)
        for station in range(STATIONS_DEV)
    ]

    def total(values):
        return jnp.sum(jnp.sum(values, axis=1, keepdims=True), axis=0, keepdims=True)

    def inner(left, right):
        terms = left[0] * right[0]
        for q in range(1, 4):
            terms = terms + left[q] * right[q]
        return total(terms)

    def normal(model):
        result = [jnp.zeros((EV_DEV, LANES), jnp.float32) for _ in range(4)]
        for rates in deriv:
            data = model[3]
            for q in range(3):
                data = data + rates[q] * model[q]
            sides = [None, None, None]
            for a in range(EV_DEV):
                row = jnp.broadcast_to(data[a : a + 1], (EV_DEV, LANES))
                for side in range(3):
                    term = counts[a][side] * row
                    sides[side] = term if a == 0 else sides[side] + term
            mixed = along(*sides)
            for q in range(3):
                result[q] = result[q] + rates[q] * mixed
            result[3] = result[3] + mixed
        return result

    rhs_square = total(tables[0][SQUARE_AT : SQUARE_AT + 1])
    beta = jnp.sqrt(rhs_square + eps_small)
    unit_square = rhs_square / (beta * beta)
    adjoint = [value / beta for value in back]
    alpha = jnp.sqrt(inner(adjoint, adjoint) + eps_small)
    model = [value / alpha for value in adjoint]
    search = model
    location = [jnp.zeros((EV_DEV, LANES), jnp.float32) for _ in range(4)]
    phi_bar = beta
    rho_bar = alpha
    for turn in range(2):
        normal_model = normal(model)
        square = inner(model, normal_model) - 2.0 * alpha * inner(model, adjoint)
        square = jnp.maximum(square + alpha * alpha * unit_square, 0.0)
        beta = jnp.sqrt(square + eps_small)
        rho = jnp.sqrt(rho_bar * rho_bar + beta * beta)
        cosine = rho_bar / rho
        sine = beta / rho
        phi = cosine * phi_bar
        phi_bar = sine * phi_bar
        step = phi / rho
        location = [location[q] + step * search[q] for q in range(4)]
        if turn == 0:
            unit_square = square / (beta * beta)
            adjoint = [(normal_model[q] - alpha * adjoint[q]) / beta for q in range(4)]
            vector = [adjoint[q] - beta * model[q] for q in range(4)]
            alpha = jnp.sqrt(inner(vector, vector) + eps_small)
            model = [value / alpha for value in vector]
            theta = sine * alpha
            rho_bar = -cosine * alpha
            search = [model[q] - theta / rho * search[q] for q in range(4)]

    lanes = lax.broadcasted_iota(jnp.int32, (ROWS, LANES), 1)
    mine = (lanes == device_index()).astype(jnp.float32)
    own = dot_exact(mine, jnp.concatenate(location, axis=0), NT)
    for q in range(4):
        out_ref[q : q + 1, :] = own[0:1, q * EV_DEV : (q + 1) * EV_DEV]


def from_other_chip(block):
    count = lax.axis_size("g") * lax.axis_size("c")
    partners = [(i, i - 1 + 2 * (i % 2)) for i in range(count)]
    route = [(i, other) for i, other in partners if 0 <= other < count]
    return lax.ppermute(block, ("g", "c"), route)


def spread(row, axis):
    copies = jnp.broadcast_to(row, (lax.axis_size(axis), row.shape[1]))
    return lax.all_to_all(copies, axis, 0, 0, tiled=True)


VMEM = pl.BlockSpec(memory_space=pltpu.VMEM)
SMEM = pl.BlockSpec(memory_space=pltpu.SMEM)
HBM = pl.BlockSpec(memory_space=pltpu.HBM)
PARAMS = pltpu.CompilerParams(vmem_limit_bytes=VMEM_BYTES)


def pack(traces, ray_slowness, travel_time, pair_first, pair_second, pair_lag, pair_live):
    arguments = (
        traces.reshape(TRACES_DEV, EV_DEV, LENGTH),
        ray_slowness,
        travel_time,
        pair_first.reshape(1, PAIR_DEV),
        pair_second.reshape(1, PAIR_DEV),
        pair_lag,
    )
    return pl.pallas_call(
        pack_kernel,
        out_shape=pltpu.VMEM((TRACES_DEV + 1, ROWS, LENGTH), jnp.float32),
        in_specs=[SMEM] + [HBM] * 6,
        out_specs=VMEM,
        scratch_shapes=[
            pltpu.VMEM((3, STATIONS_DEV, EV_DEV), jnp.float32),
            pltpu.VMEM((STATIONS_DEV, EV_DEV), jnp.float32),
            pltpu.VMEM((1, PAIR_DEV), jnp.int32),
            pltpu.VMEM((1, PAIR_DEV), jnp.int32),
            pltpu.VMEM((STATIONS_DEV, PAIR_DEV), jnp.int32),
            pltpu.SemaphoreType.DMA((6,)),
        ],
        compiler_params=PARAMS,
        name="pack",
    )(pair_live, *[pltpu.with_memory_space_constraint(value, pltpu.HBM) for value in arguments])


def firsts(message):
    toeplitz = jax.ShapeDtypeStruct((TRACES_DEV, EV_DEV * LAGS, SPAN), jnp.bfloat16)
    return pl.pallas_call(
        first_kernel,
        out_shape=(
            toeplitz,
            toeplitz,
            pltpu.SMEM((PLACE_ROWS, PAIR_DEV), jnp.int32),
            jax.ShapeDtypeStruct((PAIR_DEV, EV_DEV * LAGS), jnp.float32),
            jax.ShapeDtypeStruct((1, PAYLOAD), jnp.float32),
        ),
        in_specs=[VMEM],
        out_specs=(VMEM, VMEM, SMEM, VMEM, VMEM),
        scratch_shapes=[
            pltpu.VMEM((PLACE_ROWS, PAIR_DEV), jnp.int32),
            pltpu.SemaphoreType.DMA,
        ],
        compiler_params=PARAMS,
        name="firsts",
    )(message)


MOVED = jax.ShapeDtypeStruct((TRACES_DEV * PAIR_DEV * ROWS, LANES), jnp.float32)


def early(places, chip):
    return pl.pallas_call(
        early_kernel,
        out_shape=MOVED,
        in_specs=[SMEM, VMEM],
        out_specs=VMEM,
        scratch_shapes=[pltpu.VMEM((2 * PART_ROWS + 2 * ROWS, LANES), jnp.float32)],
        compiler_params=PARAMS,
        name="early",
    )(places, chip)


def late(places, moved, chip, from_cross, high, low, pick, rates):
    refined_shift, block, _ = pl.pallas_call(
        late_kernel,
        out_shape=(
            jax.ShapeDtypeStruct((STATIONS_DEV, PAIR_DEV), jnp.float32),
            jax.ShapeDtypeStruct((1, PAYLOAD), jnp.float32),
            MOVED,
        ),
        in_specs=[SMEM] + [VMEM] * 7,
        out_specs=(VMEM, VMEM, VMEM),
        scratch_shapes=[pltpu.VMEM((PART_ROWS + 2 * ROWS, LANES), jnp.float32)],
        input_output_aliases={1: 2},
        compiler_params=PARAMS,
        name="late",
    )(places, moved, chip, from_cross, high, low, pick, rates)
    return refined_shift, block


def solve(gathered, shift):
    return pl.pallas_call(
        solve_kernel,
        out_shape=(
            jax.ShapeDtypeStruct((4, EV_DEV), jnp.float32),
            jax.ShapeDtypeStruct((STATIONS_DEV, PAIR_DEV), jnp.float32),
        ),
        in_specs=[VMEM, VMEM],
        out_specs=(VMEM, VMEM),
        scratch_shapes=[pltpu.VMEM((PAYLOAD, LANES), jnp.float32)],
        compiler_params=PARAMS,
        name="solve",
    )(gathered, shift)


def body(traces, ray_slowness, travel_time, pair_first, pair_second, pair_lag, pair_live):
    message = pack(
        traces, ray_slowness, travel_time, pair_first, pair_second, pair_lag, pair_live
    )
    from_cross = from_other_chip(message)
    high, low, places, pick, rates = firsts(message)
    places = pltpu.with_memory_space_constraint(places, pltpu.SMEM)
    chip = lax.all_gather(message, "c", axis=0)
    moved = early(places, chip)
    shift, block = late(places, moved, chip, from_cross, high, low, pick, rates)
    block = jnp.sum(spread(block, "x"), axis=0, keepdims=True)
    chips = lax.axis_size("g")
    gathered = lax.all_gather(spread(block, "g"), "c", axis=0)
    location, refined_shift = solve(gathered.reshape(2 * chips, PAYLOAD), shift)
    return refined_shift, location


def solution(mesh):
    ev, st = mesh.devices.shape
    fine = Mesh(mesh.devices.reshape(ev // 2, 2, st), ("g", "c", "x"))
    event_axes = ("g", "c")
    in_specs = (
        P("x", None, event_axes, None),
        P(None, "x", event_axes),
        P("x", event_axes),
        P(event_axes),
        P(event_axes),
        P("x", event_axes),
        P(event_axes),
    )
    out_specs = (P("x", event_axes), P(None, event_axes))
    return jax.shard_map(body, mesh=fine, in_specs=in_specs, out_specs=out_specs, check_vma=False)
```

```python
import jax
import jax.numpy as jnp
from jax import lax
from jax.experimental import pallas as pl
from jax.experimental.pallas import tpu as pltpu
from jax.sharding import Mesh
from jax.sharding import PartitionSpec as P

LAGS = 32
LANES = 128
ROWS = 8
EV_DEV = 8
NEAR = 3 * EV_DEV
STATIONS_DEV = 3
TRACES_DEV = 9
LENGTH = 1024
CHUNKS = LENGTH // LANES
QUARTER = LENGTH // 4
WINDOW = LENGTH // 2
SPAN = WINDOW + LANES
SPAN_CHUNKS = SPAN // LANES
PAIR_DEV = 128
PART_ROWS = TRACES_DEV * EV_DEV * CHUNKS
VMEM_BYTES = 24 * 1024 * 1024
PLACE_ROWS = 16
GROUP = 16
PAYLOAD = 5 * LANES
SQUARE_AT = 4 * NEAR

eps_small = 1e-06
sample_step = 0.01
NT = (((1,), (1,)), ((), ()))
NN = (((1,), (0,)), ((), ()))


def device_index():
    return lax.axis_index("g") * 2 + lax.axis_index("c")


def dot_bf16(left, right, dims):
    return lax.dot_general(left, right, dims, preferred_element_type=jnp.float32)


def count_place(event):
    return LANES + NEAR * event if event < 5 else 2 * LANES + NEAR * (event - 5)


def rate_place(group, station, q):
    index = (group * STATIONS_DEV + station) * 3 + q
    return 3 * LANES + 8 * index if index < 32 else 2 * LANES + 96 + 8 * (index - 32)


def thirds(values):
    high = values.astype(jnp.bfloat16)
    rest = values - high.astype(jnp.float32)
    middle = rest.astype(jnp.bfloat16)
    low = (rest - middle.astype(jnp.float32)).astype(jnp.bfloat16)
    return jnp.concatenate([high, middle, low], axis=0)


def dot_signs(left, signs, dims):
    rows = left.shape[0]
    parts = dot_bf16(thirds(left), signs, dims)
    return parts[0:rows] + parts[rows : 2 * rows] + parts[2 * rows :]


def split_bf16(values):
    high = values.astype(jnp.bfloat16)
    low = (values - high.astype(jnp.float32)).astype(jnp.bfloat16)
    return high, low


def pack_kernel(
    traces_ref,
    slowness_ref,
    time_ref,
    first_ref,
    second_ref,
    lag_ref,
    out_ref,
    slowness,
    time,
    first,
    second,
    lag,
    sems,
):
    pairs = [
        (traces_ref, out_ref.at[pl.ds(0, TRACES_DEV)]),
        (slowness_ref, slowness),
        (time_ref, time),
        (first_ref, first),
        (second_ref, second),
        (lag_ref, lag),
    ]
    copies = [
        pltpu.make_async_copy(source, target, sems.at[at])
        for at, (source, target) in enumerate(pairs)
    ]
    for copy in copies:
        copy.start()
    aux = out_ref.at[TRACES_DEV]
    aux[...] = jnp.zeros((ROWS, LENGTH), jnp.float32)
    for copy in copies[1:]:
        copy.wait()
    base = device_index() * EV_DEV - EV_DEV
    for row, ids in enumerate((first, second)):
        aux[row : row + 1, 0:LANES] = (ids[...] - base).astype(jnp.float32)
    aux[0:STATIONS_DEV, LANES : LANES + EV_DEV] = time[...]
    for q in range(3):
        lane = (2 + q) * LANES
        aux[0:STATIONS_DEV, lane : lane + EV_DEV] = slowness[q]
    aux[0:STATIONS_DEV, 5 * LANES : 6 * LANES] = lag[...].astype(jnp.float32)
    copies[0].wait()


def first_windows(own_ref, high_ref, low_ref, items):
    for item in items:
        window = own_ref[item, :, QUARTER : QUARTER + WINDOW]
        power = jnp.sum(window * window, axis=1, keepdims=True)
        window = window * lax.rsqrt(power + eps_small)
        padded = jnp.concatenate([window, jnp.zeros((EV_DEV, LANES), jnp.float32)], axis=1)
        for event in range(EV_DEV):
            wide = jnp.broadcast_to(padded[event : event + 1], (LAGS, SPAN))
            wide = pltpu.roll(wide, 0, 1, stride=1, stride_axis=0)
            high, low = split_bf16(wide)
            high_ref[item, pl.ds(event * LAGS, LAGS), :] = high
            low_ref[item, pl.ds(event * LAGS, LAGS), :] = low


def first_kernel(
    live_ref, own_ref, high_ref, low_ref, places_ref, pick_ref, rates_ref, places, sem
):
    aux = own_ref[TRACES_DEV]
    first = aux[0:1, 0:LANES].astype(jnp.int32)
    second = aux[1:2, 0:LANES].astype(jnp.int32)
    begin = aux[0:STATIONS_DEV, 5 * LANES : 6 * LANES].astype(jnp.int32) + (QUARTER - LAGS // 2)
    side = lax.shift_right_arithmetic(second, 3)
    mate_side = 2 - 2 * lax.axis_index("c")
    away = jnp.logical_and(side != 1, side != mate_side)
    part = jnp.where(side == 1, 0, jnp.where(away, 2, 1))
    alive = lax.broadcasted_iota(jnp.int32, (1, PAIR_DEV), 1) < live_ref[0]
    far = jnp.logical_and(away, alive)
    event = jnp.bitwise_and(second, EV_DEV - 1)
    rows = part * PART_ROWS + event * CHUNKS + lax.shift_right_arithmetic(begin, 7)
    near = jnp.logical_and(jnp.logical_not(away), alive)
    upper = lax.broadcasted_iota(jnp.int32, (PAIR_DEV, PAIR_DEV), 0)
    lower = lax.broadcasted_iota(jnp.int32, (PAIR_DEV, PAIR_DEV), 1)
    lane_ids = lower[0:1]
    ahead = (upper <= lower).astype(jnp.bfloat16)
    slots = lax.broadcasted_iota(jnp.int32, (ROWS, PAIR_DEV), 1).astype(jnp.bfloat16)
    hots, counts, listed = [], [], []
    for marked in (far, near):
        ones = marked.astype(jnp.float32)
        wide = jnp.broadcast_to(ones, (ROWS, PAIR_DEV)).astype(jnp.bfloat16)
        place = jnp.where(marked, dot_bf16(wide, ahead, NN)[0:1] - 1.0, -1.0)
        hots.append((upper.astype(jnp.float32) == place).astype(jnp.bfloat16))
        counts.append(jnp.sum(ones, axis=1, keepdims=True).astype(jnp.int32))
    first_windows(own_ref, high_ref, low_ref, range(2))
    for hot in hots:
        listed.append(dot_bf16(slots, hot, NT)[0:1])
    first_windows(own_ref, high_ref, low_ref, range(2, 4))
    places[...] = jnp.zeros((PLACE_ROWS, PAIR_DEV), jnp.int32)
    places[0:3, :] = rows
    places[3:6, :] = jnp.bitwise_and(begin, LANES - 1)
    for at in range(2):
        filled = jnp.where(lane_ids < counts[at], listed[at], listed[at][:, 0:1])
        places[6 + at : 7 + at, :] = filled.astype(jnp.int32)
        places[8 + at : 9 + at, :] = jnp.broadcast_to(counts[at], (1, PAIR_DEV))
    places[10:11, :] = jnp.broadcast_to(live_ref[0], (1, PAIR_DEV))
    move = pltpu.make_async_copy(places, places_ref, sem)
    move.start()
    first_windows(own_ref, high_ref, low_ref, range(4, TRACES_DEV))
    ends = jnp.bitwise_and(first, EV_DEV - 1).astype(jnp.float32)
    column = jnp.transpose(jnp.broadcast_to(ends, (LANES, PAIR_DEV)))
    groups = lax.broadcasted_iota(jnp.int32, (PAIR_DEV, LANES), 1) // LAGS
    for half in range(2):
        mine = column == (groups + half * (LANES // LAGS)).astype(jnp.float32)
        pick_ref[:, half * LANES : (half + 1) * LANES] = mine.astype(jnp.float32)
    rates_ref[...] = jnp.zeros((1, PAYLOAD), jnp.float32)
    for station in range(STATIONS_DEV):
        for q in range(3):
            lane = (2 + q) * LANES
            own = aux[station : station + 1, lane : lane + EV_DEV]
            for group in range(4):
                at = rate_place(group, station, q)
                rates_ref[:, at : at + EV_DEV] = jnp.where(
                    lax.axis_index("x") == group, own, 0.0
                )
    move.wait()


def fill_table(ref, table_ref, part):
    for item in range(TRACES_DEV):
        values = ref[item]
        power = jnp.sum(values * values, axis=1, keepdims=True)
        values = values * lax.rsqrt(power + eps_small)
        for chunk in range(CHUNKS):
            start = part * PART_ROWS + item * EV_DEV * CHUNKS + chunk
            table_ref[pl.ds(start, EV_DEV, stride=CHUNKS), :] = values[
                :, chunk * LANES : (chunk + 1) * LANES
            ]


def align(places_ref, table_ref, moved_ref, slot, offset):
    lane_ids = lax.broadcasted_iota(jnp.int32, (ROWS, LANES), 1)
    for station in range(STATIONS_DEV):
        row = places_ref[station, slot] - offset
        lane = places_ref[3 + station, slot]
        turn = jnp.bitwise_and(-lane, LANES - 1)
        keep = lane_ids >= lane
        for component in range(3):
            item = station * 3 + component
            at = item * EV_DEV * CHUNKS
            here = table_ref[pl.ds(row + at, ROWS), :]
            after = table_ref[pl.ds(row + (at + 1), ROWS), :]
            moved = pltpu.roll(jnp.where(keep, here, after), turn, 1)
            to = pl.multiple_of((item * PAIR_DEV + slot) * ROWS, ROWS)
            moved_ref[pl.ds(to, ROWS), :] = moved


def groups_of(count):
    return lax.div(count + (GROUP - 1), GROUP)


def early_kernel(places_ref, chip_ref, moved_ref, table_ref):
    table_ref[pl.ds(2 * PART_ROWS, 2 * ROWS), :] = jnp.zeros((2 * ROWS, LANES), jnp.float32)
    core = lax.axis_index("c")
    fill_table(chip_ref.at[core], table_ref, 0)
    fill_table(chip_ref.at[1 - core], table_ref, 1)

    def step(index, carry):
        for turn in range(GROUP):
            align(places_ref, table_ref, moved_ref, places_ref[7, index * GROUP + turn], 0)
        return carry

    lax.fori_loop(0, groups_of(places_ref[9, 0]), step, 0)


def incidence(aux):
    events = lax.broadcasted_iota(jnp.int32, (NEAR, PAIR_DEV), 0).astype(jnp.float32)
    starts = (events == aux[0:1, 0:LANES]).astype(jnp.float32)
    return starts - (events == aux[1:2, 0:LANES]).astype(jnp.float32)


def near_block(left, own, right, part):
    lane = part * LANES
    return jnp.concatenate(
        [aux[0:STATIONS_DEV, lane : lane + EV_DEV] for aux in (left, own, right)], axis=1
    )


def late_kernel(
    places_ref,
    moved_in_ref,
    chip_ref,
    cross_ref,
    high_ref,
    low_ref,
    pick_ref,
    rates_ref,
    shift_ref,
    block_ref,
    moved_ref,
    table_ref,
):
    del moved_in_ref
    table_ref[pl.ds(PART_ROWS, 2 * ROWS), :] = jnp.zeros((2 * ROWS, LANES), jnp.float32)
    fill_table(cross_ref, table_ref, 0)

    def step(index, carry):
        for turn in range(GROUP):
            slot = places_ref[6, index * GROUP + turn]
            align(places_ref, table_ref, moved_ref, slot, 2 * PART_ROWS)
        return carry

    lax.fori_loop(0, groups_of(places_ref[8, 0]), step, 0)

    core = lax.axis_index("c")
    aux_own = chip_ref[core, TRACES_DEV]
    aux_left = jnp.where(core == 0, cross_ref[TRACES_DEV], chip_ref[0, TRACES_DEV])
    aux_right = jnp.where(core == 0, chip_ref[1, TRACES_DEV], cross_ref[TRACES_DEV])

    lane_ids = lax.broadcasted_iota(jnp.int32, (1, LANES), 1)
    centred = (lane_ids - LAGS // 2).astype(jnp.float32)
    weights = jnp.where(lane_ids < LAGS, centred, jnp.where(lane_ids < 2 * LAGS, 1.0, 0.0))
    folded = []
    for station in range(STATIONS_DEV):
        energy = jnp.zeros((PAIR_DEV, EV_DEV * LAGS), jnp.float32)
        for component in range(3):
            item = station * 3 + component
            pieces = [
                moved_ref[pl.ds(item * PAIR_DEV * ROWS + chunk, PAIR_DEV, stride=ROWS), :]
                for chunk in range(SPAN_CHUNKS)
            ]
            high, low = split_bf16(jnp.concatenate(pieces, axis=1))
            both = dot_bf16(jnp.concatenate([high, low], axis=0), high_ref[item], NT)
            xcorr = both[0:PAIR_DEV] + both[PAIR_DEV:] + dot_bf16(high, low_ref[item], NT)
            energy = energy + xcorr * xcorr
        energy = energy * pick_ref[...]
        energy = energy[:, 0:LANES] + energy[:, LANES:]
        energy = energy + pltpu.roll(energy, LANES // 2, 1)
        energy = energy + pltpu.roll(energy, LANES // 4, 1)
        folded.append(energy)
    pair = folded[0] * weights + folded[1] * pltpu.roll(weights, LANES // 2, 1)
    tables = [jnp.transpose(pair), jnp.transpose(folded[2] * weights)]
    station_shift = []
    for station in range(STATIONS_DEV):
        rows = tables[station // 2][(station % 2) * 2 * LAGS : (station % 2 + 1) * 2 * LAGS]
        above = jnp.sum(rows[0:LAGS], axis=0, keepdims=True)
        below = jnp.sum(rows[LAGS:], axis=0, keepdims=True)
        station_shift.append(above / (below + eps_small))
    alive = lax.broadcasted_iota(jnp.int32, (1, PAIR_DEV), 1) < places_ref[10, 0]
    shift = jnp.where(alive, jnp.concatenate(station_shift, axis=0), 0.0)
    shift_ref[...] = shift

    signs = jnp.where(alive, incidence(aux_own), 0.0).astype(jnp.bfloat16)
    times = dot_signs(near_block(aux_left, aux_own, aux_right, 1), signs, NN)
    lags = aux_own[0:STATIONS_DEV, 5 * LANES : 6 * LANES]
    rhs = jnp.where(alive, sample_step * (lags + shift), 0.0) - times
    per_event = dot_signs(rhs, signs, NT)
    counts = dot_bf16(signs[EV_DEV : 2 * EV_DEV], signs, NT)
    counts = jnp.where(lax.axis_index("x") == 0, counts, 0.0)
    block_ref[...] = rates_ref[...]
    for event in range(EV_DEV):
        at = count_place(event)
        block_ref[:, at : at + NEAR] = counts[event : event + 1]
    for q in range(4):
        terms = per_event
        if q < 3:
            terms = terms * near_block(aux_left, aux_own, aux_right, 2 + q)
        block_ref[:, q * NEAR : (q + 1) * NEAR] = jnp.sum(terms, axis=0, keepdims=True)
    total = jnp.sum(jnp.sum(rhs * rhs, axis=1, keepdims=True), axis=0, keepdims=True)
    block_ref[:, SQUARE_AT : SQUARE_AT + 1] = total


def symmetric(counts, turned_ref):
    for side, block in ((0, 0), (2, 1)):
        for a in range(EV_DEV):
            at = block * EV_DEV * EV_DEV + a
            turned_ref[pl.ds(at, EV_DEV, stride=EV_DEV), :] = counts[a][side]
    lower = sum(counts[a][0] for a in range(1, EV_DEV)) + counts[0][0]
    upper = sum(counts[a][2] for a in range(1, EV_DEV)) + counts[0][2]
    ends = pltpu.roll(upper, 1, 1) + pltpu.roll(lower, LANES - 1, 1)
    rows = lax.broadcasted_iota(jnp.int32, (EV_DEV, LANES), 0)
    result = []
    for a in range(EV_DEV):
        to_lower = turned_ref[pl.ds(a * EV_DEV, EV_DEV), :]
        to_upper = turned_ref[pl.ds((EV_DEV + a) * EV_DEV, EV_DEV), :]
        result.append(
            [
                counts[a][0] + pltpu.roll(to_upper, 1, 1),
                counts[a][1] - jnp.where(rows == a, ends, 0.0),
                counts[a][2] + pltpu.roll(to_lower, LANES - 1, 1),
            ]
        )
    return result


def solve_kernel(gathered_ref, shift_ref, out_ref, shift_out_ref, rows_ref, turned_ref):
    shift_out_ref[...] = shift_ref[...]
    half = LANES // 2
    tables = []
    for row in range(PAYLOAD // LANES):
        for core in range(2):
            values = gathered_ref[pl.ds(core * half, half), row * LANES : (row + 1) * LANES]
            rows_ref[pl.ds(row * LANES + core, half, stride=2), :] = values
        tables.append(jnp.transpose(rows_ref[pl.ds(row * LANES, LANES), :]))

    def read(at):
        return tables[at // LANES][at % LANES : at % LANES + 8]

    def along(lower, own, upper):
        return own + pltpu.roll(upper, 1, 1) + pltpu.roll(lower, LANES - 1, 1)

    back = [along(*[read(q * NEAR + 8 * side) for side in range(3)]) for q in range(4)]
    counts = symmetric(
        [[read(count_place(a) + 8 * side) for side in range(3)] for a in range(EV_DEV)], turned_ref
    )
    deriv = [
        [read(rate_place(group, station, q)) for q in range(3)]
        for group in range(4)
        for station in range(STATIONS_DEV)
    ]

    def total(values):
        return jnp.sum(jnp.sum(values, axis=1, keepdims=True), axis=0, keepdims=True)

    def inner(left, right):
        terms = left[0] * right[0]
        for q in range(1, 4):
            terms = terms + left[q] * right[q]
        return total(terms)

    def normal(model):
        result = [jnp.zeros((EV_DEV, LANES), jnp.float32) for _ in range(4)]
        for rates in deriv:
            data = model[3]
            for q in range(3):
                data = data + rates[q] * model[q]
            sides = [None, None, None]
            for a in range(EV_DEV):
                row = jnp.broadcast_to(data[a : a + 1], (EV_DEV, LANES))
                for side in range(3):
                    term = counts[a][side] * row
                    sides[side] = term if a == 0 else sides[side] + term
            mixed = along(*sides)
            for q in range(3):
                result[q] = result[q] + rates[q] * mixed
            result[3] = result[3] + mixed
        return result

    rhs_square = total(tables[0][SQUARE_AT : SQUARE_AT + 1])
    beta = jnp.sqrt(rhs_square + eps_small)
    unit_square = rhs_square / (beta * beta)
    adjoint = [value / beta for value in back]
    alpha = jnp.sqrt(inner(adjoint, adjoint) + eps_small)
    model = [value / alpha for value in adjoint]
    search = model
    location = [jnp.zeros((EV_DEV, LANES), jnp.float32) for _ in range(4)]
    phi_bar = beta
    rho_bar = alpha
    for turn in range(2):
        normal_model = normal(model)
        square = inner(model, normal_model) - 2.0 * alpha * inner(model, adjoint)
        square = jnp.maximum(square + alpha * alpha * unit_square, 0.0)
        beta = jnp.sqrt(square + eps_small)
        rho = jnp.sqrt(rho_bar * rho_bar + beta * beta)
        cosine = rho_bar / rho
        sine = beta / rho
        phi = cosine * phi_bar
        phi_bar = sine * phi_bar
        step = phi / rho
        location = [location[q] + step * search[q] for q in range(4)]
        if turn == 0:
            unit_square = square / (beta * beta)
            adjoint = [(normal_model[q] - alpha * adjoint[q]) / beta for q in range(4)]
            vector = [adjoint[q] - beta * model[q] for q in range(4)]
            alpha = jnp.sqrt(inner(vector, vector) + eps_small)
            model = [value / alpha for value in vector]
            theta = sine * alpha
            rho_bar = -cosine * alpha
            search = [model[q] - theta / rho * search[q] for q in range(4)]

    lanes = lax.broadcasted_iota(jnp.int32, (ROWS, LANES), 1)
    mine = (lanes == device_index()).astype(jnp.float32)
    parts = dot_bf16(mine.astype(jnp.bfloat16), thirds(jnp.concatenate(location, axis=0)), NT)
    rows = 4 * EV_DEV
    own = parts[:, 0:rows] + parts[:, rows : 2 * rows] + parts[:, 2 * rows :]
    for q in range(4):
        out_ref[q : q + 1, :] = own[0:1, q * EV_DEV : (q + 1) * EV_DEV]


def from_other_chip(block):
    count = lax.axis_size("g") * lax.axis_size("c")
    partners = [(i, i - 1 + 2 * (i % 2)) for i in range(count)]
    route = [(i, other) for i, other in partners if 0 <= other < count]
    return lax.ppermute(block, ("g", "c"), route)


def spread(row, axis):
    copies = jnp.broadcast_to(row, (lax.axis_size(axis), row.shape[1]))
    return lax.all_to_all(copies, axis, 0, 0, tiled=True)


VMEM = pl.BlockSpec(memory_space=pltpu.VMEM)
SMEM = pl.BlockSpec(memory_space=pltpu.SMEM)
HBM = pl.BlockSpec(memory_space=pltpu.HBM)
PARAMS = pltpu.CompilerParams(vmem_limit_bytes=VMEM_BYTES)


def pack(traces, ray_slowness, travel_time, pair_first, pair_second, pair_lag):
    arguments = (
        traces.reshape(TRACES_DEV, EV_DEV, LENGTH),
        ray_slowness,
        travel_time,
        pair_first.reshape(1, PAIR_DEV),
        pair_second.reshape(1, PAIR_DEV),
        pair_lag,
    )
    return pl.pallas_call(
        pack_kernel,
        out_shape=pltpu.VMEM((TRACES_DEV + 1, ROWS, LENGTH), jnp.float32),
        in_specs=[HBM] * 6,
        out_specs=VMEM,
        scratch_shapes=[
            pltpu.VMEM((3, STATIONS_DEV, EV_DEV), jnp.float32),
            pltpu.VMEM((STATIONS_DEV, EV_DEV), jnp.float32),
            pltpu.VMEM((1, PAIR_DEV), jnp.int32),
            pltpu.VMEM((1, PAIR_DEV), jnp.int32),
            pltpu.VMEM((STATIONS_DEV, PAIR_DEV), jnp.int32),
            pltpu.SemaphoreType.DMA((6,)),
        ],
        compiler_params=PARAMS,
        name="pack",
    )(*[pltpu.with_memory_space_constraint(value, pltpu.HBM) for value in arguments])


def firsts(pair_live, message):
    toeplitz = jax.ShapeDtypeStruct((TRACES_DEV, EV_DEV * LAGS, SPAN), jnp.bfloat16)
    return pl.pallas_call(
        first_kernel,
        out_shape=(
            toeplitz,
            toeplitz,
            pltpu.SMEM((PLACE_ROWS, PAIR_DEV), jnp.int32),
            jax.ShapeDtypeStruct((PAIR_DEV, EV_DEV * LAGS), jnp.float32),
            jax.ShapeDtypeStruct((1, PAYLOAD), jnp.float32),
        ),
        in_specs=[SMEM, VMEM],
        out_specs=(VMEM, VMEM, SMEM, VMEM, VMEM),
        scratch_shapes=[
            pltpu.VMEM((PLACE_ROWS, PAIR_DEV), jnp.int32),
            pltpu.SemaphoreType.DMA,
        ],
        compiler_params=PARAMS,
        name="firsts",
    )(pair_live, message)


MOVED = jax.ShapeDtypeStruct((TRACES_DEV * PAIR_DEV * ROWS, LANES), jnp.float32)


def early(places, chip):
    return pl.pallas_call(
        early_kernel,
        out_shape=MOVED,
        in_specs=[SMEM, VMEM],
        out_specs=VMEM,
        scratch_shapes=[pltpu.VMEM((2 * PART_ROWS + 2 * ROWS, LANES), jnp.float32)],
        compiler_params=PARAMS,
        name="early",
    )(places, chip)


def late(places, moved, chip, from_cross, high, low, pick, rates):
    refined_shift, block, _ = pl.pallas_call(
        late_kernel,
        out_shape=(
            jax.ShapeDtypeStruct((STATIONS_DEV, PAIR_DEV), jnp.float32),
            jax.ShapeDtypeStruct((1, PAYLOAD), jnp.float32),
            MOVED,
        ),
        in_specs=[SMEM] + [VMEM] * 7,
        out_specs=(VMEM, VMEM, VMEM),
        scratch_shapes=[pltpu.VMEM((PART_ROWS + 2 * ROWS, LANES), jnp.float32)],
        input_output_aliases={1: 2},
        compiler_params=PARAMS,
        name="late",
    )(places, moved, chip, from_cross, high, low, pick, rates)
    return refined_shift, block


def solve(gathered, shift):
    return pl.pallas_call(
        solve_kernel,
        out_shape=(
            jax.ShapeDtypeStruct((4, EV_DEV), jnp.float32),
            jax.ShapeDtypeStruct((STATIONS_DEV, PAIR_DEV), jnp.float32),
        ),
        in_specs=[VMEM, VMEM],
        out_specs=(VMEM, VMEM),
        scratch_shapes=[
            pltpu.VMEM((PAYLOAD, LANES), jnp.float32),
            pltpu.VMEM((2 * EV_DEV * EV_DEV, LANES), jnp.float32),
        ],
        compiler_params=PARAMS,
        name="solve",
    )(gathered, shift)


def body(traces, ray_slowness, travel_time, pair_first, pair_second, pair_lag, pair_live):
    message = pack(traces, ray_slowness, travel_time, pair_first, pair_second, pair_lag)
    from_cross = from_other_chip(message)
    pair_live = lax.optimization_barrier((message, pair_live))[1]
    high, low, places, pick, rates = firsts(pair_live, message)
    places = pltpu.with_memory_space_constraint(places, pltpu.SMEM)
    chip = lax.all_gather(message, "c", axis=0)
    moved = early(places, chip)
    shift, block = late(places, moved, chip, from_cross, high, low, pick, rates)
    block = jnp.sum(spread(block, "x"), axis=0, keepdims=True)
    chips = lax.axis_size("g")
    gathered = lax.all_gather(spread(block, "g"), "c", axis=0)
    location, refined_shift = solve(gathered.reshape(2 * chips, PAYLOAD), shift)
    return refined_shift, location


def solution(mesh):
    ev, st = mesh.devices.shape
    fine = Mesh(mesh.devices.reshape(ev // 2, 2, st), ("g", "c", "x"))
    event_axes = ("g", "c")
    in_specs = (
        P("x", None, event_axes, None),
        P(None, "x", event_axes),
        P("x", event_axes),
        P(event_axes),
        P(event_axes),
        P("x", event_axes),
        P(event_axes),
    )
    out_specs = (P("x", event_axes), P(None, event_axes))
    return jax.shard_map(body, mesh=fine, in_specs=in_specs, out_specs=out_specs, check_vma=False)
```

```python
import jax
import jax.numpy as jnp
from jax import lax
from jax.experimental import pallas as pl
from jax.experimental.pallas import tpu as pltpu
from jax.sharding import Mesh
from jax.sharding import PartitionSpec as P

LAGS = 32
LANES = 128
ROWS = 8
EV_DEV = 8
NEAR = 3 * EV_DEV
STATIONS_DEV = 3
TRACES_DEV = 9
LENGTH = 1024
CHUNKS = LENGTH // LANES
QUARTER = LENGTH // 4
WINDOW = LENGTH // 2
SPAN = WINDOW + LANES
SPAN_CHUNKS = SPAN // LANES
PAIR_DEV = 128
PART_ROWS = TRACES_DEV * EV_DEV * CHUNKS
VMEM_BYTES = 24 * 1024 * 1024
PLACE_ROWS = 16
GROUP = 16
PAYLOAD = 5 * LANES
SQUARE_AT = 4 * NEAR

eps_small = 1e-06
sample_step = 0.01
NT = (((1,), (1,)), ((), ()))
NN = (((1,), (0,)), ((), ()))


def device_index():
    return lax.axis_index("g") * 2 + lax.axis_index("c")


def dot_bf16(left, right, dims):
    return lax.dot_general(left, right, dims, preferred_element_type=jnp.float32)


def count_place(event):
    return LANES + NEAR * event if event < 5 else 2 * LANES + NEAR * (event - 5)


def rate_place(group, station, q):
    index = (group * STATIONS_DEV + station) * 3 + q
    return 3 * LANES + 8 * index if index < 32 else 2 * LANES + 96 + 8 * (index - 32)


def thirds(values):
    high = values.astype(jnp.bfloat16)
    rest = values - high.astype(jnp.float32)
    middle = rest.astype(jnp.bfloat16)
    low = (rest - middle.astype(jnp.float32)).astype(jnp.bfloat16)
    return jnp.concatenate([high, middle, low], axis=0)


def dot_signs(left, signs, dims):
    rows = left.shape[0]
    parts = dot_bf16(thirds(left), signs, dims)
    return parts[0:rows] + parts[rows : 2 * rows] + parts[2 * rows :]


def split_bf16(values):
    high = values.astype(jnp.bfloat16)
    low = (values - high.astype(jnp.float32)).astype(jnp.bfloat16)
    return high, low


def pack_kernel(
    traces_ref,
    slowness_ref,
    time_ref,
    first_ref,
    second_ref,
    lag_ref,
    out_ref,
    slowness,
    time,
    first,
    second,
    lag,
    sems,
):
    pairs = [
        (traces_ref, out_ref.at[pl.ds(0, TRACES_DEV)]),
        (slowness_ref, slowness),
        (time_ref, time),
        (first_ref, first),
        (second_ref, second),
        (lag_ref, lag),
    ]
    copies = [
        pltpu.make_async_copy(source, target, sems.at[at])
        for at, (source, target) in enumerate(pairs)
    ]
    for copy in copies:
        copy.start()
    aux = out_ref.at[TRACES_DEV]
    aux[...] = jnp.zeros((ROWS, LENGTH), jnp.float32)
    for copy in copies[1:]:
        copy.wait()
    base = device_index() * EV_DEV - EV_DEV
    for row, ids in enumerate((first, second)):
        aux[row : row + 1, 0:LANES] = (ids[...] - base).astype(jnp.float32)
    aux[0:STATIONS_DEV, LANES : LANES + EV_DEV] = time[...]
    for q in range(3):
        lane = (2 + q) * LANES
        aux[0:STATIONS_DEV, lane : lane + EV_DEV] = slowness[q]
    aux[0:STATIONS_DEV, 5 * LANES : 6 * LANES] = lag[...].astype(jnp.float32)
    copies[0].wait()


def first_windows(own_ref, high_ref, low_ref, items):
    for item in items:
        window = own_ref[item, :, QUARTER : QUARTER + WINDOW]
        power = jnp.sum(window * window, axis=1, keepdims=True)
        window = window * lax.rsqrt(power + eps_small)
        padded = jnp.concatenate([window, jnp.zeros((EV_DEV, LANES), jnp.float32)], axis=1)
        for event in range(EV_DEV):
            wide = jnp.broadcast_to(padded[event : event + 1], (LAGS, SPAN))
            wide = pltpu.roll(wide, 0, 1, stride=1, stride_axis=0)
            high, low = split_bf16(wide)
            high_ref[item, pl.ds(event * LAGS, LAGS), :] = high
            low_ref[item, pl.ds(event * LAGS, LAGS), :] = low


def first_kernel(
    live_ref, own_ref, high_ref, low_ref, places_ref, pick_ref, rates_ref
):
    aux = own_ref[TRACES_DEV]
    first = aux[0:1, 0:LANES].astype(jnp.int32)
    second = aux[1:2, 0:LANES].astype(jnp.int32)
    begin = aux[0:STATIONS_DEV, 5 * LANES : 6 * LANES].astype(jnp.int32) + (QUARTER - LAGS // 2)
    side = lax.shift_right_arithmetic(second, 3)
    mate_side = 2 - 2 * lax.axis_index("c")
    away = jnp.logical_and(side != 1, side != mate_side)
    part = jnp.where(side == 1, 0, jnp.where(away, 2, 1))
    alive = lax.broadcasted_iota(jnp.int32, (1, PAIR_DEV), 1) < live_ref[0]
    far = jnp.logical_and(away, alive)
    event = jnp.bitwise_and(second, EV_DEV - 1)
    rows = part * PART_ROWS + event * CHUNKS + lax.shift_right_arithmetic(begin, 7)
    near = jnp.logical_and(jnp.logical_not(away), alive)
    upper = lax.broadcasted_iota(jnp.int32, (PAIR_DEV, PAIR_DEV), 0)
    lower = lax.broadcasted_iota(jnp.int32, (PAIR_DEV, PAIR_DEV), 1)
    lane_ids = lower[0:1]
    ahead = (upper <= lower).astype(jnp.bfloat16)
    slots = lax.broadcasted_iota(jnp.int32, (ROWS, PAIR_DEV), 1).astype(jnp.bfloat16)
    hots, counts, listed = [], [], []
    for marked in (far, near):
        ones = marked.astype(jnp.float32)
        wide = jnp.broadcast_to(ones, (ROWS, PAIR_DEV)).astype(jnp.bfloat16)
        place = jnp.where(marked, dot_bf16(wide, ahead, NN)[0:1] - 1.0, -1.0)
        hots.append((upper.astype(jnp.float32) == place).astype(jnp.bfloat16))
        counts.append(jnp.sum(ones, axis=1, keepdims=True).astype(jnp.int32))
    first_windows(own_ref, high_ref, low_ref, range(2))
    for hot in hots:
        listed.append(dot_bf16(slots, hot, NT)[0:1])
    first_windows(own_ref, high_ref, low_ref, range(2, 4))
    places_ref[...] = jnp.zeros((PLACE_ROWS, PAIR_DEV), jnp.int32)
    places_ref[0:3, :] = rows
    places_ref[3:6, :] = jnp.bitwise_and(begin, LANES - 1)
    for at in range(2):
        filled = jnp.where(lane_ids < counts[at], listed[at], listed[at][:, 0:1])
        places_ref[6 + at : 7 + at, :] = filled.astype(jnp.int32)
        places_ref[8 + at : 9 + at, :] = jnp.broadcast_to(counts[at], (1, PAIR_DEV))
    places_ref[10:11, :] = jnp.broadcast_to(live_ref[0], (1, PAIR_DEV))
    first_windows(own_ref, high_ref, low_ref, range(4, TRACES_DEV))
    ends = jnp.bitwise_and(first, EV_DEV - 1).astype(jnp.float32)
    column = jnp.transpose(jnp.broadcast_to(ends, (LANES, PAIR_DEV)))
    groups = lax.broadcasted_iota(jnp.int32, (PAIR_DEV, LANES), 1) // LAGS
    for half in range(2):
        mine = column == (groups + half * (LANES // LAGS)).astype(jnp.float32)
        pick_ref[:, half * LANES : (half + 1) * LANES] = mine.astype(jnp.float32)
    rates_ref[...] = jnp.zeros((1, PAYLOAD), jnp.float32)
    for station in range(STATIONS_DEV):
        for q in range(3):
            lane = (2 + q) * LANES
            own = aux[station : station + 1, lane : lane + EV_DEV]
            for group in range(4):
                at = rate_place(group, station, q)
                rates_ref[:, at : at + EV_DEV] = jnp.where(
                    lax.axis_index("x") == group, own, 0.0
                )


def fill_table(ref, table_ref, part):
    for item in range(TRACES_DEV):
        values = ref[item]
        power = jnp.sum(values * values, axis=1, keepdims=True)
        values = values * lax.rsqrt(power + eps_small)
        for chunk in range(CHUNKS):
            start = part * PART_ROWS + item * EV_DEV * CHUNKS + chunk
            table_ref[pl.ds(start, EV_DEV, stride=CHUNKS), :] = values[
                :, chunk * LANES : (chunk + 1) * LANES
            ]


def align(places_ref, table_ref, moved_ref, slot, offset):
    lane_ids = lax.broadcasted_iota(jnp.int32, (ROWS, LANES), 1)
    for station in range(STATIONS_DEV):
        row = places_ref[station, slot] - offset
        lane = places_ref[3 + station, slot]
        turn = jnp.bitwise_and(-lane, LANES - 1)
        keep = lane_ids >= lane
        for component in range(3):
            item = station * 3 + component
            at = item * EV_DEV * CHUNKS
            here = table_ref[pl.ds(row + at, ROWS), :]
            after = table_ref[pl.ds(row + (at + 1), ROWS), :]
            moved = pltpu.roll(jnp.where(keep, here, after), turn, 1)
            to = pl.multiple_of((item * PAIR_DEV + slot) * ROWS, ROWS)
            moved_ref[pl.ds(to, ROWS), :] = moved


def groups_of(count):
    return lax.div(count + (GROUP - 1), GROUP)


def early_kernel(listed_ref, chip_ref, moved_ref, places_ref, table_ref, sem):
    fetch = pltpu.make_async_copy(listed_ref, places_ref, sem)
    fetch.start()
    table_ref[pl.ds(2 * PART_ROWS, 2 * ROWS), :] = jnp.zeros((2 * ROWS, LANES), jnp.float32)
    core = lax.axis_index("c")
    fill_table(chip_ref.at[core], table_ref, 0)
    fill_table(chip_ref.at[1 - core], table_ref, 1)
    fetch.wait()

    def step(index, carry):
        for turn in range(GROUP):
            align(places_ref, table_ref, moved_ref, places_ref[7, index * GROUP + turn], 0)
        return carry

    lax.fori_loop(0, groups_of(places_ref[9, 0]), step, 0)


def incidence(aux):
    events = lax.broadcasted_iota(jnp.int32, (NEAR, PAIR_DEV), 0).astype(jnp.float32)
    starts = (events == aux[0:1, 0:LANES]).astype(jnp.float32)
    return starts - (events == aux[1:2, 0:LANES]).astype(jnp.float32)


def near_block(left, own, right, part):
    lane = part * LANES
    return jnp.concatenate(
        [aux[0:STATIONS_DEV, lane : lane + EV_DEV] for aux in (left, own, right)], axis=1
    )


def late_kernel(
    places_ref,
    moved_in_ref,
    chip_ref,
    cross_ref,
    high_ref,
    low_ref,
    pick_ref,
    rates_ref,
    shift_ref,
    block_ref,
    moved_ref,
    table_ref,
):
    del moved_in_ref
    table_ref[pl.ds(PART_ROWS, 2 * ROWS), :] = jnp.zeros((2 * ROWS, LANES), jnp.float32)
    fill_table(cross_ref, table_ref, 0)

    def step(index, carry):
        for turn in range(GROUP):
            slot = places_ref[6, index * GROUP + turn]
            align(places_ref, table_ref, moved_ref, slot, 2 * PART_ROWS)
        return carry

    lax.fori_loop(0, groups_of(places_ref[8, 0]), step, 0)

    core = lax.axis_index("c")
    aux_own = chip_ref[core, TRACES_DEV]
    aux_left = jnp.where(core == 0, cross_ref[TRACES_DEV], chip_ref[0, TRACES_DEV])
    aux_right = jnp.where(core == 0, chip_ref[1, TRACES_DEV], cross_ref[TRACES_DEV])

    lane_ids = lax.broadcasted_iota(jnp.int32, (1, LANES), 1)
    centred = (lane_ids - LAGS // 2).astype(jnp.float32)
    weights = jnp.where(lane_ids < LAGS, centred, jnp.where(lane_ids < 2 * LAGS, 1.0, 0.0))
    folded = []
    for station in range(STATIONS_DEV):
        energy = jnp.zeros((PAIR_DEV, EV_DEV * LAGS), jnp.float32)
        for component in range(3):
            item = station * 3 + component
            pieces = [
                moved_ref[pl.ds(item * PAIR_DEV * ROWS + chunk, PAIR_DEV, stride=ROWS), :]
                for chunk in range(SPAN_CHUNKS)
            ]
            high, low = split_bf16(jnp.concatenate(pieces, axis=1))
            both = dot_bf16(jnp.concatenate([high, low], axis=0), high_ref[item], NT)
            xcorr = both[0:PAIR_DEV] + both[PAIR_DEV:] + dot_bf16(high, low_ref[item], NT)
            energy = energy + xcorr * xcorr
        energy = energy * pick_ref[...]
        energy = energy[:, 0:LANES] + energy[:, LANES:]
        energy = energy + pltpu.roll(energy, LANES // 2, 1)
        energy = energy + pltpu.roll(energy, LANES // 4, 1)
        folded.append(energy)
    pair = folded[0] * weights + folded[1] * pltpu.roll(weights, LANES // 2, 1)
    tables = [jnp.transpose(pair), jnp.transpose(folded[2] * weights)]
    station_shift = []
    for station in range(STATIONS_DEV):
        rows = tables[station // 2][(station % 2) * 2 * LAGS : (station % 2 + 1) * 2 * LAGS]
        above = jnp.sum(rows[0:LAGS], axis=0, keepdims=True)
        below = jnp.sum(rows[LAGS:], axis=0, keepdims=True)
        station_shift.append(above / (below + eps_small))
    alive = lax.broadcasted_iota(jnp.int32, (1, PAIR_DEV), 1) < places_ref[10, 0]
    shift = jnp.where(alive, jnp.concatenate(station_shift, axis=0), 0.0)
    shift_ref[...] = shift

    signs = jnp.where(alive, incidence(aux_own), 0.0).astype(jnp.bfloat16)
    times = dot_signs(near_block(aux_left, aux_own, aux_right, 1), signs, NN)
    lags = aux_own[0:STATIONS_DEV, 5 * LANES : 6 * LANES]
    rhs = jnp.where(alive, sample_step * (lags + shift), 0.0) - times
    per_event = dot_signs(rhs, signs, NT)
    counts = dot_bf16(signs[EV_DEV : 2 * EV_DEV], signs, NT)
    counts = jnp.where(lax.axis_index("x") == 0, counts, 0.0)
    block_ref[...] = rates_ref[...]
    for event in range(EV_DEV):
        at = count_place(event)
        block_ref[:, at : at + NEAR] = counts[event : event + 1]
    for q in range(4):
        terms = per_event
        if q < 3:
            terms = terms * near_block(aux_left, aux_own, aux_right, 2 + q)
        block_ref[:, q * NEAR : (q + 1) * NEAR] = jnp.sum(terms, axis=0, keepdims=True)
    total = jnp.sum(jnp.sum(rhs * rhs, axis=1, keepdims=True), axis=0, keepdims=True)
    block_ref[:, SQUARE_AT : SQUARE_AT + 1] = total


def symmetric(counts, turned_ref):
    for side, block in ((0, 0), (2, 1)):
        for a in range(EV_DEV):
            at = block * EV_DEV * EV_DEV + a
            turned_ref[pl.ds(at, EV_DEV, stride=EV_DEV), :] = counts[a][side]
    lower = sum(counts[a][0] for a in range(1, EV_DEV)) + counts[0][0]
    upper = sum(counts[a][2] for a in range(1, EV_DEV)) + counts[0][2]
    ends = pltpu.roll(upper, 1, 1) + pltpu.roll(lower, LANES - 1, 1)
    rows = lax.broadcasted_iota(jnp.int32, (EV_DEV, LANES), 0)
    result = []
    for a in range(EV_DEV):
        to_lower = turned_ref[pl.ds(a * EV_DEV, EV_DEV), :]
        to_upper = turned_ref[pl.ds((EV_DEV + a) * EV_DEV, EV_DEV), :]
        result.append(
            [
                counts[a][0] + pltpu.roll(to_upper, 1, 1),
                counts[a][1] - jnp.where(rows == a, ends, 0.0),
                counts[a][2] + pltpu.roll(to_lower, LANES - 1, 1),
            ]
        )
    return result


def solve_kernel(gathered_ref, shift_ref, out_ref, shift_out_ref, rows_ref, turned_ref):
    shift_out_ref[...] = shift_ref[...]
    half = LANES // 2
    tables = []
    for row in range(PAYLOAD // LANES):
        for core in range(2):
            values = gathered_ref[pl.ds(core * half, half), row * LANES : (row + 1) * LANES]
            rows_ref[pl.ds(row * LANES + core, half, stride=2), :] = values
        tables.append(jnp.transpose(rows_ref[pl.ds(row * LANES, LANES), :]))

    def read(at):
        return tables[at // LANES][at % LANES : at % LANES + 8]

    def along(lower, own, upper):
        return own + pltpu.roll(upper, 1, 1) + pltpu.roll(lower, LANES - 1, 1)

    back = [along(*[read(q * NEAR + 8 * side) for side in range(3)]) for q in range(4)]
    counts = symmetric(
        [[read(count_place(a) + 8 * side) for side in range(3)] for a in range(EV_DEV)], turned_ref
    )
    deriv = [
        [read(rate_place(group, station, q)) for q in range(3)]
        for group in range(4)
        for station in range(STATIONS_DEV)
    ]

    def total(values):
        return jnp.sum(jnp.sum(values, axis=1, keepdims=True), axis=0, keepdims=True)

    def inner(left, right):
        terms = left[0] * right[0]
        for q in range(1, 4):
            terms = terms + left[q] * right[q]
        return total(terms)

    def normal(model):
        result = [jnp.zeros((EV_DEV, LANES), jnp.float32) for _ in range(4)]
        for rates in deriv:
            data = model[3]
            for q in range(3):
                data = data + rates[q] * model[q]
            sides = [None, None, None]
            for a in range(EV_DEV):
                row = jnp.broadcast_to(data[a : a + 1], (EV_DEV, LANES))
                for side in range(3):
                    term = counts[a][side] * row
                    sides[side] = term if a == 0 else sides[side] + term
            mixed = along(*sides)
            for q in range(3):
                result[q] = result[q] + rates[q] * mixed
            result[3] = result[3] + mixed
        return result

    rhs_square = total(tables[0][SQUARE_AT : SQUARE_AT + 1])
    beta = jnp.sqrt(rhs_square + eps_small)
    unit_square = rhs_square / (beta * beta)
    adjoint = [value / beta for value in back]
    alpha = jnp.sqrt(inner(adjoint, adjoint) + eps_small)
    model = [value / alpha for value in adjoint]
    search = model
    location = [jnp.zeros((EV_DEV, LANES), jnp.float32) for _ in range(4)]
    phi_bar = beta
    rho_bar = alpha
    for turn in range(2):
        normal_model = normal(model)
        square = inner(model, normal_model) - 2.0 * alpha * inner(model, adjoint)
        square = jnp.maximum(square + alpha * alpha * unit_square, 0.0)
        beta = jnp.sqrt(square + eps_small)
        rho = jnp.sqrt(rho_bar * rho_bar + beta * beta)
        cosine = rho_bar / rho
        sine = beta / rho
        phi = cosine * phi_bar
        phi_bar = sine * phi_bar
        step = phi / rho
        location = [location[q] + step * search[q] for q in range(4)]
        if turn == 0:
            unit_square = square / (beta * beta)
            adjoint = [(normal_model[q] - alpha * adjoint[q]) / beta for q in range(4)]
            vector = [adjoint[q] - beta * model[q] for q in range(4)]
            alpha = jnp.sqrt(inner(vector, vector) + eps_small)
            model = [value / alpha for value in vector]
            theta = sine * alpha
            rho_bar = -cosine * alpha
            search = [model[q] - theta / rho * search[q] for q in range(4)]

    lanes = lax.broadcasted_iota(jnp.int32, (ROWS, LANES), 1)
    mine = (lanes == device_index()).astype(jnp.float32)
    parts = dot_bf16(mine.astype(jnp.bfloat16), thirds(jnp.concatenate(location, axis=0)), NT)
    rows = 4 * EV_DEV
    own = parts[:, 0:rows] + parts[:, rows : 2 * rows] + parts[:, 2 * rows :]
    for q in range(4):
        out_ref[q : q + 1, :] = own[0:1, q * EV_DEV : (q + 1) * EV_DEV]


def from_other_chip(block):
    count = lax.axis_size("g") * lax.axis_size("c")
    partners = [(i, i - 1 + 2 * (i % 2)) for i in range(count)]
    route = [(i, other) for i, other in partners if 0 <= other < count]
    return lax.ppermute(block, ("g", "c"), route)


def spread(row, axis):
    copies = jnp.broadcast_to(row, (lax.axis_size(axis), row.shape[1]))
    return lax.all_to_all(copies, axis, 0, 0, tiled=True)


VMEM = pl.BlockSpec(memory_space=pltpu.VMEM)
SMEM = pl.BlockSpec(memory_space=pltpu.SMEM)
HBM = pl.BlockSpec(memory_space=pltpu.HBM)
PARAMS = pltpu.CompilerParams(vmem_limit_bytes=VMEM_BYTES)


def pack(traces, ray_slowness, travel_time, pair_first, pair_second, pair_lag):
    arguments = (
        traces.reshape(TRACES_DEV, EV_DEV, LENGTH),
        ray_slowness,
        travel_time,
        pair_first.reshape(1, PAIR_DEV),
        pair_second.reshape(1, PAIR_DEV),
        pair_lag,
    )
    return pl.pallas_call(
        pack_kernel,
        out_shape=pltpu.VMEM((TRACES_DEV + 1, ROWS, LENGTH), jnp.float32),
        in_specs=[HBM] * 6,
        out_specs=VMEM,
        scratch_shapes=[
            pltpu.VMEM((3, STATIONS_DEV, EV_DEV), jnp.float32),
            pltpu.VMEM((STATIONS_DEV, EV_DEV), jnp.float32),
            pltpu.VMEM((1, PAIR_DEV), jnp.int32),
            pltpu.VMEM((1, PAIR_DEV), jnp.int32),
            pltpu.VMEM((STATIONS_DEV, PAIR_DEV), jnp.int32),
            pltpu.SemaphoreType.DMA((6,)),
        ],
        compiler_params=PARAMS,
        name="pack",
    )(*[pltpu.with_memory_space_constraint(value, pltpu.HBM) for value in arguments])


def firsts(pair_live, message):
    toeplitz = jax.ShapeDtypeStruct((TRACES_DEV, EV_DEV * LAGS, SPAN), jnp.bfloat16)
    return pl.pallas_call(
        first_kernel,
        out_shape=(
            toeplitz,
            toeplitz,
            jax.ShapeDtypeStruct((PLACE_ROWS, PAIR_DEV), jnp.int32),
            jax.ShapeDtypeStruct((PAIR_DEV, EV_DEV * LAGS), jnp.float32),
            jax.ShapeDtypeStruct((1, PAYLOAD), jnp.float32),
        ),
        in_specs=[SMEM, VMEM],
        out_specs=(VMEM,) * 5,
        compiler_params=PARAMS,
        name="firsts",
    )(pair_live, message)


MOVED = jax.ShapeDtypeStruct((TRACES_DEV * PAIR_DEV * ROWS + ROWS, LANES), jnp.float32)


def early(places, chip):
    return pl.pallas_call(
        early_kernel,
        out_shape=(MOVED, pltpu.SMEM((PLACE_ROWS, PAIR_DEV), jnp.int32)),
        in_specs=[VMEM, VMEM],
        out_specs=(VMEM, SMEM),
        scratch_shapes=[
            pltpu.VMEM((2 * PART_ROWS + 2 * ROWS, LANES), jnp.float32),
            pltpu.SemaphoreType.DMA,
        ],
        compiler_params=PARAMS,
        name="early",
    )(places, chip)


def late(places, moved, chip, from_cross, high, low, pick, rates):
    refined_shift, block, _ = pl.pallas_call(
        late_kernel,
        out_shape=(
            jax.ShapeDtypeStruct((STATIONS_DEV, PAIR_DEV), jnp.float32),
            jax.ShapeDtypeStruct((1, PAYLOAD), jnp.float32),
            MOVED,
        ),
        in_specs=[SMEM] + [VMEM] * 7,
        out_specs=(VMEM, VMEM, VMEM),
        scratch_shapes=[pltpu.VMEM((PART_ROWS + 2 * ROWS, LANES), jnp.float32)],
        input_output_aliases={1: 2},
        compiler_params=PARAMS,
        name="late",
    )(places, moved, chip, from_cross, high, low, pick, rates)
    return refined_shift, block


def solve(gathered, shift):
    return pl.pallas_call(
        solve_kernel,
        out_shape=(
            jax.ShapeDtypeStruct((4, EV_DEV), jnp.float32),
            jax.ShapeDtypeStruct((STATIONS_DEV, PAIR_DEV), jnp.float32),
        ),
        in_specs=[VMEM, VMEM],
        out_specs=(VMEM, VMEM),
        scratch_shapes=[
            pltpu.VMEM((PAYLOAD + ROWS, LANES), jnp.float32),
            pltpu.VMEM((2 * EV_DEV * EV_DEV + ROWS, LANES), jnp.float32),
        ],
        compiler_params=PARAMS,
        name="solve",
    )(gathered, shift)


def body(traces, ray_slowness, travel_time, pair_first, pair_second, pair_lag, pair_live):
    message = pack(traces, ray_slowness, travel_time, pair_first, pair_second, pair_lag)
    from_cross = from_other_chip(message)
    pair_live = lax.optimization_barrier((message, pair_live))[1]
    high, low, places, pick, rates = firsts(pair_live, message)
    chip = lax.all_gather(message, "c", axis=0)
    moved, places = early(places, chip)
    places = pltpu.with_memory_space_constraint(places, pltpu.SMEM)
    shift, block = late(places, moved, chip, from_cross, high, low, pick, rates)
    block = jnp.sum(spread(block, "x"), axis=0, keepdims=True)
    chips = lax.axis_size("g")
    gathered = lax.all_gather(spread(block, "g"), "c", axis=0)
    location, refined_shift = solve(gathered.reshape(2 * chips, PAYLOAD), shift)
    return refined_shift, location


def solution(mesh):
    ev, st = mesh.devices.shape
    fine = Mesh(mesh.devices.reshape(ev // 2, 2, st), ("g", "c", "x"))
    event_axes = ("g", "c")
    in_specs = (
        P("x", None, event_axes, None),
        P(None, "x", event_axes),
        P("x", event_axes),
        P(event_axes),
        P(event_axes),
        P("x", event_axes),
        P(event_axes),
    )
    out_specs = (P("x", event_axes), P(None, event_axes))
    return jax.shard_map(body, mesh=fine, in_specs=in_specs, out_specs=out_specs, check_vma=False)
```

```python
import jax
import jax.numpy as jnp
from jax import lax
from jax.experimental import pallas as pl
from jax.experimental.pallas import tpu as pltpu
from jax.sharding import Mesh
from jax.sharding import PartitionSpec as P

LAGS = 32
LANES = 128
ROWS = 8
EV_DEV = 8
NEAR = 3 * EV_DEV
STATIONS_DEV = 3
TRACES_DEV = 9
LENGTH = 1024
CHUNKS = LENGTH // LANES
QUARTER = LENGTH // 4
WINDOW = LENGTH // 2
SPAN = WINDOW + LANES
SPAN_CHUNKS = SPAN // LANES
PAIR_DEV = 128
PART_ROWS = TRACES_DEV * EV_DEV * CHUNKS
VMEM_BYTES = 24 * 1024 * 1024
PLACE_ROWS = 16
FIRST_ITEMS = 3
GROUP = 16
PAYLOAD = 5 * LANES
SQUARE_AT = 4 * NEAR

eps_small = 1e-06
sample_step = 0.01
NT = (((1,), (1,)), ((), ()))
NN = (((1,), (0,)), ((), ()))


def device_index():
    return lax.axis_index("g") * 2 + lax.axis_index("c")


def dot_bf16(left, right, dims):
    return lax.dot_general(left, right, dims, preferred_element_type=jnp.float32)


def count_place(event):
    return LANES + NEAR * event if event < 5 else 2 * LANES + NEAR * (event - 5)


def rate_place(group, station, q):
    index = (group * STATIONS_DEV + station) * 3 + q
    return 3 * LANES + 8 * index if index < 32 else 2 * LANES + 96 + 8 * (index - 32)


def thirds(values):
    high = values.astype(jnp.bfloat16)
    rest = values - high.astype(jnp.float32)
    middle = rest.astype(jnp.bfloat16)
    low = (rest - middle.astype(jnp.float32)).astype(jnp.bfloat16)
    return jnp.concatenate([high, middle, low], axis=0)


def dot_signs(left, signs, dims):
    rows = left.shape[0]
    parts = dot_bf16(thirds(left), signs, dims)
    return parts[0:rows] + parts[rows : 2 * rows] + parts[2 * rows :]


def split_bf16(values):
    high = values.astype(jnp.bfloat16)
    low = (values - high.astype(jnp.float32)).astype(jnp.bfloat16)
    return high, low


def pack_kernel(
    traces_ref,
    slowness_ref,
    time_ref,
    first_ref,
    second_ref,
    lag_ref,
    out_ref,
    slowness,
    time,
    first,
    second,
    lag,
    sems,
):
    pairs = [
        (traces_ref, out_ref.at[pl.ds(0, TRACES_DEV)]),
        (slowness_ref, slowness),
        (time_ref, time),
        (first_ref, first),
        (second_ref, second),
        (lag_ref, lag),
    ]
    copies = [
        pltpu.make_async_copy(source, target, sems.at[at])
        for at, (source, target) in enumerate(pairs)
    ]
    for copy in copies:
        copy.start()
    aux = out_ref.at[TRACES_DEV]
    aux[...] = jnp.zeros((ROWS, LENGTH), jnp.float32)
    for copy in copies[1:]:
        copy.wait()
    base = device_index() * EV_DEV - EV_DEV
    for row, ids in enumerate((first, second)):
        aux[row : row + 1, 0:LANES] = (ids[...] - base).astype(jnp.float32)
    aux[0:STATIONS_DEV, LANES : LANES + EV_DEV] = time[...]
    for q in range(3):
        lane = (2 + q) * LANES
        aux[0:STATIONS_DEV, lane : lane + EV_DEV] = slowness[q]
    aux[0:STATIONS_DEV, 5 * LANES : 6 * LANES] = lag[...].astype(jnp.float32)
    copies[0].wait()


def first_windows(own_ref, high_ref, low_ref, items):
    for item in items:
        window = own_ref[item, :, QUARTER : QUARTER + WINDOW]
        power = jnp.sum(window * window, axis=1, keepdims=True)
        window = window * lax.rsqrt(power + eps_small)
        padded = jnp.concatenate([window, jnp.zeros((EV_DEV, LANES), jnp.float32)], axis=1)
        at = item - items[0]
        for event in range(EV_DEV):
            wide = jnp.broadcast_to(padded[event : event + 1], (LAGS, SPAN))
            wide = pltpu.roll(wide, 0, 1, stride=1, stride_axis=0)
            high, low = split_bf16(wide)
            high_ref[at, pl.ds(event * LAGS, LAGS), :] = high
            low_ref[at, pl.ds(event * LAGS, LAGS), :] = low


def first_kernel(
    live_ref, own_ref, high_ref, low_ref, places_ref, pick_ref, rates_ref
):
    aux = own_ref[TRACES_DEV]
    first = aux[0:1, 0:LANES].astype(jnp.int32)
    second = aux[1:2, 0:LANES].astype(jnp.int32)
    begin = aux[0:STATIONS_DEV, 5 * LANES : 6 * LANES].astype(jnp.int32) + (QUARTER - LAGS // 2)
    side = lax.shift_right_arithmetic(second, 3)
    mate_side = 2 - 2 * lax.axis_index("c")
    away = jnp.logical_and(side != 1, side != mate_side)
    part = jnp.where(side == 1, 0, jnp.where(away, 2, 1))
    alive = lax.broadcasted_iota(jnp.int32, (1, PAIR_DEV), 1) < live_ref[0]
    far = jnp.logical_and(away, alive)
    event = jnp.bitwise_and(second, EV_DEV - 1)
    rows = part * PART_ROWS + event * CHUNKS + lax.shift_right_arithmetic(begin, 7)
    near = jnp.logical_and(jnp.logical_not(away), alive)
    upper = lax.broadcasted_iota(jnp.int32, (PAIR_DEV, PAIR_DEV), 0)
    lower = lax.broadcasted_iota(jnp.int32, (PAIR_DEV, PAIR_DEV), 1)
    lane_ids = lower[0:1]
    ahead = (upper <= lower).astype(jnp.bfloat16)
    slots = lax.broadcasted_iota(jnp.int32, (ROWS, PAIR_DEV), 1).astype(jnp.bfloat16)
    hots, counts, listed = [], [], []
    for marked in (far, near):
        ones = marked.astype(jnp.float32)
        wide = jnp.broadcast_to(ones, (ROWS, PAIR_DEV)).astype(jnp.bfloat16)
        place = jnp.where(marked, dot_bf16(wide, ahead, NN)[0:1] - 1.0, -1.0)
        hots.append((upper.astype(jnp.float32) == place).astype(jnp.bfloat16))
        counts.append(jnp.sum(ones, axis=1, keepdims=True).astype(jnp.int32))
    for hot in hots:
        listed.append(dot_bf16(slots, hot, NT)[0:1])
    places_ref[...] = jnp.zeros((PLACE_ROWS, PAIR_DEV), jnp.int32)
    places_ref[0:3, :] = rows
    places_ref[3:6, :] = jnp.bitwise_and(begin, LANES - 1)
    for at in range(2):
        filled = jnp.where(lane_ids < counts[at], listed[at], listed[at][:, 0:1])
        places_ref[6 + at : 7 + at, :] = filled.astype(jnp.int32)
        places_ref[8 + at : 9 + at, :] = jnp.broadcast_to(counts[at], (1, PAIR_DEV))
    places_ref[10:11, :] = jnp.broadcast_to(live_ref[0], (1, PAIR_DEV))
    first_windows(own_ref, high_ref, low_ref, range(FIRST_ITEMS))
    ends = jnp.bitwise_and(first, EV_DEV - 1).astype(jnp.float32)
    column = jnp.transpose(jnp.broadcast_to(ends, (LANES, PAIR_DEV)))
    groups = lax.broadcasted_iota(jnp.int32, (PAIR_DEV, LANES), 1) // LAGS
    for half in range(2):
        mine = column == (groups + half * (LANES // LAGS)).astype(jnp.float32)
        pick_ref[:, half * LANES : (half + 1) * LANES] = mine.astype(jnp.float32)
    rates_ref[...] = jnp.zeros((1, PAYLOAD), jnp.float32)
    for station in range(STATIONS_DEV):
        for q in range(3):
            lane = (2 + q) * LANES
            own = aux[station : station + 1, lane : lane + EV_DEV]
            for group in range(4):
                at = rate_place(group, station, q)
                rates_ref[:, at : at + EV_DEV] = jnp.where(
                    lax.axis_index("x") == group, own, 0.0
                )


def fill_table(ref, table_ref, part):
    for item in range(TRACES_DEV):
        values = ref[item]
        power = jnp.sum(values * values, axis=1, keepdims=True)
        values = values * lax.rsqrt(power + eps_small)
        for chunk in range(CHUNKS):
            start = part * PART_ROWS + item * EV_DEV * CHUNKS + chunk
            table_ref[pl.ds(start, EV_DEV, stride=CHUNKS), :] = values[
                :, chunk * LANES : (chunk + 1) * LANES
            ]


def align(places_ref, table_ref, moved_ref, slot, offset):
    lane_ids = lax.broadcasted_iota(jnp.int32, (ROWS, LANES), 1)
    for station in range(STATIONS_DEV):
        row = places_ref[station, slot] - offset
        lane = places_ref[3 + station, slot]
        turn = jnp.bitwise_and(-lane, LANES - 1)
        keep = lane_ids >= lane
        for component in range(3):
            item = station * 3 + component
            at = item * EV_DEV * CHUNKS
            here = table_ref[pl.ds(row + at, ROWS), :]
            after = table_ref[pl.ds(row + (at + 1), ROWS), :]
            moved = pltpu.roll(jnp.where(keep, here, after), turn, 1)
            to = pl.multiple_of((item * PAIR_DEV + slot) * ROWS, ROWS)
            moved_ref[pl.ds(to, ROWS), :] = moved


def groups_of(count):
    return lax.div(count + (GROUP - 1), GROUP)


def early_kernel(
    listed_ref, chip_ref, moved_ref, places_ref, high_ref, low_ref, table_ref, sem
):
    fetch = pltpu.make_async_copy(listed_ref, places_ref, sem)
    fetch.start()
    table_ref[pl.ds(2 * PART_ROWS, 2 * ROWS), :] = jnp.zeros((2 * ROWS, LANES), jnp.float32)
    core = lax.axis_index("c")
    first_windows(chip_ref.at[core], high_ref, low_ref, range(FIRST_ITEMS, TRACES_DEV))
    fill_table(chip_ref.at[core], table_ref, 0)
    fill_table(chip_ref.at[1 - core], table_ref, 1)
    fetch.wait()

    def step(index, carry):
        for turn in range(GROUP):
            align(places_ref, table_ref, moved_ref, places_ref[7, index * GROUP + turn], 0)
        return carry

    lax.fori_loop(0, groups_of(places_ref[9, 0]), step, 0)


def incidence(aux):
    events = lax.broadcasted_iota(jnp.int32, (NEAR, PAIR_DEV), 0).astype(jnp.float32)
    starts = (events == aux[0:1, 0:LANES]).astype(jnp.float32)
    return starts - (events == aux[1:2, 0:LANES]).astype(jnp.float32)


def near_block(left, own, right, part):
    lane = part * LANES
    return jnp.concatenate(
        [aux[0:STATIONS_DEV, lane : lane + EV_DEV] for aux in (left, own, right)], axis=1
    )


def late_kernel(
    places_ref,
    moved_in_ref,
    chip_ref,
    cross_ref,
    high_ref,
    low_ref,
    last_high_ref,
    last_low_ref,
    pick_ref,
    rates_ref,
    shift_ref,
    block_ref,
    moved_ref,
    table_ref,
):
    del moved_in_ref
    table_ref[pl.ds(PART_ROWS, 2 * ROWS), :] = jnp.zeros((2 * ROWS, LANES), jnp.float32)
    fill_table(cross_ref, table_ref, 0)

    def step(index, carry):
        for turn in range(GROUP):
            slot = places_ref[6, index * GROUP + turn]
            align(places_ref, table_ref, moved_ref, slot, 2 * PART_ROWS)
        return carry

    lax.fori_loop(0, groups_of(places_ref[8, 0]), step, 0)

    core = lax.axis_index("c")
    aux_own = chip_ref[core, TRACES_DEV]
    aux_left = jnp.where(core == 0, cross_ref[TRACES_DEV], chip_ref[0, TRACES_DEV])
    aux_right = jnp.where(core == 0, chip_ref[1, TRACES_DEV], cross_ref[TRACES_DEV])

    lane_ids = lax.broadcasted_iota(jnp.int32, (1, LANES), 1)
    centred = (lane_ids - LAGS // 2).astype(jnp.float32)
    weights = jnp.where(lane_ids < LAGS, centred, jnp.where(lane_ids < 2 * LAGS, 1.0, 0.0))
    folded = []
    for station in range(STATIONS_DEV):
        energy = jnp.zeros((PAIR_DEV, EV_DEV * LAGS), jnp.float32)
        for component in range(3):
            item = station * 3 + component
            pieces = [
                moved_ref[pl.ds(item * PAIR_DEV * ROWS + chunk, PAIR_DEV, stride=ROWS), :]
                for chunk in range(SPAN_CHUNKS)
            ]
            high, low = split_bf16(jnp.concatenate(pieces, axis=1))
            if item < FIRST_ITEMS:
                first_high, first_low = high_ref[item], low_ref[item]
            else:
                first_high = last_high_ref[item - FIRST_ITEMS]
                first_low = last_low_ref[item - FIRST_ITEMS]
            both = dot_bf16(jnp.concatenate([high, low], axis=0), first_high, NT)
            xcorr = both[0:PAIR_DEV] + both[PAIR_DEV:] + dot_bf16(high, first_low, NT)
            energy = energy + xcorr * xcorr
        energy = energy * pick_ref[...]
        energy = energy[:, 0:LANES] + energy[:, LANES:]
        energy = energy + pltpu.roll(energy, LANES // 2, 1)
        energy = energy + pltpu.roll(energy, LANES // 4, 1)
        folded.append(energy)
    pair = folded[0] * weights + folded[1] * pltpu.roll(weights, LANES // 2, 1)
    tables = [jnp.transpose(pair), jnp.transpose(folded[2] * weights)]
    station_shift = []
    for station in range(STATIONS_DEV):
        rows = tables[station // 2][(station % 2) * 2 * LAGS : (station % 2 + 1) * 2 * LAGS]
        above = jnp.sum(rows[0:LAGS], axis=0, keepdims=True)
        below = jnp.sum(rows[LAGS:], axis=0, keepdims=True)
        station_shift.append(above / (below + eps_small))
    alive = lax.broadcasted_iota(jnp.int32, (1, PAIR_DEV), 1) < places_ref[10, 0]
    shift = jnp.where(alive, jnp.concatenate(station_shift, axis=0), 0.0)
    shift_ref[...] = shift

    signs = jnp.where(alive, incidence(aux_own), 0.0).astype(jnp.bfloat16)
    times = dot_signs(near_block(aux_left, aux_own, aux_right, 1), signs, NN)
    lags = aux_own[0:STATIONS_DEV, 5 * LANES : 6 * LANES]
    rhs = jnp.where(alive, sample_step * (lags + shift), 0.0) - times
    per_event = dot_signs(rhs, signs, NT)
    counts = dot_bf16(signs[EV_DEV : 2 * EV_DEV], signs, NT)
    counts = jnp.where(lax.axis_index("x") == 0, counts, 0.0)
    block_ref[...] = rates_ref[...]
    for event in range(EV_DEV):
        at = count_place(event)
        block_ref[:, at : at + NEAR] = counts[event : event + 1]
    for q in range(4):
        terms = per_event
        if q < 3:
            terms = terms * near_block(aux_left, aux_own, aux_right, 2 + q)
        block_ref[:, q * NEAR : (q + 1) * NEAR] = jnp.sum(terms, axis=0, keepdims=True)
    total = jnp.sum(jnp.sum(rhs * rhs, axis=1, keepdims=True), axis=0, keepdims=True)
    block_ref[:, SQUARE_AT : SQUARE_AT + 1] = total


def symmetric(counts, turned_ref):
    for side, block in ((0, 0), (2, 1)):
        for a in range(EV_DEV):
            at = block * EV_DEV * EV_DEV + a
            turned_ref[pl.ds(at, EV_DEV, stride=EV_DEV), :] = counts[a][side]
    lower = sum(counts[a][0] for a in range(1, EV_DEV)) + counts[0][0]
    upper = sum(counts[a][2] for a in range(1, EV_DEV)) + counts[0][2]
    ends = pltpu.roll(upper, 1, 1) + pltpu.roll(lower, LANES - 1, 1)
    rows = lax.broadcasted_iota(jnp.int32, (EV_DEV, LANES), 0)
    result = []
    for a in range(EV_DEV):
        to_lower = turned_ref[pl.ds(a * EV_DEV, EV_DEV), :]
        to_upper = turned_ref[pl.ds((EV_DEV + a) * EV_DEV, EV_DEV), :]
        result.append(
            [
                counts[a][0] + pltpu.roll(to_upper, 1, 1),
                counts[a][1] - jnp.where(rows == a, ends, 0.0),
                counts[a][2] + pltpu.roll(to_lower, LANES - 1, 1),
            ]
        )
    return result


def solve_kernel(gathered_ref, shift_ref, out_ref, shift_out_ref, rows_ref, turned_ref):
    shift_out_ref[...] = shift_ref[...]
    half = LANES // 2
    tables = []
    for row in range(PAYLOAD // LANES):
        for core in range(2):
            values = gathered_ref[pl.ds(core * half, half), row * LANES : (row + 1) * LANES]
            rows_ref[pl.ds(row * LANES + core, half, stride=2), :] = values
        tables.append(jnp.transpose(rows_ref[pl.ds(row * LANES, LANES), :]))

    def read(at):
        return tables[at // LANES][at % LANES : at % LANES + 8]

    def along(lower, own, upper):
        return own + pltpu.roll(upper, 1, 1) + pltpu.roll(lower, LANES - 1, 1)

    back = [along(*[read(q * NEAR + 8 * side) for side in range(3)]) for q in range(4)]
    counts = symmetric(
        [[read(count_place(a) + 8 * side) for side in range(3)] for a in range(EV_DEV)], turned_ref
    )
    deriv = [
        [read(rate_place(group, station, q)) for q in range(3)]
        for group in range(4)
        for station in range(STATIONS_DEV)
    ]

    def total(values):
        return jnp.sum(jnp.sum(values, axis=1, keepdims=True), axis=0, keepdims=True)

    def inner(left, right):
        terms = left[0] * right[0]
        for q in range(1, 4):
            terms = terms + left[q] * right[q]
        return total(terms)

    def normal(model):
        result = [jnp.zeros((EV_DEV, LANES), jnp.float32) for _ in range(4)]
        for rates in deriv:
            data = model[3]
            for q in range(3):
                data = data + rates[q] * model[q]
            sides = [None, None, None]
            for a in range(EV_DEV):
                row = jnp.broadcast_to(data[a : a + 1], (EV_DEV, LANES))
                for side in range(3):
                    term = counts[a][side] * row
                    sides[side] = term if a == 0 else sides[side] + term
            mixed = along(*sides)
            for q in range(3):
                result[q] = result[q] + rates[q] * mixed
            result[3] = result[3] + mixed
        return result

    rhs_square = total(tables[0][SQUARE_AT : SQUARE_AT + 1])
    beta = jnp.sqrt(rhs_square + eps_small)
    unit_square = rhs_square / (beta * beta)
    adjoint = [value / beta for value in back]
    alpha = jnp.sqrt(inner(adjoint, adjoint) + eps_small)
    model = [value / alpha for value in adjoint]
    search = model
    location = [jnp.zeros((EV_DEV, LANES), jnp.float32) for _ in range(4)]
    phi_bar = beta
    rho_bar = alpha
    for turn in range(2):
        normal_model = normal(model)
        square = inner(model, normal_model) - 2.0 * alpha * inner(model, adjoint)
        square = jnp.maximum(square + alpha * alpha * unit_square, 0.0)
        beta = jnp.sqrt(square + eps_small)
        rho = jnp.sqrt(rho_bar * rho_bar + beta * beta)
        cosine = rho_bar / rho
        sine = beta / rho
        phi = cosine * phi_bar
        phi_bar = sine * phi_bar
        step = phi / rho
        location = [location[q] + step * search[q] for q in range(4)]
        if turn == 0:
            unit_square = square / (beta * beta)
            adjoint = [(normal_model[q] - alpha * adjoint[q]) / beta for q in range(4)]
            vector = [adjoint[q] - beta * model[q] for q in range(4)]
            alpha = jnp.sqrt(inner(vector, vector) + eps_small)
            model = [value / alpha for value in vector]
            theta = sine * alpha
            rho_bar = -cosine * alpha
            search = [model[q] - theta / rho * search[q] for q in range(4)]

    lanes = lax.broadcasted_iota(jnp.int32, (ROWS, LANES), 1)
    mine = (lanes == device_index()).astype(jnp.float32)
    parts = dot_bf16(mine.astype(jnp.bfloat16), thirds(jnp.concatenate(location, axis=0)), NT)
    rows = 4 * EV_DEV
    own = parts[:, 0:rows] + parts[:, rows : 2 * rows] + parts[:, 2 * rows :]
    for q in range(4):
        out_ref[q : q + 1, :] = own[0:1, q * EV_DEV : (q + 1) * EV_DEV]


def from_other_chip(block):
    count = lax.axis_size("g") * lax.axis_size("c")
    partners = [(i, i - 1 + 2 * (i % 2)) for i in range(count)]
    route = [(i, other) for i, other in partners if 0 <= other < count]
    return lax.ppermute(block, ("g", "c"), route)


def spread(row, axis):
    copies = jnp.broadcast_to(row, (lax.axis_size(axis), row.shape[1]))
    return lax.all_to_all(copies, axis, 0, 0, tiled=True)


VMEM = pl.BlockSpec(memory_space=pltpu.VMEM)
SMEM = pl.BlockSpec(memory_space=pltpu.SMEM)
HBM = pl.BlockSpec(memory_space=pltpu.HBM)
PARAMS = pltpu.CompilerParams(vmem_limit_bytes=VMEM_BYTES)


def pack(traces, ray_slowness, travel_time, pair_first, pair_second, pair_lag):
    arguments = (
        traces.reshape(TRACES_DEV, EV_DEV, LENGTH),
        ray_slowness,
        travel_time,
        pair_first.reshape(1, PAIR_DEV),
        pair_second.reshape(1, PAIR_DEV),
        pair_lag,
    )
    return pl.pallas_call(
        pack_kernel,
        out_shape=pltpu.VMEM((TRACES_DEV + 1, ROWS, LENGTH), jnp.float32),
        in_specs=[HBM] * 6,
        out_specs=VMEM,
        scratch_shapes=[
            pltpu.VMEM((3, STATIONS_DEV, EV_DEV), jnp.float32),
            pltpu.VMEM((STATIONS_DEV, EV_DEV), jnp.float32),
            pltpu.VMEM((1, PAIR_DEV), jnp.int32),
            pltpu.VMEM((1, PAIR_DEV), jnp.int32),
            pltpu.VMEM((STATIONS_DEV, PAIR_DEV), jnp.int32),
            pltpu.SemaphoreType.DMA((6,)),
        ],
        compiler_params=PARAMS,
        name="pack",
    )(*[pltpu.with_memory_space_constraint(value, pltpu.HBM) for value in arguments])


def firsts(pair_live, message):
    toeplitz = jax.ShapeDtypeStruct((FIRST_ITEMS, EV_DEV * LAGS, SPAN), jnp.bfloat16)
    return pl.pallas_call(
        first_kernel,
        out_shape=(
            toeplitz,
            toeplitz,
            jax.ShapeDtypeStruct((PLACE_ROWS, PAIR_DEV), jnp.int32),
            jax.ShapeDtypeStruct((PAIR_DEV, EV_DEV * LAGS), jnp.float32),
            jax.ShapeDtypeStruct((1, PAYLOAD), jnp.float32),
        ),
        in_specs=[SMEM, VMEM],
        out_specs=(VMEM,) * 5,
        compiler_params=PARAMS,
        name="firsts",
    )(pair_live, message)


MOVED = jax.ShapeDtypeStruct((TRACES_DEV * PAIR_DEV * ROWS + ROWS, LANES), jnp.float32)


def early(places, chip):
    toeplitz = jax.ShapeDtypeStruct(
        (TRACES_DEV - FIRST_ITEMS, EV_DEV * LAGS, SPAN), jnp.bfloat16
    )
    return pl.pallas_call(
        early_kernel,
        out_shape=(MOVED, pltpu.SMEM((PLACE_ROWS, PAIR_DEV), jnp.int32), toeplitz, toeplitz),
        in_specs=[VMEM, VMEM],
        out_specs=(VMEM, SMEM, VMEM, VMEM),
        scratch_shapes=[
            pltpu.VMEM((2 * PART_ROWS + 2 * ROWS, LANES), jnp.float32),
            pltpu.SemaphoreType.DMA,
        ],
        compiler_params=PARAMS,
        name="early",
    )(places, chip)


def late(places, moved, chip, from_cross, toeplitz, pick, rates):
    refined_shift, block, _ = pl.pallas_call(
        late_kernel,
        out_shape=(
            jax.ShapeDtypeStruct((STATIONS_DEV, PAIR_DEV), jnp.float32),
            jax.ShapeDtypeStruct((1, PAYLOAD), jnp.float32),
            MOVED,
        ),
        in_specs=[SMEM] + [VMEM] * 9,
        out_specs=(VMEM, VMEM, VMEM),
        scratch_shapes=[pltpu.VMEM((PART_ROWS + 2 * ROWS, LANES), jnp.float32)],
        input_output_aliases={1: 2},
        compiler_params=PARAMS,
        name="late",
    )(places, moved, chip, from_cross, *toeplitz, pick, rates)
    return refined_shift, block


def solve(gathered, shift):
    return pl.pallas_call(
        solve_kernel,
        out_shape=(
            jax.ShapeDtypeStruct((4, EV_DEV), jnp.float32),
            jax.ShapeDtypeStruct((STATIONS_DEV, PAIR_DEV), jnp.float32),
        ),
        in_specs=[VMEM, VMEM],
        out_specs=(VMEM, VMEM),
        scratch_shapes=[
            pltpu.VMEM((PAYLOAD + ROWS, LANES), jnp.float32),
            pltpu.VMEM((2 * EV_DEV * EV_DEV + ROWS, LANES), jnp.float32),
        ],
        compiler_params=PARAMS,
        name="solve",
    )(gathered, shift)


def body(traces, ray_slowness, travel_time, pair_first, pair_second, pair_lag, pair_live):
    message = pack(traces, ray_slowness, travel_time, pair_first, pair_second, pair_lag)
    from_cross = from_other_chip(message)
    pair_live = lax.optimization_barrier((message, pair_live))[1]
    high, low, places, pick, rates = firsts(pair_live, message)
    chip = lax.all_gather(message, "c", axis=0)
    moved, places, last_high, last_low = early(places, chip)
    places = pltpu.with_memory_space_constraint(places, pltpu.SMEM)
    toeplitz = (high, low, last_high, last_low)
    shift, block = late(places, moved, chip, from_cross, toeplitz, pick, rates)
    block = jnp.sum(spread(block, "x"), axis=0, keepdims=True)
    chips = lax.axis_size("g")
    gathered = lax.all_gather(spread(block, "g"), "c", axis=0)
    location, refined_shift = solve(gathered.reshape(2 * chips, PAYLOAD), shift)
    return refined_shift, location


def solution(mesh):
    ev, st = mesh.devices.shape
    fine = Mesh(mesh.devices.reshape(ev // 2, 2, st), ("g", "c", "x"))
    event_axes = ("g", "c")
    in_specs = (
        P("x", None, event_axes, None),
        P(None, "x", event_axes),
        P("x", event_axes),
        P(event_axes),
        P(event_axes),
        P("x", event_axes),
        P(event_axes),
    )
    out_specs = (P("x", event_axes), P(None, event_axes))
    return jax.shard_map(body, mesh=fine, in_specs=in_specs, out_specs=out_specs, check_vma=False)
```

```python
import jax
import jax.numpy as jnp
from jax import lax
from jax.experimental import pallas as pl
from jax.experimental.pallas import tpu as pltpu
from jax.sharding import Mesh
from jax.sharding import PartitionSpec as P

LAGS = 32
LANES = 128
ROWS = 8
EV_DEV = 8
NEAR = 3 * EV_DEV
STATIONS_DEV = 3
TRACES_DEV = 9
LENGTH = 1024
CHUNKS = LENGTH // LANES
QUARTER = LENGTH // 4
WINDOW = LENGTH // 2
SPAN = WINDOW + LANES
SPAN_CHUNKS = SPAN // LANES
PAIR_DEV = 128
PART_ROWS = TRACES_DEV * EV_DEV * CHUNKS
VMEM_BYTES = 24 * 1024 * 1024
PLACE_ROWS = 16
FIRST_ITEMS = 3
TILES = TRACES_DEV * CHUNKS + 1
AUX = TILES - 1
GROUP = 16
PAYLOAD = 5 * LANES
SQUARE_AT = 4 * NEAR

eps_small = 1e-06
sample_step = 0.01
NT = (((1,), (1,)), ((), ()))
NN = (((1,), (0,)), ((), ()))


def device_index():
    return lax.axis_index("g") * 2 + lax.axis_index("c")


def dot_bf16(left, right, dims):
    return lax.dot_general(left, right, dims, preferred_element_type=jnp.float32)


def count_place(event):
    return LANES + NEAR * event if event < 5 else 2 * LANES + NEAR * (event - 5)


def rate_place(group, station, q):
    index = (group * STATIONS_DEV + station) * 3 + q
    return 3 * LANES + 8 * index if index < 32 else 2 * LANES + 96 + 8 * (index - 32)


def rounded(values):
    return values.astype(jnp.bfloat16).astype(jnp.float32)


def thirds(values):
    high = rounded(values)
    middle = rounded(values - high)
    low = values - high - middle
    return jnp.concatenate([high, middle, low], axis=0).astype(jnp.bfloat16)


def dot_signs(left, signs, dims):
    rows = left.shape[0]
    parts = dot_bf16(thirds(left), signs, dims)
    return parts[0:rows] + parts[rows : 2 * rows] + parts[2 * rows :]


def split_bf16(values):
    high = values.astype(jnp.bfloat16)
    low = (values - high.astype(jnp.float32)).astype(jnp.bfloat16)
    return high, low


def pack_kernel(
    traces_ref,
    slowness_ref,
    time_ref,
    first_ref,
    second_ref,
    lag_ref,
    out_ref,
    slowness,
    time,
    first,
    second,
    lag,
    sems,
):
    pairs = [
        (traces_ref, out_ref.at[pl.ds(0, AUX)]),
        (slowness_ref, slowness),
        (time_ref, time),
        (first_ref, first),
        (second_ref, second),
        (lag_ref, lag),
    ]
    copies = [
        pltpu.make_async_copy(source, target, sems.at[at])
        for at, (source, target) in enumerate(pairs)
    ]
    for copy in copies:
        copy.start()
    aux = out_ref.at[AUX]
    aux[...] = jnp.zeros((ROWS, LANES), jnp.float32)
    for copy in copies[1:]:
        copy.wait()
    base = device_index() * EV_DEV - EV_DEV
    aux[0:STATIONS_DEV, 0:EV_DEV] = time[...]
    for q in range(3):
        lane = (1 + q) * EV_DEV
        aux[0:STATIONS_DEV, lane : lane + EV_DEV] = slowness[q]
    for row, ids in enumerate((first, second)):
        aux[3 + row : 4 + row, :] = (ids[...] - base).astype(jnp.float32)
    aux[5:8, :] = lag[...].astype(jnp.float32)
    copies[0].wait()


def first_windows(own_ref, high_ref, low_ref, items):
    for item in items:
        tiles = [own_ref[item * CHUNKS + chunk] for chunk in range(2, 6)]
        window = jnp.concatenate(tiles, axis=1)
        power = jnp.sum(window * window, axis=1, keepdims=True)
        window = window * lax.rsqrt(power + eps_small)
        padded = jnp.concatenate([window, jnp.zeros((EV_DEV, LANES), jnp.float32)], axis=1)
        at = item - items[0]
        for event in range(EV_DEV):
            wide = jnp.broadcast_to(padded[event : event + 1], (LAGS, SPAN))
            wide = pltpu.roll(wide, 0, 1, stride=1, stride_axis=0)
            high, low = split_bf16(wide)
            high_ref[at, pl.ds(event * LAGS, LAGS), :] = high
            low_ref[at, pl.ds(event * LAGS, LAGS), :] = low


def first_kernel(
    live_ref, own_ref, high_ref, low_ref, places_ref, pick_ref, rates_ref
):
    aux = own_ref[AUX]
    first = aux[3:4].astype(jnp.int32)
    second = aux[4:5].astype(jnp.int32)
    begin = aux[5:8].astype(jnp.int32) + (QUARTER - LAGS // 2)
    side = lax.shift_right_arithmetic(second, 3)
    mate_side = 2 - 2 * lax.axis_index("c")
    away = jnp.logical_and(side != 1, side != mate_side)
    part = jnp.where(side == 1, 0, jnp.where(away, 2, 1))
    alive = lax.broadcasted_iota(jnp.int32, (1, PAIR_DEV), 1) < live_ref[0]
    far = jnp.logical_and(away, alive)
    event = jnp.bitwise_and(second, EV_DEV - 1)
    rows = part * PART_ROWS + event * CHUNKS + lax.shift_right_arithmetic(begin, 7)
    near = jnp.logical_and(jnp.logical_not(away), alive)
    upper = lax.broadcasted_iota(jnp.int32, (PAIR_DEV, PAIR_DEV), 0)
    lower = lax.broadcasted_iota(jnp.int32, (PAIR_DEV, PAIR_DEV), 1)
    lane_ids = lower[0:1]
    ahead = (upper <= lower).astype(jnp.bfloat16)
    slots = lax.broadcasted_iota(jnp.int32, (ROWS, PAIR_DEV), 1).astype(jnp.bfloat16)
    hots, counts, listed = [], [], []
    for marked in (far, near):
        ones = marked.astype(jnp.float32)
        wide = jnp.broadcast_to(ones, (ROWS, PAIR_DEV)).astype(jnp.bfloat16)
        place = jnp.where(marked, dot_bf16(wide, ahead, NN)[0:1] - 1.0, -1.0)
        hots.append((upper.astype(jnp.float32) == place).astype(jnp.bfloat16))
        counts.append(jnp.sum(ones, axis=1, keepdims=True).astype(jnp.int32))
    for hot in hots:
        listed.append(dot_bf16(slots, hot, NT)[0:1])
    places_ref[...] = jnp.zeros((PLACE_ROWS, PAIR_DEV), jnp.int32)
    places_ref[0:3, :] = rows
    places_ref[3:6, :] = jnp.bitwise_and(begin, LANES - 1)
    for at in range(2):
        filled = jnp.where(lane_ids < counts[at], listed[at], listed[at][:, 0:1])
        places_ref[6 + at : 7 + at, :] = filled.astype(jnp.int32)
        places_ref[8 + at : 9 + at, :] = jnp.broadcast_to(counts[at], (1, PAIR_DEV))
    places_ref[10:11, :] = jnp.broadcast_to(live_ref[0], (1, PAIR_DEV))
    first_windows(own_ref, high_ref, low_ref, range(FIRST_ITEMS))
    ends = jnp.bitwise_and(first, EV_DEV - 1).astype(jnp.float32)
    column = jnp.transpose(jnp.broadcast_to(ends, (LANES, PAIR_DEV)))
    groups = lax.broadcasted_iota(jnp.int32, (PAIR_DEV, LANES), 1) // LAGS
    for half in range(2):
        mine = column == (groups + half * (LANES // LAGS)).astype(jnp.float32)
        pick_ref[:, half * LANES : (half + 1) * LANES] = mine.astype(jnp.float32)
    rates_ref[...] = jnp.zeros((1, PAYLOAD), jnp.float32)
    for station in range(STATIONS_DEV):
        for q in range(3):
            lane = (1 + q) * EV_DEV
            own = aux[station : station + 1, lane : lane + EV_DEV]
            for group in range(4):
                at = rate_place(group, station, q)
                rates_ref[:, at : at + EV_DEV] = jnp.where(
                    lax.axis_index("x") == group, own, 0.0
                )


def fill_table(ref, table_ref, part):
    for item in range(TRACES_DEV):
        tiles = [ref[item * CHUNKS + chunk] for chunk in range(CHUNKS)]
        squares = tiles[0] * tiles[0]
        for tile in tiles[1:]:
            squares = squares + tile * tile
        scale = lax.rsqrt(jnp.sum(squares, axis=1, keepdims=True) + eps_small)
        for chunk in range(CHUNKS):
            start = part * PART_ROWS + item * EV_DEV * CHUNKS + chunk
            table_ref[pl.ds(start, EV_DEV, stride=CHUNKS), :] = tiles[chunk] * scale


def align(places_ref, table_ref, moved_ref, slot, offset):
    lane_ids = lax.broadcasted_iota(jnp.int32, (ROWS, LANES), 1)
    for station in range(STATIONS_DEV):
        row = places_ref[station, slot] - offset
        lane = places_ref[3 + station, slot]
        turn = jnp.bitwise_and(-lane, LANES - 1)
        keep = lane_ids >= lane
        for component in range(3):
            item = station * 3 + component
            at = item * EV_DEV * CHUNKS
            here = table_ref[pl.ds(row + at, ROWS), :]
            after = table_ref[pl.ds(row + (at + 1), ROWS), :]
            moved = pltpu.roll(jnp.where(keep, here, after), turn, 1)
            to = pl.multiple_of((item * PAIR_DEV + slot) * ROWS, ROWS)
            moved_ref[pl.ds(to, ROWS), :] = moved


def groups_of(count):
    return lax.div(count + (GROUP - 1), GROUP)


def early_kernel(
    listed_ref, chip_ref, moved_ref, places_ref, high_ref, low_ref, table_ref, sem
):
    fetch = pltpu.make_async_copy(listed_ref, places_ref, sem)
    fetch.start()
    table_ref[pl.ds(2 * PART_ROWS, 2 * ROWS), :] = jnp.zeros((2 * ROWS, LANES), jnp.float32)
    core = lax.axis_index("c")
    first_windows(chip_ref.at[core], high_ref, low_ref, range(FIRST_ITEMS, TRACES_DEV))
    fill_table(chip_ref.at[core], table_ref, 0)
    fill_table(chip_ref.at[1 - core], table_ref, 1)
    fetch.wait()

    def step(index, carry):
        for turn in range(GROUP):
            align(places_ref, table_ref, moved_ref, places_ref[7, index * GROUP + turn], 0)
        return carry

    lax.fori_loop(0, groups_of(places_ref[9, 0]), step, 0)


def incidence(aux):
    events = lax.broadcasted_iota(jnp.int32, (NEAR, PAIR_DEV), 0).astype(jnp.float32)
    starts = (events == aux[3:4]).astype(jnp.float32)
    return starts - (events == aux[4:5]).astype(jnp.float32)


def near_block(left, own, right, part):
    lane = part * EV_DEV
    return jnp.concatenate(
        [aux[0:STATIONS_DEV, lane : lane + EV_DEV] for aux in (left, own, right)], axis=1
    )


def late_kernel(
    places_ref,
    moved_in_ref,
    chip_ref,
    cross_ref,
    high_ref,
    low_ref,
    last_high_ref,
    last_low_ref,
    pick_ref,
    rates_ref,
    shift_ref,
    block_ref,
    moved_ref,
    table_ref,
):
    del moved_in_ref
    table_ref[pl.ds(PART_ROWS, 2 * ROWS), :] = jnp.zeros((2 * ROWS, LANES), jnp.float32)
    fill_table(cross_ref, table_ref, 0)

    def step(index, carry):
        for turn in range(GROUP):
            slot = places_ref[6, index * GROUP + turn]
            align(places_ref, table_ref, moved_ref, slot, 2 * PART_ROWS)
        return carry

    lax.fori_loop(0, groups_of(places_ref[8, 0]), step, 0)

    core = lax.axis_index("c")
    aux_own = chip_ref[core, AUX]
    aux_left = jnp.where(core == 0, cross_ref[AUX], chip_ref[0, AUX])
    aux_right = jnp.where(core == 0, chip_ref[1, AUX], cross_ref[AUX])

    lane_ids = lax.broadcasted_iota(jnp.int32, (1, LANES), 1)
    centred = (lane_ids - LAGS // 2).astype(jnp.float32)
    weights = jnp.where(lane_ids < LAGS, centred, jnp.where(lane_ids < 2 * LAGS, 1.0, 0.0))
    folded = []
    for station in range(STATIONS_DEV):
        energy = jnp.zeros((PAIR_DEV, EV_DEV * LAGS), jnp.float32)
        for component in range(3):
            item = station * 3 + component
            pieces = [
                moved_ref[pl.ds(item * PAIR_DEV * ROWS + chunk, PAIR_DEV, stride=ROWS), :]
                for chunk in range(SPAN_CHUNKS)
            ]
            high, low = split_bf16(jnp.concatenate(pieces, axis=1))
            if item < FIRST_ITEMS:
                first_high, first_low = high_ref[item], low_ref[item]
            else:
                first_high = last_high_ref[item - FIRST_ITEMS]
                first_low = last_low_ref[item - FIRST_ITEMS]
            both = dot_bf16(jnp.concatenate([high, low], axis=0), first_high, NT)
            xcorr = both[0:PAIR_DEV] + both[PAIR_DEV:] + dot_bf16(high, first_low, NT)
            energy = energy + xcorr * xcorr
        energy = energy * pick_ref[...]
        energy = energy[:, 0:LANES] + energy[:, LANES:]
        energy = energy + pltpu.roll(energy, LANES // 2, 1)
        energy = energy + pltpu.roll(energy, LANES // 4, 1)
        folded.append(energy)
    pair = folded[0] * weights + folded[1] * pltpu.roll(weights, LANES // 2, 1)
    tables = [jnp.transpose(pair), jnp.transpose(folded[2] * weights)]
    station_shift = []
    for station in range(STATIONS_DEV):
        rows = tables[station // 2][(station % 2) * 2 * LAGS : (station % 2 + 1) * 2 * LAGS]
        above = jnp.sum(rows[0:LAGS], axis=0, keepdims=True)
        below = jnp.sum(rows[LAGS:], axis=0, keepdims=True)
        station_shift.append(above / (below + eps_small))
    alive = lax.broadcasted_iota(jnp.int32, (1, PAIR_DEV), 1) < places_ref[10, 0]
    shift = jnp.where(alive, jnp.concatenate(station_shift, axis=0), 0.0)
    shift_ref[...] = shift

    signs = jnp.where(alive, incidence(aux_own), 0.0)
    own_signs = signs[EV_DEV : 2 * EV_DEV].astype(jnp.bfloat16)
    signs = signs.astype(jnp.bfloat16)
    times = dot_signs(near_block(aux_left, aux_own, aux_right, 0), signs, NN)
    lags = aux_own[5:8]
    rhs = jnp.where(alive, sample_step * (lags + shift), 0.0) - times
    per_event = dot_signs(rhs, signs, NT)
    counts = dot_bf16(own_signs, signs, NT)
    counts = jnp.where(lax.axis_index("x") == 0, counts, 0.0)
    block_ref[...] = rates_ref[...]
    for event in range(EV_DEV):
        at = count_place(event)
        block_ref[:, at : at + NEAR] = counts[event : event + 1]
    for q in range(4):
        terms = per_event
        if q < 3:
            terms = terms * near_block(aux_left, aux_own, aux_right, 1 + q)
        block_ref[:, q * NEAR : (q + 1) * NEAR] = jnp.sum(terms, axis=0, keepdims=True)
    total = jnp.sum(jnp.sum(rhs * rhs, axis=1, keepdims=True), axis=0, keepdims=True)
    block_ref[:, SQUARE_AT : SQUARE_AT + 1] = total


def symmetric(counts, turned_ref):
    for side, block in ((0, 0), (2, 1)):
        for a in range(EV_DEV):
            at = block * EV_DEV * EV_DEV + a
            turned_ref[pl.ds(at, EV_DEV, stride=EV_DEV), :] = counts[a][side]
    lower = sum(counts[a][0] for a in range(1, EV_DEV)) + counts[0][0]
    upper = sum(counts[a][2] for a in range(1, EV_DEV)) + counts[0][2]
    ends = pltpu.roll(upper, 1, 1) + pltpu.roll(lower, LANES - 1, 1)
    rows = lax.broadcasted_iota(jnp.int32, (EV_DEV, LANES), 0)
    result = []
    for a in range(EV_DEV):
        to_lower = turned_ref[pl.ds(a * EV_DEV, EV_DEV), :]
        to_upper = turned_ref[pl.ds((EV_DEV + a) * EV_DEV, EV_DEV), :]
        result.append(
            [
                counts[a][0] + pltpu.roll(to_upper, 1, 1),
                counts[a][1] - jnp.where(rows == a, ends, 0.0),
                counts[a][2] + pltpu.roll(to_lower, LANES - 1, 1),
            ]
        )
    return result


def solve_kernel(gathered_ref, shift_ref, out_ref, shift_out_ref, rows_ref, turned_ref):
    shift_out_ref[...] = shift_ref[...]
    half = LANES // 2
    tables = []
    for row in range(PAYLOAD // LANES):
        for core in range(2):
            values = gathered_ref[pl.ds(core * half, half), row * LANES : (row + 1) * LANES]
            rows_ref[pl.ds(row * LANES + core, half, stride=2), :] = values
        tables.append(jnp.transpose(rows_ref[pl.ds(row * LANES, LANES), :]))

    def read(at):
        return tables[at // LANES][at % LANES : at % LANES + 8]

    def along(lower, own, upper):
        return own + pltpu.roll(upper, 1, 1) + pltpu.roll(lower, LANES - 1, 1)

    back = [along(*[read(q * NEAR + 8 * side) for side in range(3)]) for q in range(4)]
    counts = symmetric(
        [[read(count_place(a) + 8 * side) for side in range(3)] for a in range(EV_DEV)], turned_ref
    )
    deriv = [
        [read(rate_place(group, station, q)) for q in range(3)]
        for group in range(4)
        for station in range(STATIONS_DEV)
    ]

    def total(values):
        return jnp.sum(jnp.sum(values, axis=1, keepdims=True), axis=0, keepdims=True)

    def inner(left, right):
        terms = left[0] * right[0]
        for q in range(1, 4):
            terms = terms + left[q] * right[q]
        return total(terms)

    def normal(model):
        result = [jnp.zeros((EV_DEV, LANES), jnp.float32) for _ in range(4)]
        for rates in deriv:
            data = model[3]
            for q in range(3):
                data = data + rates[q] * model[q]
            sides = [None, None, None]
            for a in range(EV_DEV):
                row = jnp.broadcast_to(data[a : a + 1], (EV_DEV, LANES))
                for side in range(3):
                    term = counts[a][side] * row
                    sides[side] = term if a == 0 else sides[side] + term
            mixed = along(*sides)
            for q in range(3):
                result[q] = result[q] + rates[q] * mixed
            result[3] = result[3] + mixed
        return result

    rhs_square = total(tables[0][SQUARE_AT : SQUARE_AT + 1])
    beta = jnp.sqrt(rhs_square + eps_small)
    unit_square = rhs_square / (beta * beta)
    adjoint = [value / beta for value in back]
    alpha = jnp.sqrt(inner(adjoint, adjoint) + eps_small)
    model = [value / alpha for value in adjoint]
    search = model
    location = [jnp.zeros((EV_DEV, LANES), jnp.float32) for _ in range(4)]
    phi_bar = beta
    rho_bar = alpha
    for turn in range(2):
        normal_model = normal(model)
        square = inner(model, normal_model) - 2.0 * alpha * inner(model, adjoint)
        square = jnp.maximum(square + alpha * alpha * unit_square, 0.0)
        beta = jnp.sqrt(square + eps_small)
        rho = jnp.sqrt(rho_bar * rho_bar + beta * beta)
        cosine = rho_bar / rho
        sine = beta / rho
        phi = cosine * phi_bar
        phi_bar = sine * phi_bar
        step = phi / rho
        location = [location[q] + step * search[q] for q in range(4)]
        if turn == 0:
            unit_square = square / (beta * beta)
            adjoint = [(normal_model[q] - alpha * adjoint[q]) / beta for q in range(4)]
            vector = [adjoint[q] - beta * model[q] for q in range(4)]
            alpha = jnp.sqrt(inner(vector, vector) + eps_small)
            model = [value / alpha for value in vector]
            theta = sine * alpha
            rho_bar = -cosine * alpha
            search = [model[q] - theta / rho * search[q] for q in range(4)]

    lanes = lax.broadcasted_iota(jnp.int32, (ROWS, LANES), 1)
    mine = (lanes == device_index()).astype(jnp.float32)
    parts = dot_bf16(mine.astype(jnp.bfloat16), thirds(jnp.concatenate(location, axis=0)), NT)
    rows = 4 * EV_DEV
    own = parts[:, 0:rows] + parts[:, rows : 2 * rows] + parts[:, 2 * rows :]
    for q in range(4):
        out_ref[q : q + 1, :] = own[0:1, q * EV_DEV : (q + 1) * EV_DEV]


def from_other_chip(block):
    count = lax.axis_size("g") * lax.axis_size("c")
    partners = [(i, i - 1 + 2 * (i % 2)) for i in range(count)]
    route = [(i, other) for i, other in partners if 0 <= other < count]
    return lax.ppermute(block, ("g", "c"), route)


def spread(row, axis):
    copies = jnp.broadcast_to(row, (lax.axis_size(axis), row.shape[1]))
    return lax.all_to_all(copies, axis, 0, 0, tiled=True)


VMEM = pl.BlockSpec(memory_space=pltpu.VMEM)
SMEM = pl.BlockSpec(memory_space=pltpu.SMEM)
HBM = pl.BlockSpec(memory_space=pltpu.HBM)
PARAMS = pltpu.CompilerParams(vmem_limit_bytes=VMEM_BYTES)


def pack(traces, ray_slowness, travel_time, pair_first, pair_second, pair_lag):
    tiles = traces.reshape(TRACES_DEV, EV_DEV, CHUNKS, LANES).transpose(0, 2, 1, 3)
    arguments = (
        tiles.reshape(AUX, EV_DEV, LANES),
        ray_slowness,
        travel_time,
        pair_first.reshape(1, PAIR_DEV),
        pair_second.reshape(1, PAIR_DEV),
        pair_lag,
    )
    return pl.pallas_call(
        pack_kernel,
        out_shape=pltpu.VMEM((TILES, ROWS, LANES), jnp.float32),
        in_specs=[HBM] * 6,
        out_specs=VMEM,
        scratch_shapes=[
            pltpu.VMEM((3, STATIONS_DEV, EV_DEV), jnp.float32),
            pltpu.VMEM((STATIONS_DEV, EV_DEV), jnp.float32),
            pltpu.VMEM((1, PAIR_DEV), jnp.int32),
            pltpu.VMEM((1, PAIR_DEV), jnp.int32),
            pltpu.VMEM((STATIONS_DEV, PAIR_DEV), jnp.int32),
            pltpu.SemaphoreType.DMA((6,)),
        ],
        compiler_params=PARAMS,
        name="pack",
    )(*[pltpu.with_memory_space_constraint(value, pltpu.HBM) for value in arguments])


def firsts(pair_live, message):
    toeplitz = jax.ShapeDtypeStruct((FIRST_ITEMS, EV_DEV * LAGS, SPAN), jnp.bfloat16)
    return pl.pallas_call(
        first_kernel,
        out_shape=(
            toeplitz,
            toeplitz,
            jax.ShapeDtypeStruct((PLACE_ROWS, PAIR_DEV), jnp.int32),
            jax.ShapeDtypeStruct((PAIR_DEV, EV_DEV * LAGS), jnp.float32),
            jax.ShapeDtypeStruct((1, PAYLOAD), jnp.float32),
        ),
        in_specs=[SMEM, VMEM],
        out_specs=(VMEM,) * 5,
        compiler_params=PARAMS,
        name="firsts",
    )(pair_live, message)


MOVED = jax.ShapeDtypeStruct((TRACES_DEV * PAIR_DEV * ROWS + ROWS, LANES), jnp.float32)


def early(places, chip):
    toeplitz = jax.ShapeDtypeStruct(
        (TRACES_DEV - FIRST_ITEMS, EV_DEV * LAGS, SPAN), jnp.bfloat16
    )
    return pl.pallas_call(
        early_kernel,
        out_shape=(MOVED, pltpu.SMEM((PLACE_ROWS, PAIR_DEV), jnp.int32), toeplitz, toeplitz),
        in_specs=[VMEM, VMEM],
        out_specs=(VMEM, SMEM, VMEM, VMEM),
        scratch_shapes=[
            pltpu.VMEM((2 * PART_ROWS + 2 * ROWS, LANES), jnp.float32),
            pltpu.SemaphoreType.DMA,
        ],
        compiler_params=PARAMS,
        name="early",
    )(places, chip)


def late(places, moved, chip, from_cross, toeplitz, pick, rates):
    refined_shift, block, _ = pl.pallas_call(
        late_kernel,
        out_shape=(
            jax.ShapeDtypeStruct((STATIONS_DEV, PAIR_DEV), jnp.float32),
            jax.ShapeDtypeStruct((1, PAYLOAD), jnp.float32),
            MOVED,
        ),
        in_specs=[SMEM] + [VMEM] * 9,
        out_specs=(VMEM, VMEM, VMEM),
        scratch_shapes=[pltpu.VMEM((PART_ROWS + 2 * ROWS, LANES), jnp.float32)],
        input_output_aliases={1: 2},
        compiler_params=PARAMS,
        name="late",
    )(places, moved, chip, from_cross, *toeplitz, pick, rates)
    return refined_shift, block


def solve(gathered, shift):
    return pl.pallas_call(
        solve_kernel,
        out_shape=(
            jax.ShapeDtypeStruct((4, EV_DEV), jnp.float32),
            jax.ShapeDtypeStruct((STATIONS_DEV, PAIR_DEV), jnp.float32),
        ),
        in_specs=[VMEM, VMEM],
        out_specs=(VMEM, VMEM),
        scratch_shapes=[
            pltpu.VMEM((PAYLOAD + ROWS, LANES), jnp.float32),
            pltpu.VMEM((2 * EV_DEV * EV_DEV + ROWS, LANES), jnp.float32),
        ],
        compiler_params=PARAMS,
        name="solve",
    )(gathered, shift)


def body(traces, ray_slowness, travel_time, pair_first, pair_second, pair_lag, pair_live):
    message = pack(traces, ray_slowness, travel_time, pair_first, pair_second, pair_lag)
    from_cross = from_other_chip(message)
    pair_live = lax.optimization_barrier((message, pair_live))[1]
    high, low, places, pick, rates = firsts(pair_live, message)
    chip = lax.all_gather(message, "c", axis=0)
    moved, places, last_high, last_low = early(places, chip)
    places = pltpu.with_memory_space_constraint(places, pltpu.SMEM)
    toeplitz = (high, low, last_high, last_low)
    shift, block = late(places, moved, chip, from_cross, toeplitz, pick, rates)
    block = jnp.sum(spread(block, "x"), axis=0, keepdims=True)
    chips = lax.axis_size("g")
    gathered = lax.all_gather(spread(block, "g"), "c", axis=0)
    location, refined_shift = solve(gathered.reshape(2 * chips, PAYLOAD), shift)
    return refined_shift, location


def solution(mesh):
    ev, st = mesh.devices.shape
    fine = Mesh(mesh.devices.reshape(ev // 2, 2, st), ("g", "c", "x"))
    event_axes = ("g", "c")
    in_specs = (
        P("x", None, event_axes, None),
        P(None, "x", event_axes),
        P("x", event_axes),
        P(event_axes),
        P(event_axes),
        P("x", event_axes),
        P(event_axes),
    )
    out_specs = (P("x", event_axes), P(None, event_axes))
    return jax.shard_map(body, mesh=fine, in_specs=in_specs, out_specs=out_specs, check_vma=False)
```

```python
import jax
import jax.numpy as jnp
from jax import lax
from jax.experimental import pallas as pl
from jax.experimental.pallas import tpu as pltpu
from jax.sharding import Mesh
from jax.sharding import PartitionSpec as P

LAGS = 32
LANES = 128
ROWS = 8
EV_DEV = 8
NEAR = 3 * EV_DEV
STATIONS_DEV = 3
TRACES_DEV = 9
LENGTH = 1024
CHUNKS = LENGTH // LANES
QUARTER = LENGTH // 4
WINDOW = LENGTH // 2
SPAN = WINDOW + LANES
SPAN_CHUNKS = SPAN // LANES
PAIR_DEV = 128
PART_ROWS = TRACES_DEV * EV_DEV * CHUNKS
VMEM_BYTES = 24 * 1024 * 1024
PLACE_ROWS = 16
FIRST_ITEMS = 3
TILES = TRACES_DEV * CHUNKS + 1
AUX = TILES - 1
GROUP = 16
PAYLOAD = 5 * LANES
SQUARE_AT = 4 * NEAR

eps_small = 1e-06
sample_step = 0.01
NT = (((1,), (1,)), ((), ()))
NN = (((1,), (0,)), ((), ()))


def device_index():
    return lax.axis_index("g") * 2 + lax.axis_index("c")


def dot_bf16(left, right, dims):
    return lax.dot_general(left, right, dims, preferred_element_type=jnp.float32)


def count_place(event):
    return LANES + NEAR * event if event < 5 else 2 * LANES + NEAR * (event - 5)


def rate_place(group, station, q):
    index = (group * STATIONS_DEV + station) * 3 + q
    return 3 * LANES + 8 * index if index < 32 else 2 * LANES + 96 + 8 * (index - 32)


def rounded(values):
    return values.astype(jnp.bfloat16).astype(jnp.float32)


def thirds(values):
    high = rounded(values)
    middle = rounded(values - high)
    low = values - high - middle
    return jnp.concatenate([high, middle, low], axis=0).astype(jnp.bfloat16)


def dot_signs(left, signs, dims):
    rows = left.shape[0]
    parts = dot_bf16(thirds(left), signs, dims)
    return parts[0:rows] + parts[rows : 2 * rows] + parts[2 * rows :]


def split_bf16(values):
    high = values.astype(jnp.bfloat16)
    low = (values - high.astype(jnp.float32)).astype(jnp.bfloat16)
    return high, low


def pack_kernel(
    traces_ref,
    slowness_ref,
    time_ref,
    first_ref,
    second_ref,
    lag_ref,
    out_ref,
    slowness,
    time,
    first,
    second,
    lag,
    sems,
):
    pairs = [
        (traces_ref, out_ref.at[pl.ds(0, AUX)]),
        (slowness_ref, slowness),
        (time_ref, time),
        (first_ref, first),
        (second_ref, second),
        (lag_ref, lag),
    ]
    copies = [
        pltpu.make_async_copy(source, target, sems.at[at])
        for at, (source, target) in enumerate(pairs)
    ]
    for copy in copies:
        copy.start()
    aux = out_ref.at[AUX]
    aux[...] = jnp.zeros((ROWS, LANES), jnp.float32)
    for copy in copies[1:]:
        copy.wait()
    base = device_index() * EV_DEV - EV_DEV
    aux[0:STATIONS_DEV, 0:EV_DEV] = time[...]
    for q in range(3):
        lane = (1 + q) * EV_DEV
        aux[0:STATIONS_DEV, lane : lane + EV_DEV] = slowness[q]
    for row, ids in enumerate((first, second)):
        aux[3 + row : 4 + row, :] = (ids[...] - base).astype(jnp.float32)
    aux[5:8, :] = lag[...].astype(jnp.float32)
    copies[0].wait()


def first_windows(own_ref, high_ref, low_ref, items):
    for item in items:
        tiles = [own_ref[item * CHUNKS + chunk] for chunk in range(2, 6)]
        window = jnp.concatenate(tiles, axis=1)
        power = jnp.sum(window * window, axis=1, keepdims=True)
        window = window * lax.rsqrt(power + eps_small)
        padded = jnp.concatenate([window, jnp.zeros((EV_DEV, LANES), jnp.float32)], axis=1)
        at = item - items[0]
        for event in range(EV_DEV):
            wide = jnp.broadcast_to(padded[event : event + 1], (LAGS, SPAN))
            wide = pltpu.roll(wide, 0, 1, stride=1, stride_axis=0)
            high, low = split_bf16(wide)
            high_ref[at, pl.ds(event * LAGS, LAGS), :] = high
            low_ref[at, pl.ds(event * LAGS, LAGS), :] = low


def first_kernel(
    live_ref, own_ref, high_ref, low_ref, places_ref, pick_ref, rates_ref
):
    aux = own_ref[AUX]
    first = aux[3:4].astype(jnp.int32)
    second = aux[4:5].astype(jnp.int32)
    begin = aux[5:8].astype(jnp.int32) + (QUARTER - LAGS // 2)
    side = lax.shift_right_arithmetic(second, 3)
    mate_side = 2 - 2 * lax.axis_index("c")
    away = jnp.logical_and(side != 1, side != mate_side)
    part = jnp.where(side == 1, 0, jnp.where(away, 2, 1))
    alive = lax.broadcasted_iota(jnp.int32, (1, PAIR_DEV), 1) < live_ref[0]
    far = jnp.logical_and(away, alive)
    event = jnp.bitwise_and(second, EV_DEV - 1)
    rows = part * PART_ROWS + event * CHUNKS + lax.shift_right_arithmetic(begin, 7)
    near = jnp.logical_and(jnp.logical_not(away), alive)
    upper = lax.broadcasted_iota(jnp.int32, (PAIR_DEV, PAIR_DEV), 0)
    lower = lax.broadcasted_iota(jnp.int32, (PAIR_DEV, PAIR_DEV), 1)
    lane_ids = lower[0:1]
    ahead = (upper <= lower).astype(jnp.bfloat16)
    slots = lax.broadcasted_iota(jnp.int32, (ROWS, PAIR_DEV), 1).astype(jnp.bfloat16)
    hots, counts, listed = [], [], []
    for marked in (far, near):
        ones = marked.astype(jnp.float32)
        wide = jnp.broadcast_to(ones, (ROWS, PAIR_DEV)).astype(jnp.bfloat16)
        place = jnp.where(marked, dot_bf16(wide, ahead, NN)[0:1] - 1.0, -1.0)
        hots.append((upper.astype(jnp.float32) == place).astype(jnp.bfloat16))
        counts.append(jnp.sum(ones, axis=1, keepdims=True).astype(jnp.int32))
    for hot in hots:
        listed.append(dot_bf16(slots, hot, NT)[0:1])
    places_ref[...] = jnp.zeros((PLACE_ROWS, PAIR_DEV), jnp.int32)
    places_ref[0:3, :] = rows
    places_ref[3:6, :] = jnp.bitwise_and(begin, LANES - 1)
    for at in range(2):
        filled = jnp.where(lane_ids < counts[at], listed[at], listed[at][:, 0:1])
        places_ref[6 + at : 7 + at, :] = filled.astype(jnp.int32)
        places_ref[8 + at : 9 + at, :] = jnp.broadcast_to(counts[at], (1, PAIR_DEV))
    places_ref[10:11, :] = jnp.broadcast_to(live_ref[0], (1, PAIR_DEV))
    first_windows(own_ref, high_ref, low_ref, range(FIRST_ITEMS))
    ends = jnp.bitwise_and(first, EV_DEV - 1).astype(jnp.float32)
    column = jnp.transpose(jnp.broadcast_to(ends, (LANES, PAIR_DEV)))
    groups = lax.broadcasted_iota(jnp.int32, (PAIR_DEV, LANES), 1) // LAGS
    for half in range(2):
        mine = column == (groups + half * (LANES // LAGS)).astype(jnp.float32)
        pick_ref[:, half * LANES : (half + 1) * LANES] = mine.astype(jnp.float32)
    rates_ref[...] = jnp.zeros((1, PAYLOAD), jnp.float32)
    for station in range(STATIONS_DEV):
        for q in range(3):
            lane = (1 + q) * EV_DEV
            own = aux[station : station + 1, lane : lane + EV_DEV]
            for group in range(4):
                at = rate_place(group, station, q)
                rates_ref[:, at : at + EV_DEV] = jnp.where(
                    lax.axis_index("x") == group, own, 0.0
                )


def fill_table(ref, table_ref, part):
    for item in range(TRACES_DEV):
        tiles = [ref[item * CHUNKS + chunk] for chunk in range(CHUNKS)]
        squares = tiles[0] * tiles[0]
        for tile in tiles[1:]:
            squares = squares + tile * tile
        scale = lax.rsqrt(jnp.sum(squares, axis=1, keepdims=True) + eps_small)
        for chunk in range(CHUNKS):
            start = part * PART_ROWS + item * EV_DEV * CHUNKS + chunk
            table_ref[pl.ds(start, EV_DEV, stride=CHUNKS), :] = tiles[chunk] * scale


def align(places_ref, table_ref, moved_ref, slot, offset):
    lane_ids = lax.broadcasted_iota(jnp.int32, (ROWS, LANES), 1)
    for station in range(STATIONS_DEV):
        row = places_ref[station, slot] - offset
        lane = places_ref[3 + station, slot]
        turn = jnp.bitwise_and(-lane, LANES - 1)
        keep = lane_ids >= lane
        for component in range(3):
            item = station * 3 + component
            at = item * EV_DEV * CHUNKS
            here = table_ref[pl.ds(row + at, ROWS), :]
            after = table_ref[pl.ds(row + (at + 1), ROWS), :]
            moved = pltpu.roll(jnp.where(keep, here, after), turn, 1)
            to = pl.multiple_of((item * PAIR_DEV + slot) * ROWS, ROWS)
            moved_ref[pl.ds(to, ROWS), :] = moved


def groups_of(count):
    return lax.div(count + (GROUP - 1), GROUP)


def early_kernel(
    listed_ref, chip_ref, moved_ref, places_ref, high_ref, low_ref, table_ref, sem
):
    fetch = pltpu.make_async_copy(listed_ref, places_ref, sem)
    fetch.start()
    table_ref[pl.ds(2 * PART_ROWS, 2 * ROWS), :] = jnp.zeros((2 * ROWS, LANES), jnp.float32)
    core = lax.axis_index("c")
    first_windows(chip_ref.at[core], high_ref, low_ref, range(FIRST_ITEMS, TRACES_DEV))
    fill_table(chip_ref.at[core], table_ref, 0)
    fill_table(chip_ref.at[1 - core], table_ref, 1)
    fetch.wait()

    def step(index, carry):
        for turn in range(GROUP):
            align(places_ref, table_ref, moved_ref, places_ref[7, index * GROUP + turn], 0)
        return carry

    lax.fori_loop(0, groups_of(places_ref[9, 0]), step, 0)


def incidence(aux):
    events = lax.broadcasted_iota(jnp.int32, (NEAR, PAIR_DEV), 0).astype(jnp.float32)
    starts = (events == aux[3:4]).astype(jnp.float32)
    return starts - (events == aux[4:5]).astype(jnp.float32)


def near_block(left, own, right, part):
    lane = part * EV_DEV
    return jnp.concatenate(
        [aux[0:STATIONS_DEV, lane : lane + EV_DEV] for aux in (left, own, right)], axis=1
    )


def late_kernel(
    places_ref,
    moved_in_ref,
    chip_ref,
    cross_ref,
    high_ref,
    low_ref,
    last_high_ref,
    last_low_ref,
    pick_ref,
    rates_ref,
    shift_ref,
    block_ref,
    moved_ref,
    table_ref,
):
    del moved_in_ref
    table_ref[pl.ds(PART_ROWS, 2 * ROWS), :] = jnp.zeros((2 * ROWS, LANES), jnp.float32)
    fill_table(cross_ref, table_ref, 0)

    def step(index, carry):
        for turn in range(GROUP):
            slot = places_ref[6, index * GROUP + turn]
            align(places_ref, table_ref, moved_ref, slot, 2 * PART_ROWS)
        return carry

    lax.fori_loop(0, groups_of(places_ref[8, 0]), step, 0)

    core = lax.axis_index("c")
    aux_own = chip_ref[core, AUX]
    aux_left = jnp.where(core == 0, cross_ref[AUX], chip_ref[0, AUX])
    aux_right = jnp.where(core == 0, chip_ref[1, AUX], cross_ref[AUX])

    lane_ids = lax.broadcasted_iota(jnp.int32, (1, LANES), 1)
    centred = (lane_ids - LAGS // 2).astype(jnp.float32)
    weights = jnp.where(lane_ids < LAGS, centred, jnp.where(lane_ids < 2 * LAGS, 1.0, 0.0))
    folded = []
    for station in range(STATIONS_DEV):
        energy = jnp.zeros((PAIR_DEV, EV_DEV * LAGS), jnp.float32)
        for component in range(3):
            item = station * 3 + component
            pieces = [
                moved_ref[pl.ds(item * PAIR_DEV * ROWS + chunk, PAIR_DEV, stride=ROWS), :]
                for chunk in range(SPAN_CHUNKS)
            ]
            high, low = split_bf16(jnp.concatenate(pieces, axis=1))
            if item < FIRST_ITEMS:
                first_high, first_low = high_ref[item], low_ref[item]
            else:
                first_high = last_high_ref[item - FIRST_ITEMS]
                first_low = last_low_ref[item - FIRST_ITEMS]
            both = dot_bf16(jnp.concatenate([high, low], axis=0), first_high, NT)
            xcorr = both[0:PAIR_DEV] + both[PAIR_DEV:] + dot_bf16(high, first_low, NT)
            energy = energy + xcorr * xcorr
        energy = energy * pick_ref[...]
        energy = energy[:, 0:LANES] + energy[:, LANES:]
        energy = energy + pltpu.roll(energy, LANES // 2, 1)
        energy = energy + pltpu.roll(energy, LANES // 4, 1)
        folded.append(energy)
    pair = folded[0] * weights + folded[1] * pltpu.roll(weights, LANES // 2, 1)
    tables = [jnp.transpose(pair), jnp.transpose(folded[2] * weights)]
    station_shift = []
    for station in range(STATIONS_DEV):
        rows = tables[station // 2][(station % 2) * 2 * LAGS : (station % 2 + 1) * 2 * LAGS]
        above = jnp.sum(rows[0:LAGS], axis=0, keepdims=True)
        below = jnp.sum(rows[LAGS:], axis=0, keepdims=True)
        station_shift.append(above / (below + eps_small))
    alive = lax.broadcasted_iota(jnp.int32, (1, PAIR_DEV), 1) < places_ref[10, 0]
    shift = jnp.where(alive, jnp.concatenate(station_shift, axis=0), 0.0)
    shift_ref[...] = shift

    signs = jnp.where(alive, incidence(aux_own), 0.0)
    own_signs = signs[EV_DEV : 2 * EV_DEV].astype(jnp.bfloat16)
    signs = signs.astype(jnp.bfloat16)
    times = dot_signs(near_block(aux_left, aux_own, aux_right, 0), signs, NN)
    lags = aux_own[5:8]
    rhs = jnp.where(alive, sample_step * (lags + shift), 0.0) - times
    per_event = dot_signs(rhs, signs, NT)
    counts = dot_bf16(own_signs, signs, NT)
    counts = jnp.where(lax.axis_index("x") == 0, counts, 0.0)
    block_ref[...] = rates_ref[...]
    for event in range(EV_DEV):
        at = count_place(event)
        block_ref[:, at : at + NEAR] = counts[event : event + 1]
    for q in range(4):
        terms = per_event
        if q < 3:
            terms = terms * near_block(aux_left, aux_own, aux_right, 1 + q)
        block_ref[:, q * NEAR : (q + 1) * NEAR] = jnp.sum(terms, axis=0, keepdims=True)
    total = jnp.sum(jnp.sum(rhs * rhs, axis=1, keepdims=True), axis=0, keepdims=True)
    block_ref[:, SQUARE_AT : SQUARE_AT + 1] = total


def symmetric(counts, turned_ref):
    for side, block in ((0, 0), (2, 1)):
        for a in range(EV_DEV):
            at = block * EV_DEV * EV_DEV + a
            turned_ref[pl.ds(at, EV_DEV, stride=EV_DEV), :] = counts[a][side]
    lower = sum(counts[a][0] for a in range(1, EV_DEV)) + counts[0][0]
    upper = sum(counts[a][2] for a in range(1, EV_DEV)) + counts[0][2]
    ends = pltpu.roll(upper, 1, 1) + pltpu.roll(lower, LANES - 1, 1)
    rows = lax.broadcasted_iota(jnp.int32, (EV_DEV, LANES), 0)
    result = []
    for a in range(EV_DEV):
        to_lower = turned_ref[pl.ds(a * EV_DEV, EV_DEV), :]
        to_upper = turned_ref[pl.ds((EV_DEV + a) * EV_DEV, EV_DEV), :]
        result.append(
            [
                counts[a][0] + pltpu.roll(to_upper, 1, 1),
                counts[a][1] - jnp.where(rows == a, ends, 0.0),
                counts[a][2] + pltpu.roll(to_lower, LANES - 1, 1),
            ]
        )
    return result


def solve_kernel(gathered_ref, shift_ref, out_ref, shift_out_ref, rows_ref, turned_ref):
    shift_out_ref[...] = shift_ref[...]
    half = LANES // 2
    tables = []
    for row in range(PAYLOAD // LANES):
        for core in range(2):
            values = gathered_ref[pl.ds(core * half, half), row * LANES : (row + 1) * LANES]
            rows_ref[pl.ds(row * LANES + core, half, stride=2), :] = values
        tables.append(jnp.transpose(rows_ref[pl.ds(row * LANES, LANES), :]))

    def read(at):
        return tables[at // LANES][at % LANES : at % LANES + 8]

    def along(lower, own, upper):
        return own + pltpu.roll(upper, 1, 1) + pltpu.roll(lower, LANES - 1, 1)

    back = [along(*[read(q * NEAR + 8 * side) for side in range(3)]) for q in range(4)]
    counts = symmetric(
        [[read(count_place(a) + 8 * side) for side in range(3)] for a in range(EV_DEV)], turned_ref
    )
    deriv = [
        [read(rate_place(group, station, q)) for q in range(3)]
        for group in range(4)
        for station in range(STATIONS_DEV)
    ]

    def total(values):
        return jnp.sum(jnp.sum(values, axis=1, keepdims=True), axis=0, keepdims=True)

    def inner(left, right):
        terms = left[0] * right[0]
        for q in range(1, 4):
            terms = terms + left[q] * right[q]
        return total(terms)

    def normal(model):
        result = [jnp.zeros((EV_DEV, LANES), jnp.float32) for _ in range(4)]
        for rates in deriv:
            data = model[3]
            for q in range(3):
                data = data + rates[q] * model[q]
            sides = [None, None, None]
            for a in range(EV_DEV):
                row = jnp.broadcast_to(data[a : a + 1], (EV_DEV, LANES))
                for side in range(3):
                    term = counts[a][side] * row
                    sides[side] = term if a == 0 else sides[side] + term
            joined = along(*sides)
            for q in range(3):
                result[q] = result[q] + rates[q] * joined
            result[3] = result[3] + joined
        return result

    def mixed(left, left_scale, right, right_scale):
        return [left[q] * left_scale + right[q] * right_scale for q in range(4)]

    def residual(square):
        square = jnp.maximum(square, 0.0)
        return square, jnp.sqrt(square + eps_small)

    rhs_square = total(tables[0][SQUARE_AT : SQUARE_AT + 1])
    back_normal = normal(back)
    back_square = inner(back, back)
    back_bend = inner(back, back_normal)
    first_beta = jnp.sqrt(rhs_square + eps_small)
    from_beta = 1.0 / first_beta
    adjoint_square = back_square * from_beta * from_beta
    alpha = jnp.sqrt(adjoint_square + eps_small)
    scale = from_beta / alpha
    unit_square = rhs_square * from_beta * from_beta
    square, beta = residual(
        back_bend * scale * scale - 2.0 * adjoint_square + alpha * alpha * unit_square
    )
    rho = jnp.sqrt(alpha * alpha + beta * beta)
    cosine = alpha / rho
    sine = beta / rho
    step = cosine * first_beta / rho
    phi_bar = sine * first_beta
    to_beta = 1.0 / beta
    adjoint = mixed(back_normal, scale * to_beta, back, -(alpha * from_beta * to_beta))
    vector = mixed(adjoint, 1.0, back, -(beta * scale))
    vector_normal = normal(vector)
    vector_square = inner(vector, vector)
    vector_bend = inner(vector, vector_normal)
    vector_adjoint = inner(vector, adjoint)
    unit_square = square * to_beta * to_beta
    next_alpha = jnp.sqrt(vector_square + eps_small)
    to_alpha = 1.0 / next_alpha
    _, beta = residual(
        vector_bend * to_alpha * to_alpha
        - 2.0 * vector_adjoint
        + next_alpha * next_alpha * unit_square
    )
    theta = sine * next_alpha
    rho_bar = -cosine * next_alpha
    last_rho = jnp.sqrt(rho_bar * rho_bar + beta * beta)
    last_step = rho_bar / last_rho * phi_bar / last_rho
    location = mixed(
        back, (step - last_step * theta / rho) * scale, vector, last_step * to_alpha
    )

    lanes = lax.broadcasted_iota(jnp.int32, (ROWS, LANES), 1)
    mine = (lanes == device_index()).astype(jnp.float32)
    parts = dot_bf16(mine.astype(jnp.bfloat16), thirds(jnp.concatenate(location, axis=0)), NT)
    rows = 4 * EV_DEV
    own = parts[:, 0:rows] + parts[:, rows : 2 * rows] + parts[:, 2 * rows :]
    for q in range(4):
        out_ref[q : q + 1, :] = own[0:1, q * EV_DEV : (q + 1) * EV_DEV]


def from_other_chip(block):
    count = lax.axis_size("g") * lax.axis_size("c")
    partners = [(i, i - 1 + 2 * (i % 2)) for i in range(count)]
    route = [(i, other) for i, other in partners if 0 <= other < count]
    return lax.ppermute(block, ("g", "c"), route)


def spread(row, axis):
    copies = jnp.broadcast_to(row, (lax.axis_size(axis), row.shape[1]))
    return lax.all_to_all(copies, axis, 0, 0, tiled=True)


VMEM = pl.BlockSpec(memory_space=pltpu.VMEM)
SMEM = pl.BlockSpec(memory_space=pltpu.SMEM)
HBM = pl.BlockSpec(memory_space=pltpu.HBM)
PARAMS = pltpu.CompilerParams(vmem_limit_bytes=VMEM_BYTES)


def pack(traces, ray_slowness, travel_time, pair_first, pair_second, pair_lag):
    tiles = traces.reshape(TRACES_DEV, EV_DEV, CHUNKS, LANES).transpose(0, 2, 1, 3)
    arguments = (
        tiles.reshape(AUX, EV_DEV, LANES),
        ray_slowness,
        travel_time,
        pair_first.reshape(1, PAIR_DEV),
        pair_second.reshape(1, PAIR_DEV),
        pair_lag,
    )
    return pl.pallas_call(
        pack_kernel,
        out_shape=pltpu.VMEM((TILES, ROWS, LANES), jnp.float32),
        in_specs=[HBM] * 6,
        out_specs=VMEM,
        scratch_shapes=[
            pltpu.VMEM((3, STATIONS_DEV, EV_DEV), jnp.float32),
            pltpu.VMEM((STATIONS_DEV, EV_DEV), jnp.float32),
            pltpu.VMEM((1, PAIR_DEV), jnp.int32),
            pltpu.VMEM((1, PAIR_DEV), jnp.int32),
            pltpu.VMEM((STATIONS_DEV, PAIR_DEV), jnp.int32),
            pltpu.SemaphoreType.DMA((6,)),
        ],
        compiler_params=PARAMS,
        name="pack",
    )(*[pltpu.with_memory_space_constraint(value, pltpu.HBM) for value in arguments])


def firsts(pair_live, message):
    toeplitz = jax.ShapeDtypeStruct((FIRST_ITEMS, EV_DEV * LAGS, SPAN), jnp.bfloat16)
    return pl.pallas_call(
        first_kernel,
        out_shape=(
            toeplitz,
            toeplitz,
            jax.ShapeDtypeStruct((PLACE_ROWS, PAIR_DEV), jnp.int32),
            jax.ShapeDtypeStruct((PAIR_DEV, EV_DEV * LAGS), jnp.float32),
            jax.ShapeDtypeStruct((1, PAYLOAD), jnp.float32),
        ),
        in_specs=[SMEM, VMEM],
        out_specs=(VMEM,) * 5,
        compiler_params=PARAMS,
        name="firsts",
    )(pair_live, message)


MOVED = jax.ShapeDtypeStruct((TRACES_DEV * PAIR_DEV * ROWS + ROWS, LANES), jnp.float32)


def early(places, chip):
    toeplitz = jax.ShapeDtypeStruct(
        (TRACES_DEV - FIRST_ITEMS, EV_DEV * LAGS, SPAN), jnp.bfloat16
    )
    return pl.pallas_call(
        early_kernel,
        out_shape=(MOVED, pltpu.SMEM((PLACE_ROWS, PAIR_DEV), jnp.int32), toeplitz, toeplitz),
        in_specs=[VMEM, VMEM],
        out_specs=(VMEM, SMEM, VMEM, VMEM),
        scratch_shapes=[
            pltpu.VMEM((2 * PART_ROWS + 2 * ROWS, LANES), jnp.float32),
            pltpu.SemaphoreType.DMA,
        ],
        compiler_params=PARAMS,
        name="early",
    )(places, chip)


def late(places, moved, chip, from_cross, toeplitz, pick, rates):
    refined_shift, block, _ = pl.pallas_call(
        late_kernel,
        out_shape=(
            jax.ShapeDtypeStruct((STATIONS_DEV, PAIR_DEV), jnp.float32),
            jax.ShapeDtypeStruct((1, PAYLOAD), jnp.float32),
            MOVED,
        ),
        in_specs=[SMEM] + [VMEM] * 9,
        out_specs=(VMEM, VMEM, VMEM),
        scratch_shapes=[pltpu.VMEM((PART_ROWS + 2 * ROWS, LANES), jnp.float32)],
        input_output_aliases={1: 2},
        compiler_params=PARAMS,
        name="late",
    )(places, moved, chip, from_cross, *toeplitz, pick, rates)
    return refined_shift, block


def solve(gathered, shift):
    return pl.pallas_call(
        solve_kernel,
        out_shape=(
            jax.ShapeDtypeStruct((4, EV_DEV), jnp.float32),
            jax.ShapeDtypeStruct((STATIONS_DEV, PAIR_DEV), jnp.float32),
        ),
        in_specs=[VMEM, VMEM],
        out_specs=(VMEM, VMEM),
        scratch_shapes=[
            pltpu.VMEM((PAYLOAD + ROWS, LANES), jnp.float32),
            pltpu.VMEM((2 * EV_DEV * EV_DEV + ROWS, LANES), jnp.float32),
        ],
        compiler_params=PARAMS,
        name="solve",
    )(gathered, shift)


def body(traces, ray_slowness, travel_time, pair_first, pair_second, pair_lag, pair_live):
    message = pack(traces, ray_slowness, travel_time, pair_first, pair_second, pair_lag)
    from_cross = from_other_chip(message)
    pair_live = lax.optimization_barrier((message, pair_live))[1]
    high, low, places, pick, rates = firsts(pair_live, message)
    chip = lax.all_gather(message, "c", axis=0)
    moved, places, last_high, last_low = early(places, chip)
    places = pltpu.with_memory_space_constraint(places, pltpu.SMEM)
    toeplitz = (high, low, last_high, last_low)
    shift, block = late(places, moved, chip, from_cross, toeplitz, pick, rates)
    block = jnp.sum(spread(block, "x"), axis=0, keepdims=True)
    chips = lax.axis_size("g")
    gathered = lax.all_gather(spread(block, "g"), "c", axis=0)
    location, refined_shift = solve(gathered.reshape(2 * chips, PAYLOAD), shift)
    return refined_shift, location


def solution(mesh):
    ev, st = mesh.devices.shape
    fine = Mesh(mesh.devices.reshape(ev // 2, 2, st), ("g", "c", "x"))
    event_axes = ("g", "c")
    in_specs = (
        P("x", None, event_axes, None),
        P(None, "x", event_axes),
        P("x", event_axes),
        P(event_axes),
        P(event_axes),
        P("x", event_axes),
        P(event_axes),
    )
    out_specs = (P("x", event_axes), P(None, event_axes))
    return jax.shard_map(body, mesh=fine, in_specs=in_specs, out_specs=out_specs, check_vma=False)
```

```python
import jax
import jax.numpy as jnp
from jax import lax
from jax.experimental import pallas as pl
from jax.experimental.pallas import tpu as pltpu
from jax.sharding import Mesh
from jax.sharding import PartitionSpec as P

LAGS = 32
LANES = 128
ROWS = 8
EV_DEV = 8
NEAR = 3 * EV_DEV
STATIONS_DEV = 3
TRACES_DEV = 9
LENGTH = 1024
CHUNKS = LENGTH // LANES
QUARTER = LENGTH // 4
WINDOW = LENGTH // 2
SPAN = WINDOW + LANES
SPAN_CHUNKS = SPAN // LANES
PAIR_DEV = 128
PART_ROWS = TRACES_DEV * EV_DEV * CHUNKS
VMEM_BYTES = 24 * 1024 * 1024
PLACE_ROWS = 16
FIRST_ITEMS = 3
TILES = TRACES_DEV * CHUNKS + 1
AUX = TILES - 1
GROUP = 16
PAYLOAD = 5 * LANES
SQUARE_AT = 4 * NEAR

eps_small = 1e-06
sample_step = 0.01
NT = (((1,), (1,)), ((), ()))
NN = (((1,), (0,)), ((), ()))


def device_index():
    return lax.axis_index("g") * 2 + lax.axis_index("c")


def dot_bf16(left, right, dims):
    return lax.dot_general(left, right, dims, preferred_element_type=jnp.float32)


def count_place(event):
    return LANES + NEAR * event if event < 5 else 2 * LANES + NEAR * (event - 5)


def rate_place(group, station, q):
    index = (group * STATIONS_DEV + station) * 3 + q
    return 3 * LANES + 8 * index if index < 32 else 2 * LANES + 96 + 8 * (index - 32)


def rounded(values):
    return values.astype(jnp.bfloat16).astype(jnp.float32)


def thirds(values):
    high = rounded(values)
    middle = rounded(values - high)
    low = values - high - middle
    return jnp.concatenate([high, middle, low], axis=0).astype(jnp.bfloat16)


def dot_signs(left, signs, dims):
    rows = left.shape[0]
    parts = dot_bf16(thirds(left), signs, dims)
    return parts[0:rows] + parts[rows : 2 * rows] + parts[2 * rows :]


def split_bf16(values):
    high = values.astype(jnp.bfloat16)
    low = (values - high.astype(jnp.float32)).astype(jnp.bfloat16)
    return high, low


def pack_kernel(
    traces_ref,
    slowness_ref,
    time_ref,
    first_ref,
    second_ref,
    lag_ref,
    out_ref,
    slowness,
    time,
    first,
    second,
    lag,
    sems,
):
    pairs = [
        (traces_ref, out_ref.at[pl.ds(0, AUX)]),
        (slowness_ref, slowness),
        (time_ref, time),
        (first_ref, first),
        (second_ref, second),
        (lag_ref, lag),
    ]
    copies = [
        pltpu.make_async_copy(source, target, sems.at[at])
        for at, (source, target) in enumerate(pairs)
    ]
    for copy in copies:
        copy.start()
    aux = out_ref.at[AUX]
    aux[...] = jnp.zeros((ROWS, LANES), jnp.float32)
    for copy in copies[1:]:
        copy.wait()
    base = device_index() * EV_DEV - EV_DEV
    aux[0:STATIONS_DEV, 0:EV_DEV] = time[...]
    for q in range(3):
        lane = (1 + q) * EV_DEV
        aux[0:STATIONS_DEV, lane : lane + EV_DEV] = slowness[q]
    for row, ids in enumerate((first, second)):
        aux[3 + row : 4 + row, :] = (ids[...] - base).astype(jnp.float32)
    aux[5:8, :] = lag[...].astype(jnp.float32)
    copies[0].wait()


def first_windows(own_ref, high_ref, low_ref, items):
    for item in items:
        tiles = [own_ref[item * CHUNKS + chunk] for chunk in range(2, 6)]
        window = jnp.concatenate(tiles, axis=1)
        power = jnp.sum(window * window, axis=1, keepdims=True)
        window = window * lax.rsqrt(power + eps_small)
        padded = jnp.concatenate([window, jnp.zeros((EV_DEV, LANES), jnp.float32)], axis=1)
        at = item - items[0]
        for event in range(EV_DEV):
            wide = jnp.broadcast_to(padded[event : event + 1], (LAGS, SPAN))
            wide = pltpu.roll(wide, 0, 1, stride=1, stride_axis=0)
            high, low = split_bf16(wide)
            high_ref[at, pl.ds(event * LAGS, LAGS), :] = high
            low_ref[at, pl.ds(event * LAGS, LAGS), :] = low


def first_kernel(
    live_ref, own_ref, high_ref, low_ref, places_ref, pick_ref, rates_ref
):
    aux = own_ref[AUX]
    first = aux[3:4].astype(jnp.int32)
    second = aux[4:5].astype(jnp.int32)
    begin = aux[5:8].astype(jnp.int32) + (QUARTER - LAGS // 2)
    side = lax.shift_right_arithmetic(second, 3)
    mate_side = 2 - 2 * lax.axis_index("c")
    away = jnp.logical_and(side != 1, side != mate_side)
    part = jnp.where(side == 1, 0, jnp.where(away, 2, 1))
    alive = lax.broadcasted_iota(jnp.int32, (1, PAIR_DEV), 1) < live_ref[0]
    far = jnp.logical_and(away, alive)
    event = jnp.bitwise_and(second, EV_DEV - 1)
    rows = part * PART_ROWS + event * CHUNKS + lax.shift_right_arithmetic(begin, 7)
    near = jnp.logical_and(jnp.logical_not(away), alive)
    upper = lax.broadcasted_iota(jnp.int32, (PAIR_DEV, PAIR_DEV), 0)
    lower = lax.broadcasted_iota(jnp.int32, (PAIR_DEV, PAIR_DEV), 1)
    lane_ids = lower[0:1]
    ahead = (upper <= lower).astype(jnp.bfloat16)
    slots = lax.broadcasted_iota(jnp.int32, (ROWS, PAIR_DEV), 1).astype(jnp.bfloat16)
    hots, counts, listed = [], [], []
    for marked in (far, near):
        ones = marked.astype(jnp.float32)
        wide = jnp.broadcast_to(ones, (ROWS, PAIR_DEV)).astype(jnp.bfloat16)
        place = jnp.where(marked, dot_bf16(wide, ahead, NN)[0:1] - 1.0, -1.0)
        hots.append((upper.astype(jnp.float32) == place).astype(jnp.bfloat16))
        counts.append(jnp.sum(ones, axis=1, keepdims=True).astype(jnp.int32))
    for hot in hots:
        listed.append(dot_bf16(slots, hot, NT)[0:1])
    places_ref[...] = jnp.zeros((PLACE_ROWS, PAIR_DEV), jnp.int32)
    places_ref[0:3, :] = rows
    places_ref[3:6, :] = jnp.bitwise_and(begin, LANES - 1)
    for at in range(2):
        filled = jnp.where(lane_ids < counts[at], listed[at], listed[at][:, 0:1])
        places_ref[6 + at : 7 + at, :] = filled.astype(jnp.int32)
        places_ref[8 + at : 9 + at, :] = jnp.broadcast_to(counts[at], (1, PAIR_DEV))
    places_ref[10:11, :] = jnp.broadcast_to(live_ref[0], (1, PAIR_DEV))
    first_windows(own_ref, high_ref, low_ref, range(FIRST_ITEMS))
    ends = jnp.bitwise_and(first, EV_DEV - 1).astype(jnp.float32)
    column = jnp.transpose(jnp.broadcast_to(ends, (LANES, PAIR_DEV)))
    groups = lax.broadcasted_iota(jnp.int32, (PAIR_DEV, LANES), 1) // LAGS
    for half in range(2):
        mine = column == (groups + half * (LANES // LAGS)).astype(jnp.float32)
        pick_ref[:, half * LANES : (half + 1) * LANES] = mine.astype(jnp.float32)
    rates_ref[...] = jnp.zeros((1, PAYLOAD), jnp.float32)
    counts = pair_counts(aux, alive)
    for event in range(EV_DEV):
        at = count_place(event)
        rates_ref[:, at : at + NEAR] = counts[event : event + 1]
    for station in range(STATIONS_DEV):
        for q in range(3):
            lane = (1 + q) * EV_DEV
            own = aux[station : station + 1, lane : lane + EV_DEV]
            for group in range(4):
                at = rate_place(group, station, q)
                rates_ref[:, at : at + EV_DEV] = jnp.where(
                    lax.axis_index("x") == group, own, 0.0
                )


def pair_counts(aux, alive):
    signs = jnp.where(alive, incidence(aux), 0.0)
    own_signs = signs[EV_DEV : 2 * EV_DEV].astype(jnp.bfloat16)
    counts = dot_bf16(own_signs, signs.astype(jnp.bfloat16), NT)
    return jnp.where(lax.axis_index("x") == 0, counts, 0.0)


def fill_table(ref, table_ref, part):
    for item in range(TRACES_DEV):
        tiles = [ref[item * CHUNKS + chunk] for chunk in range(CHUNKS)]
        squares = tiles[0] * tiles[0]
        for tile in tiles[1:]:
            squares = squares + tile * tile
        scale = lax.rsqrt(jnp.sum(squares, axis=1, keepdims=True) + eps_small)
        for chunk in range(CHUNKS):
            start = part * PART_ROWS + item * EV_DEV * CHUNKS + chunk
            table_ref[pl.ds(start, EV_DEV, stride=CHUNKS), :] = tiles[chunk] * scale


def align(places_ref, table_ref, moved_ref, slot, offset):
    lane_ids = lax.broadcasted_iota(jnp.int32, (ROWS, LANES), 1)
    for station in range(STATIONS_DEV):
        row = places_ref[station, slot] - offset
        lane = places_ref[3 + station, slot]
        turn = jnp.bitwise_and(-lane, LANES - 1)
        keep = lane_ids >= lane
        for component in range(3):
            item = station * 3 + component
            at = item * EV_DEV * CHUNKS
            here = table_ref[pl.ds(row + at, ROWS), :]
            after = table_ref[pl.ds(row + (at + 1), ROWS), :]
            moved = pltpu.roll(jnp.where(keep, here, after), turn, 1)
            to = pl.multiple_of((item * PAIR_DEV + slot) * ROWS, ROWS)
            moved_ref[pl.ds(to, ROWS), :] = moved


def groups_of(count):
    return lax.div(count + (GROUP - 1), GROUP)


def early_kernel(
    listed_ref, chip_ref, moved_ref, places_ref, high_ref, low_ref, table_ref, sem
):
    fetch = pltpu.make_async_copy(listed_ref, places_ref, sem)
    fetch.start()
    table_ref[pl.ds(2 * PART_ROWS, 2 * ROWS), :] = jnp.zeros((2 * ROWS, LANES), jnp.float32)
    core = lax.axis_index("c")
    first_windows(chip_ref.at[core], high_ref, low_ref, range(FIRST_ITEMS, TRACES_DEV))
    fill_table(chip_ref.at[core], table_ref, 0)
    fill_table(chip_ref.at[1 - core], table_ref, 1)
    fetch.wait()

    def step(index, carry):
        for turn in range(GROUP):
            align(places_ref, table_ref, moved_ref, places_ref[7, index * GROUP + turn], 0)
        return carry

    lax.fori_loop(0, groups_of(places_ref[9, 0]), step, 0)


def incidence(aux):
    events = lax.broadcasted_iota(jnp.int32, (NEAR, PAIR_DEV), 0).astype(jnp.float32)
    starts = (events == aux[3:4]).astype(jnp.float32)
    return starts - (events == aux[4:5]).astype(jnp.float32)


def near_block(left, own, right, part):
    lane = part * EV_DEV
    return jnp.concatenate(
        [aux[0:STATIONS_DEV, lane : lane + EV_DEV] for aux in (left, own, right)], axis=1
    )


def late_kernel(
    places_ref,
    moved_in_ref,
    chip_ref,
    cross_ref,
    high_ref,
    low_ref,
    last_high_ref,
    last_low_ref,
    pick_ref,
    rates_ref,
    shift_ref,
    block_ref,
    moved_ref,
    table_ref,
):
    del moved_in_ref
    table_ref[pl.ds(PART_ROWS, 2 * ROWS), :] = jnp.zeros((2 * ROWS, LANES), jnp.float32)
    fill_table(cross_ref, table_ref, 0)

    def step(index, carry):
        for turn in range(GROUP):
            slot = places_ref[6, index * GROUP + turn]
            align(places_ref, table_ref, moved_ref, slot, 2 * PART_ROWS)
        return carry

    lax.fori_loop(0, groups_of(places_ref[8, 0]), step, 0)

    core = lax.axis_index("c")
    aux_own = chip_ref[core, AUX]
    aux_left = jnp.where(core == 0, cross_ref[AUX], chip_ref[0, AUX])
    aux_right = jnp.where(core == 0, chip_ref[1, AUX], cross_ref[AUX])

    lane_ids = lax.broadcasted_iota(jnp.int32, (1, LANES), 1)
    centred = (lane_ids - LAGS // 2).astype(jnp.float32)
    weights = jnp.where(lane_ids < LAGS, centred, jnp.where(lane_ids < 2 * LAGS, 1.0, 0.0))
    folded = []
    for station in range(STATIONS_DEV):
        energy = jnp.zeros((PAIR_DEV, EV_DEV * LAGS), jnp.float32)
        for component in range(3):
            item = station * 3 + component
            pieces = [
                moved_ref[pl.ds(item * PAIR_DEV * ROWS + chunk, PAIR_DEV, stride=ROWS), :]
                for chunk in range(SPAN_CHUNKS)
            ]
            high, low = split_bf16(jnp.concatenate(pieces, axis=1))
            if item < FIRST_ITEMS:
                first_high, first_low = high_ref[item], low_ref[item]
            else:
                first_high = last_high_ref[item - FIRST_ITEMS]
                first_low = last_low_ref[item - FIRST_ITEMS]
            both = dot_bf16(jnp.concatenate([high, low], axis=0), first_high, NT)
            xcorr = both[0:PAIR_DEV] + both[PAIR_DEV:] + dot_bf16(high, first_low, NT)
            energy = energy + xcorr * xcorr
        energy = energy * pick_ref[...]
        energy = energy[:, 0:LANES] + energy[:, LANES:]
        energy = energy + pltpu.roll(energy, LANES // 2, 1)
        energy = energy + pltpu.roll(energy, LANES // 4, 1)
        folded.append(energy)
    pair = folded[0] * weights + folded[1] * pltpu.roll(weights, LANES // 2, 1)
    tables = [jnp.transpose(pair), jnp.transpose(folded[2] * weights)]
    station_shift = []
    for station in range(STATIONS_DEV):
        rows = tables[station // 2][(station % 2) * 2 * LAGS : (station % 2 + 1) * 2 * LAGS]
        above = jnp.sum(rows[0:LAGS], axis=0, keepdims=True)
        below = jnp.sum(rows[LAGS:], axis=0, keepdims=True)
        station_shift.append(above / (below + eps_small))
    alive = lax.broadcasted_iota(jnp.int32, (1, PAIR_DEV), 1) < places_ref[10, 0]
    shift = jnp.where(alive, jnp.concatenate(station_shift, axis=0), 0.0)
    shift_ref[...] = shift

    signs = jnp.where(alive, incidence(aux_own), 0.0)
    signs = signs.astype(jnp.bfloat16)
    times = dot_signs(near_block(aux_left, aux_own, aux_right, 0), signs, NN)
    lags = aux_own[5:8]
    rhs = jnp.where(alive, sample_step * (lags + shift), 0.0) - times
    per_event = dot_signs(rhs, signs, NT)
    block_ref[...] = rates_ref[...]
    for q in range(4):
        terms = per_event
        if q < 3:
            terms = terms * near_block(aux_left, aux_own, aux_right, 1 + q)
        block_ref[:, q * NEAR : (q + 1) * NEAR] = jnp.sum(terms, axis=0, keepdims=True)
    total = jnp.sum(jnp.sum(rhs * rhs, axis=1, keepdims=True), axis=0, keepdims=True)
    block_ref[:, SQUARE_AT : SQUARE_AT + 1] = total


def symmetric(counts, turned_ref):
    for side, block in ((0, 0), (2, 1)):
        for a in range(EV_DEV):
            at = block * EV_DEV * EV_DEV + a
            turned_ref[pl.ds(at, EV_DEV, stride=EV_DEV), :] = counts[a][side]
    lower = sum(counts[a][0] for a in range(1, EV_DEV)) + counts[0][0]
    upper = sum(counts[a][2] for a in range(1, EV_DEV)) + counts[0][2]
    ends = pltpu.roll(upper, 1, 1) + pltpu.roll(lower, LANES - 1, 1)
    rows = lax.broadcasted_iota(jnp.int32, (EV_DEV, LANES), 0)
    result = []
    for a in range(EV_DEV):
        to_lower = turned_ref[pl.ds(a * EV_DEV, EV_DEV), :]
        to_upper = turned_ref[pl.ds((EV_DEV + a) * EV_DEV, EV_DEV), :]
        result.append(
            [
                counts[a][0] + pltpu.roll(to_upper, 1, 1),
                counts[a][1] - jnp.where(rows == a, ends, 0.0),
                counts[a][2] + pltpu.roll(to_lower, LANES - 1, 1),
            ]
        )
    return result


def solve_kernel(gathered_ref, shift_ref, out_ref, shift_out_ref, rows_ref, turned_ref):
    shift_out_ref[...] = shift_ref[...]
    half = LANES // 2
    tables = []
    for row in range(PAYLOAD // LANES):
        for core in range(2):
            values = gathered_ref[pl.ds(core * half, half), row * LANES : (row + 1) * LANES]
            rows_ref[pl.ds(row * LANES + core, half, stride=2), :] = values
        tables.append(jnp.transpose(rows_ref[pl.ds(row * LANES, LANES), :]))

    def read(at):
        return tables[at // LANES][at % LANES : at % LANES + 8]

    def along(lower, own, upper):
        return own + pltpu.roll(upper, 1, 1) + pltpu.roll(lower, LANES - 1, 1)

    back = [along(*[read(q * NEAR + 8 * side) for side in range(3)]) for q in range(4)]
    counts = symmetric(
        [[read(count_place(a) + 8 * side) for side in range(3)] for a in range(EV_DEV)], turned_ref
    )
    deriv = [
        [read(rate_place(group, station, q)) for q in range(3)]
        for group in range(4)
        for station in range(STATIONS_DEV)
    ]

    def total(values):
        return jnp.sum(jnp.sum(values, axis=1, keepdims=True), axis=0, keepdims=True)

    def inner(left, right):
        terms = left[0] * right[0]
        for q in range(1, 4):
            terms = terms + left[q] * right[q]
        return total(terms)

    def normal(model):
        result = [jnp.zeros((EV_DEV, LANES), jnp.float32) for _ in range(4)]
        for rates in deriv:
            data = model[3]
            for q in range(3):
                data = data + rates[q] * model[q]
            sides = [None, None, None]
            for a in range(EV_DEV):
                row = jnp.broadcast_to(data[a : a + 1], (EV_DEV, LANES))
                for side in range(3):
                    term = counts[a][side] * row
                    sides[side] = term if a == 0 else sides[side] + term
            joined = along(*sides)
            for q in range(3):
                result[q] = result[q] + rates[q] * joined
            result[3] = result[3] + joined
        return result

    def mixed(left, left_scale, right, right_scale):
        return [left[q] * left_scale + right[q] * right_scale for q in range(4)]

    def residual(square):
        square = jnp.maximum(square, 0.0)
        return square, jnp.sqrt(square + eps_small)

    rhs_square = total(tables[0][SQUARE_AT : SQUARE_AT + 1])
    back_normal = normal(back)
    back_square = inner(back, back)
    back_bend = inner(back, back_normal)
    first_beta = jnp.sqrt(rhs_square + eps_small)
    from_beta = 1.0 / first_beta
    adjoint_square = back_square * from_beta * from_beta
    alpha = jnp.sqrt(adjoint_square + eps_small)
    scale = from_beta / alpha
    unit_square = rhs_square * from_beta * from_beta
    square, beta = residual(
        back_bend * scale * scale - 2.0 * adjoint_square + alpha * alpha * unit_square
    )
    rho = jnp.sqrt(alpha * alpha + beta * beta)
    cosine = alpha / rho
    sine = beta / rho
    step = cosine * first_beta / rho
    phi_bar = sine * first_beta
    to_beta = 1.0 / beta
    adjoint = mixed(back_normal, scale * to_beta, back, -(alpha * from_beta * to_beta))
    vector = mixed(adjoint, 1.0, back, -(beta * scale))
    vector_normal = normal(vector)
    vector_square = inner(vector, vector)
    vector_bend = inner(vector, vector_normal)
    vector_adjoint = inner(vector, adjoint)
    unit_square = square * to_beta * to_beta
    next_alpha = jnp.sqrt(vector_square + eps_small)
    to_alpha = 1.0 / next_alpha
    _, beta = residual(
        vector_bend * to_alpha * to_alpha
        - 2.0 * vector_adjoint
        + next_alpha * next_alpha * unit_square
    )
    theta = sine * next_alpha
    rho_bar = -cosine * next_alpha
    last_rho = jnp.sqrt(rho_bar * rho_bar + beta * beta)
    last_step = rho_bar / last_rho * phi_bar / last_rho
    location = mixed(
        back, (step - last_step * theta / rho) * scale, vector, last_step * to_alpha
    )

    lanes = lax.broadcasted_iota(jnp.int32, (ROWS, LANES), 1)
    mine = (lanes == device_index()).astype(jnp.float32)
    parts = dot_bf16(mine.astype(jnp.bfloat16), thirds(jnp.concatenate(location, axis=0)), NT)
    rows = 4 * EV_DEV
    own = parts[:, 0:rows] + parts[:, rows : 2 * rows] + parts[:, 2 * rows :]
    for q in range(4):
        out_ref[q : q + 1, :] = own[0:1, q * EV_DEV : (q + 1) * EV_DEV]


def from_other_chip(block):
    count = lax.axis_size("g") * lax.axis_size("c")
    partners = [(i, i - 1 + 2 * (i % 2)) for i in range(count)]
    route = [(i, other) for i, other in partners if 0 <= other < count]
    return lax.ppermute(block, ("g", "c"), route)


def spread(row, axis):
    copies = jnp.broadcast_to(row, (lax.axis_size(axis), row.shape[1]))
    return lax.all_to_all(copies, axis, 0, 0, tiled=True)


VMEM = pl.BlockSpec(memory_space=pltpu.VMEM)
SMEM = pl.BlockSpec(memory_space=pltpu.SMEM)
HBM = pl.BlockSpec(memory_space=pltpu.HBM)
PARAMS = pltpu.CompilerParams(vmem_limit_bytes=VMEM_BYTES)


def pack(traces, ray_slowness, travel_time, pair_first, pair_second, pair_lag):
    tiles = traces.reshape(TRACES_DEV, EV_DEV, CHUNKS, LANES).transpose(0, 2, 1, 3)
    arguments = (
        tiles.reshape(AUX, EV_DEV, LANES),
        ray_slowness,
        travel_time,
        pair_first.reshape(1, PAIR_DEV),
        pair_second.reshape(1, PAIR_DEV),
        pair_lag,
    )
    return pl.pallas_call(
        pack_kernel,
        out_shape=pltpu.VMEM((TILES, ROWS, LANES), jnp.float32),
        in_specs=[HBM] * 6,
        out_specs=VMEM,
        scratch_shapes=[
            pltpu.VMEM((3, STATIONS_DEV, EV_DEV), jnp.float32),
            pltpu.VMEM((STATIONS_DEV, EV_DEV), jnp.float32),
            pltpu.VMEM((1, PAIR_DEV), jnp.int32),
            pltpu.VMEM((1, PAIR_DEV), jnp.int32),
            pltpu.VMEM((STATIONS_DEV, PAIR_DEV), jnp.int32),
            pltpu.SemaphoreType.DMA((6,)),
        ],
        compiler_params=PARAMS,
        name="pack",
    )(*[pltpu.with_memory_space_constraint(value, pltpu.HBM) for value in arguments])


def firsts(pair_live, message):
    toeplitz = jax.ShapeDtypeStruct((FIRST_ITEMS, EV_DEV * LAGS, SPAN), jnp.bfloat16)
    return pl.pallas_call(
        first_kernel,
        out_shape=(
            toeplitz,
            toeplitz,
            jax.ShapeDtypeStruct((PLACE_ROWS, PAIR_DEV), jnp.int32),
            jax.ShapeDtypeStruct((PAIR_DEV, EV_DEV * LAGS), jnp.float32),
            jax.ShapeDtypeStruct((1, PAYLOAD), jnp.float32),
        ),
        in_specs=[SMEM, VMEM],
        out_specs=(VMEM,) * 5,
        compiler_params=PARAMS,
        name="firsts",
    )(pair_live, message)


MOVED = jax.ShapeDtypeStruct((TRACES_DEV * PAIR_DEV * ROWS + ROWS, LANES), jnp.float32)


def early(places, chip):
    toeplitz = jax.ShapeDtypeStruct(
        (TRACES_DEV - FIRST_ITEMS, EV_DEV * LAGS, SPAN), jnp.bfloat16
    )
    return pl.pallas_call(
        early_kernel,
        out_shape=(MOVED, pltpu.SMEM((PLACE_ROWS, PAIR_DEV), jnp.int32), toeplitz, toeplitz),
        in_specs=[VMEM, VMEM],
        out_specs=(VMEM, SMEM, VMEM, VMEM),
        scratch_shapes=[
            pltpu.VMEM((2 * PART_ROWS + 2 * ROWS, LANES), jnp.float32),
            pltpu.SemaphoreType.DMA,
        ],
        compiler_params=PARAMS,
        name="early",
    )(places, chip)


def late(places, moved, chip, from_cross, toeplitz, pick, rates):
    refined_shift, block, _ = pl.pallas_call(
        late_kernel,
        out_shape=(
            jax.ShapeDtypeStruct((STATIONS_DEV, PAIR_DEV), jnp.float32),
            jax.ShapeDtypeStruct((1, PAYLOAD), jnp.float32),
            MOVED,
        ),
        in_specs=[SMEM] + [VMEM] * 9,
        out_specs=(VMEM, VMEM, VMEM),
        scratch_shapes=[pltpu.VMEM((PART_ROWS + 2 * ROWS, LANES), jnp.float32)],
        input_output_aliases={1: 2},
        compiler_params=PARAMS,
        name="late",
    )(places, moved, chip, from_cross, *toeplitz, pick, rates)
    return refined_shift, block


def solve(gathered, shift):
    return pl.pallas_call(
        solve_kernel,
        out_shape=(
            jax.ShapeDtypeStruct((4, EV_DEV), jnp.float32),
            jax.ShapeDtypeStruct((STATIONS_DEV, PAIR_DEV), jnp.float32),
        ),
        in_specs=[VMEM, VMEM],
        out_specs=(VMEM, VMEM),
        scratch_shapes=[
            pltpu.VMEM((PAYLOAD + ROWS, LANES), jnp.float32),
            pltpu.VMEM((2 * EV_DEV * EV_DEV + ROWS, LANES), jnp.float32),
        ],
        compiler_params=PARAMS,
        name="solve",
    )(gathered, shift)


def body(traces, ray_slowness, travel_time, pair_first, pair_second, pair_lag, pair_live):
    message = pack(traces, ray_slowness, travel_time, pair_first, pair_second, pair_lag)
    from_cross = from_other_chip(message)
    pair_live = lax.optimization_barrier((message, pair_live))[1]
    high, low, places, pick, rates = firsts(pair_live, message)
    chip = lax.all_gather(message, "c", axis=0)
    moved, places, last_high, last_low = early(places, chip)
    places = pltpu.with_memory_space_constraint(places, pltpu.SMEM)
    toeplitz = (high, low, last_high, last_low)
    shift, block = late(places, moved, chip, from_cross, toeplitz, pick, rates)
    block = jnp.sum(spread(block, "x"), axis=0, keepdims=True)
    chips = lax.axis_size("g")
    gathered = lax.all_gather(spread(block, "g"), "c", axis=0)
    location, refined_shift = solve(gathered.reshape(2 * chips, PAYLOAD), shift)
    return refined_shift, location


def solution(mesh):
    ev, st = mesh.devices.shape
    fine = Mesh(mesh.devices.reshape(ev // 2, 2, st), ("g", "c", "x"))
    event_axes = ("g", "c")
    in_specs = (
        P("x", None, event_axes, None),
        P(None, "x", event_axes),
        P("x", event_axes),
        P(event_axes),
        P(event_axes),
        P("x", event_axes),
        P(event_axes),
    )
    out_specs = (P("x", event_axes), P(None, event_axes))
    return jax.shard_map(body, mesh=fine, in_specs=in_specs, out_specs=out_specs, check_vma=False)
```
